128 devices in a mesh: scan: 16 (over y, z), tile: 8 (over x, core).
Axes of the slice: x: 4, y: 4, z: 4, core: 2. Of those that a mesh axis runs over, the one named last changes fastest.
Arguments:
- object_field: float32 [2, 2048, 4096], P(None, 'tile', 'scan'), may hold values from -4 to 4
- probe_modes: float32 [8, 2, 256, 256], replicated, may hold values from -1.5 to 1.5
- patterns: float32 [512, 256, 256], P(('scan', 'tile')), may hold values from 0.05 to 16
- positions: int32 [512, 2], P(('scan', 'tile')), may hold values from 0 to 4095, as said below
Outputs:
- object_out: float32 [2, 2048, 4096], P(None, 'tile', 'scan')
- probe_out: float32 [8, 2, 256, 256], replicated
The draws below stay inside these ranges and needn't reach their ends.
Inputs may be any that keep to these rules, and one draw needn't show every extreme that they name: `positions`: pattern j lies on the device of index j // 4 over scan+tile; its row offset lies in [t * 256, (t + 1) * 256) with t that device's tile index. With o = column offset // 256, the owner pairs o and (o + 1) mod the scan axis's size of the patterns of one device are disjoint.
All inputs are finite; a program needn't handle non-finite values.
Results may differ from the reference program's by a relative error of at most 0.00085.
The reference program's roundings to bfloat16 on the way count: a program that leaves them out, or rounds other values in their place, can miss the bound.
Values may be sent and summed in bfloat16 or wider, within the bound.
A program may use at most 128 MiB of HBM per device.

```python
import math
import jax
import jax.numpy as jnp
from jax import lax

P_SIZE = 256
M = 8
TR = 256
PAT_DEV = 4
ITERS = 1
OBJ_R = 2048
OBJ_C = 4096
NPAT = 512
N_SCAN = 16
N_TILE = 8
DEVICES = 128


def draw_positions(key, part):
    key = jax.random.fold_in(key, 11)
    row_key, offset_key, pair_key, flip_key = jax.random.split(key, 4)
    total_count = DEVICES * PAT_DEV
    device_of = jnp.arange(total_count, dtype=jnp.int32) // PAT_DEV
    band_index = device_of % N_TILE
    row_spots = band_index * TR + jax.random.randint(row_key, (total_count,), 0, TR)
    pair_keys = jax.random.split(pair_key, DEVICES)

    def choose_pairs(single_key):
        return jax.random.permutation(single_key, N_SCAN // 2)[:PAT_DEV]
    chosen = jax.vmap(choose_pairs)(pair_keys)
    flips = jax.random.randint(flip_key, (DEVICES, 1), 0, 2)
    owner_ids = ((2 * chosen + flips) % N_SCAN).reshape(-1)
    col_spots = owner_ids * P_SIZE + jax.random.randint(offset_key, (total_count,), 0, P_SIZE)
    return jnp.stack([row_spots, col_spots], axis=1).astype(jnp.int32)


def level_of(stream_key, extent, pieces, least, largest):
    def one(axis_at, parts):
        draws = jax.random.uniform(jax.random.fold_in(jax.random.fold_in(stream_key, 6), axis_at), (parts,), jnp.float32, least / len(pieces), largest / len(pieces))
        return jnp.repeat(jnp.exp(draws), extent[axis_at] // parts).reshape((-1,) + (1,) * (len(extent) - axis_at - 1))

    loudness = one(*pieces[0])
    for cut in pieces[1:]:
        loudness = loudness * one(*cut)
    return loudness


def normal_values(key, dims, deviation, reach, cuts=(), kind=jnp.bfloat16):
    values = deviation * jax.random.normal(key, dims, jnp.float32)
    if cuts:
        values = values * level_of(key, dims, cuts, -0.22, 0.18)
    return jnp.clip(values, -reach, reach).astype(kind)


def setup_inputs(seed: int = 0) -> dict:
    key_list = jax.random.split(jax.random.key(seed), 5)
    object_field = normal_values(key_list[0], (2, OBJ_R, OBJ_C), 0.7, 4.0, ((1, 8), (2, 16)), jnp.float32)
    probe_modes = normal_values(key_list[1], (M, 2, P_SIZE, P_SIZE), 0.25, 1.5, (), jnp.float32)
    patterns = jnp.clip(jnp.exp(math.log(16.0) - 5.768321 * jax.random.uniform(key_list[2], (NPAT, P_SIZE, P_SIZE), jnp.float32) ** level_of(key_list[2], (NPAT, P_SIZE, P_SIZE), ((0, 128),), -0.2, 0.2)), 0.05, 16.0)
    positions = draw_positions(jax.random.fold_in(key_list[4], 71), 0)
    return {"object_field": object_field, "probe_modes": probe_modes, "patterns": patterns, "positions": positions}


def dft_tables(length):
    counter = jnp.arange(length, dtype=jnp.int32)
    phase = counter[:, None] * counter[None, :] % length
    angle = phase.astype(jnp.float32) * (2.0 * math.pi / length)
    factor = 1.0 / math.sqrt(length)
    return ((jnp.cos(angle) * factor).astype(jnp.bfloat16), (jnp.sin(angle) * factor).astype(jnp.bfloat16))

def mat_right(real_part, imag_part, cosine, sine_table, sign):

    def product(left_op, right_op):
        return jnp.einsum('mjk,kl->mjl', left_op.astype(jnp.float32), right_op.astype(jnp.float32))
    real_out = product(real_part, cosine) - sign * product(imag_part, sine_table)
    imag_out = product(imag_part, cosine) + sign * product(real_part, sine_table)
    return (real_out, imag_out)

def mat_left(real_part, imag_part, cosine, sine_table, sign):

    def product(left_op, right_op):
        return jnp.einsum('jk,mkl->mjl', left_op.astype(jnp.float32), right_op.astype(jnp.float32))
    real_out = product(cosine, real_part) - sign * product(sine_table, imag_part)
    imag_out = product(cosine, imag_part) + sign * product(sine_table, real_part)
    return (real_out, imag_out)

def project(patch_bf, probe_now, pattern, cosine, sine_table):
    probe_re = probe_now[:, 0]
    probe_im = probe_now[:, 1]
    patch_re = patch_bf[0].astype(jnp.float32)
    patch_im = patch_bf[1].astype(jnp.float32)
    wave_re = (probe_re * patch_re - probe_im * patch_im).astype(jnp.bfloat16)
    wave_im = (probe_re * patch_im + probe_im * patch_re).astype(jnp.bfloat16)
    half_re, half_im = mat_right(wave_re, wave_im, cosine, sine_table, -1.0)
    half_re = half_re.astype(jnp.bfloat16)
    half_im = half_im.astype(jnp.bfloat16)
    far_re, far_im = mat_left(half_re, half_im, cosine, sine_table, -1.0)
    power = lax.optimization_barrier(jnp.sum(far_re * far_re + far_im * far_im, axis=0))
    scaling = jnp.sqrt(pattern) / jnp.sqrt(0.25 + power)
    fixed_re = (far_re * scaling).astype(jnp.bfloat16)
    fixed_im = (far_im * scaling).astype(jnp.bfloat16)
    back_re, back_im = mat_right(fixed_re, fixed_im, cosine, sine_table, 1.0)
    back_re = back_re.astype(jnp.bfloat16)
    back_im = back_im.astype(jnp.bfloat16)
    exit_re, exit_im = mat_left(back_re, back_im, cosine, sine_table, 1.0)
    update_re = lax.optimization_barrier(jnp.sum(probe_re * exit_re + probe_im * exit_im, axis=0))
    update_im = lax.optimization_barrier(jnp.sum(probe_re * exit_im - probe_im * exit_re, axis=0))
    update_full = jnp.stack([update_re, update_im], axis=0)
    probe_term = jnp.stack([patch_re * exit_re + patch_im * exit_im, patch_re * exit_im - patch_im * exit_re], axis=1)
    patch_power = patch_re * patch_re + patch_im * patch_im
    return (update_full, probe_term, patch_power)

def reference(object_field, probe_modes, patterns, positions):
    cosine, sine_table = dft_tables(P_SIZE)
    object_now = object_field
    probe_now = probe_modes
    zero_index = jnp.zeros((), jnp.int32)
    for sweep_index in range(ITERS):
        rounded = object_now.astype(jnp.bfloat16)
        wrapped = jnp.concatenate([rounded, rounded[:, :P_SIZE, :]], axis=1)
        wrapped = jnp.concatenate([wrapped, wrapped[:, :, :P_SIZE]], axis=2)
        probe_power = lax.optimization_barrier(jnp.sum(probe_now[:, 0] ** 2 + probe_now[:, 1] ** 2, axis=0))

        def visit(carry, item):
            accum_total, probe_numer, probe_denom = carry
            pattern, spot = item
            row_start = spot[0].astype(jnp.int32)
            col_start = spot[1].astype(jnp.int32)
            patch_bf = lax.dynamic_slice(wrapped, (zero_index, row_start, col_start), (2, P_SIZE, P_SIZE))
            update_full, probe_term, patch_power = project(patch_bf, probe_now, pattern, cosine, sine_table)
            stacked_block = jnp.concatenate([update_full, probe_power[None]], axis=0)
            previous = lax.dynamic_slice(accum_total, (zero_index, row_start, col_start), (3, P_SIZE, P_SIZE))
            accum_total = lax.dynamic_update_slice(accum_total, previous + stacked_block, (zero_index, row_start, col_start))
            return ((accum_total, probe_numer + probe_term, probe_denom + patch_power), None)
        start_carry = (jnp.zeros((3, OBJ_R + P_SIZE, OBJ_C + P_SIZE), jnp.float32), jnp.zeros((M, 2, P_SIZE, P_SIZE), jnp.float32), jnp.zeros((P_SIZE, P_SIZE), jnp.float32))
        (accum_total, probe_numer, probe_denom), unused = lax.scan(visit, start_carry, (patterns, positions))
        folded = accum_total[:, :OBJ_R, :].at[:, :P_SIZE, :].add(accum_total[:, OBJ_R:, :])
        folded = folded[:, :, :OBJ_C].at[:, :, :P_SIZE].add(folded[:, :, OBJ_C:])
        object_now = (object_now + folded[:2]) / (1.0 + folded[2])
        probe_now = (probe_now + probe_numer) / (1.0 + probe_denom)
    return (object_now, probe_now)
```

```python
import functools
import math

import jax
import jax.numpy as jnp
import ml_dtypes
import numpy as np
from jax import lax
from jax.experimental import pallas as pl
from jax.experimental.pallas import tpu as pltpu
from jax.sharding import PartitionSpec as P

F32 = jnp.float32
BF16 = jnp.bfloat16
N = 256
H = N // 2


def folded_tables():
    counter = np.arange(N, dtype=np.int32)
    phase = counter[:, None] * counter[None, :] % N
    angle = phase.astype(np.float32) * np.float32(2.0 * math.pi / N)
    factor = np.float32(1.0 / math.sqrt(N))
    cosine = (np.cos(angle) * factor).astype(ml_dtypes.bfloat16)
    sine = (np.sin(angle) * factor).astype(ml_dtypes.bfloat16)
    order = np.where(counter <= H, counter, 3 * H - counter)
    right = np.concatenate([cosine[:, : H + 1], sine[:, 1:H]], axis=1)[order]
    return np.stack([right, np.ascontiguousarray(right.T)])


def dot(left, right):
    return jnp.dot(left, right, preferred_element_type=F32)


def iota(axis):
    return lax.broadcasted_iota(jnp.int32, (N, N), axis)


def folded(index):
    return jnp.where(index <= H, index, 3 * H - index)


def one_hot(condition):
    return jnp.where(condition, 1.0, 0.0).astype(BF16)


def pieces(value, count):
    parts = []
    for _ in range(count):
        part = value.astype(BF16)
        parts.append(part)
        value = value - part.astype(F32)
    return parts


def permute(value, left, right, count):
    rows = sum(dot(left, part) for part in pieces(value, count))
    return sum(dot(part, right) for part in pieces(rows, count))


def fold_cols(a, b, sign):
    first = lax.broadcasted_iota(jnp.int32, (N, H), 1) == 0
    a_lo, a_hi, b_lo, b_hi = a[:, :H], a[:, H:], b[:, :H], b[:, H:]
    a_in = jnp.where(first, 0.0, a_hi)
    b_in = jnp.where(first, 0.0, b_hi)
    re_lo = a_lo - sign * b_in
    im_lo = b_lo + sign * a_in
    re_hi = jnp.where(first, a_hi, a_lo + sign * b_hi)
    im_hi = jnp.where(first, b_hi, b_lo - sign * a_hi)
    return jnp.concatenate([re_lo, re_hi, im_lo, im_hi], axis=1)


def fold_rows(c, sign):
    first = lax.broadcasted_iota(jnp.int32, (H, N), 0) == 0
    a_lo, a_hi, b_lo, b_hi = c[:H, :N], c[H:, :N], c[:H, N:], c[H:, N:]
    a_in = jnp.where(first, 0.0, a_hi)
    b_in = jnp.where(first, 0.0, b_hi)
    re_lo = a_lo - sign * b_in
    im_lo = b_lo + sign * a_in
    re_hi = jnp.where(first, a_hi, a_lo + sign * b_hi)
    im_hi = jnp.where(first, b_hi, b_lo - sign * a_hi)
    return jnp.concatenate([re_lo, re_hi], axis=0), jnp.concatenate([im_lo, im_hi], axis=0)


def transform(re, im, table, sign):
    right = table[0]
    half = fold_cols(dot(re, right), dot(im, right), sign).astype(BF16)
    return fold_rows(dot(table[1], half), sign)


def project_kernel(
    pos, near, far_block, below, pattern, probe, table, slots, numer, denom, folded_probe, far, power, patch, update
):
    step = pl.program_id(0)
    modes = probe.shape[0]
    row_shift, col_shift = pos[step, 0] % N, pos[step, 1] % N
    pair = pos[step, 1] // (2 * N)
    rows, cols = iota(0), iota(1)
    fold_matrix = one_hot(rows == folded(cols))

    @pl.when(step == 0)
    def _():
        slots[...] = jnp.zeros_like(slots)
        numer[...] = jnp.zeros_like(numer)
        denom[...] = jnp.zeros_like(denom)

        @pl.loop(0, modes)
        def _(m):
            for plane in range(2):
                folded_probe[m, plane] = permute(probe[m, plane], fold_matrix, fold_matrix, 3)

    row_pick = one_hot(cols == (row_shift + folded(rows)) % N)
    row_back = one_hot(rows == (row_shift + folded(cols)) % N)
    col_pick = one_hot(rows == (col_shift + folded(cols)) % N)
    col_back = one_hot(cols == (col_shift + folded(rows)) % N)
    for plane in range(2):
        top = jnp.where(cols >= col_shift, near[0, plane].astype(F32), far_block[0, plane].astype(F32))
        window = jnp.where(rows >= row_shift, top, below[0, plane].astype(F32)).astype(BF16)
        patch[plane] = dot(dot(row_pick, window).astype(BF16), col_pick)
    power[...] = jnp.full_like(power, 0.25)

    @pl.loop(0, modes)
    def _(m):
        p_re, p_im = folded_probe[m, 0], folded_probe[m, 1]
        o_re, o_im = patch[0], patch[1]
        wave_re = (p_re * o_re - p_im * o_im).astype(BF16)
        wave_im = (p_re * o_im + p_im * o_re).astype(BF16)
        f_re, f_im = transform(wave_re, wave_im, table, -1.0)
        far[m, 0] = f_re
        far[m, 1] = f_im
        power[...] += f_re * f_re + f_im * f_im

    level = permute(pattern[0], fold_matrix, fold_matrix, 3)
    power[...] = jnp.sqrt(level) / jnp.sqrt(power[...])
    update[...] = jnp.zeros_like(update)

    @pl.loop(0, modes)
    def _(m):
        scaling = power[...]
        fixed_re = (far[m, 0] * scaling).astype(BF16)
        fixed_im = (far[m, 1] * scaling).astype(BF16)
        e_re, e_im = transform(fixed_re, fixed_im, table, 1.0)
        p_re, p_im = folded_probe[m, 0], folded_probe[m, 1]
        update[0] += p_re * e_re + p_im * e_im
        update[1] += p_re * e_im - p_im * e_re
        o_re, o_im = patch[0], patch[1]
        numer[m, 0] += o_re * e_re + o_im * e_im
        numer[m, 1] += o_re * e_im - o_im * e_re

    denom[...] += patch[0] * patch[0] + patch[1] * patch[1]
    for plane in range(2):
        slots[2 * pair + plane] = permute(update[plane], row_back, col_back, 2)

    @pl.when(step == pl.num_programs(0) - 1)
    def _():
        @pl.loop(0, modes)
        def _(m):
            for plane in range(2):
                numer[m, plane] = permute(numer[m, plane], fold_matrix, fold_matrix, 2)

        denom[...] = permute(denom[...], fold_matrix, fold_matrix, 2)


def project(positions, band, below, patterns, probe, table):
    count, (modes,) = patterns.shape[0], probe.shape[:1]
    blocks = band.shape[0]
    whole = lambda shape: pl.BlockSpec(shape, lambda k, pos: (0,) * len(shape))
    near = pl.BlockSpec((1, 2, N, N), lambda k, pos: (pos[k, 1] // N, 0, 0, 0))
    after = pl.BlockSpec((1, 2, N, N), lambda k, pos: ((pos[k, 1] // N + 1) % blocks, 0, 0, 0))
    return pl.pallas_call(
        project_kernel,
        grid_spec=pltpu.PrefetchScalarGridSpec(
            num_scalar_prefetch=1,
            grid=(count,),
            in_specs=[
                near,
                after,
                pl.BlockSpec((1, 2, N, N), lambda k, pos: (k, 0, 0, 0)),
                pl.BlockSpec((1, N, N), lambda k, pos: (k, 0, 0)),
                whole((modes, 2, N, N)),
                whole((2, N, N)),
            ],
            out_specs=[whole((blocks, N, N)), whole((modes, 2, N, N)), whole((N, N))],
            scratch_shapes=[
                pltpu.VMEM((modes, 2, N, N), F32),
                pltpu.VMEM((modes, 2, N, N), F32),
                pltpu.VMEM((N, N), F32),
                pltpu.VMEM((2, N, N), F32),
                pltpu.VMEM((2, N, N), F32),
            ],
        ),
        out_shape=[
            jax.ShapeDtypeStruct((blocks, N, N), F32),
            jax.ShapeDtypeStruct((modes, 2, N, N), F32),
            jax.ShapeDtypeStruct((N, N), F32),
        ],
        compiler_params=pltpu.CompilerParams(vmem_limit_bytes=60 * 2**20),
        name="project",
    )(positions, band, band, below, patterns, probe, table)


def cut_kernel(pos, near, after, out):
    step = pl.program_id(0)
    col_shift = pos[step, 1] % N
    cols = iota(1)
    for plane in range(2):
        out[0, plane] = jnp.where(
            cols >= col_shift, near[0, plane].astype(F32), after[0, plane].astype(F32)
        ).astype(BF16)


def cut(positions, band):
    count, blocks = positions.shape[0], band.shape[0]
    return pl.pallas_call(
        cut_kernel,
        grid_spec=pltpu.PrefetchScalarGridSpec(
            num_scalar_prefetch=1,
            grid=(count,),
            in_specs=[
                pl.BlockSpec((1, 2, N, N), lambda k, pos: (pos[k, 1] // N, 0, 0, 0)),
                pl.BlockSpec((1, 2, N, N), lambda k, pos: ((pos[k, 1] // N + 1) % blocks, 0, 0, 0)),
            ],
            out_specs=pl.BlockSpec((1, 2, N, N), lambda k, pos: (k, 0, 0, 0)),
        ),
        out_shape=jax.ShapeDtypeStruct((count, 2, N, N), BF16),
        name="cut",
    )(positions, band, band)


def cover_kernel(place, pos_own, pos_above, probe, out):
    me, blocks = place[0], place[1]
    rows, cols = iota(0), iota(1)
    total = jnp.zeros((N, N), F32)
    for m in range(probe.shape[0]):
        total = total + (probe[m, 0] * probe[m, 0] + probe[m, 1] * probe[m, 1])
    out[...] = jnp.zeros_like(out)

    for above, pos in ((False, pos_own), (True, pos_above)):
        @pl.loop(0, pos_own.shape[0])
        def _(k):
            owner = pos[k, 1] // N
            row_shift, col_shift = pos[k, 0] % N, pos[k, 1] % N
            head, tail = owner == me, (owner + 1) % blocks == me

            @pl.when(head | tail)
            def _():
                moved = pltpu.roll(pltpu.roll(total, row_shift, 0), col_shift, 1)
                keep = (rows < row_shift) if above else (rows >= row_shift)
                split = jnp.where(head, col_shift, 0)
                stop = jnp.where(head, N, col_shift)
                keep = keep & (cols >= split) & (cols < stop)
                out[...] += jnp.where(keep, moved, 0.0)


def cover_of(place, pos_own, pos_above, probe):
    whole = lambda shape: pl.BlockSpec(shape, lambda i, *_: (0,) * len(shape))
    return pl.pallas_call(
        cover_kernel,
        grid_spec=pltpu.PrefetchScalarGridSpec(
            num_scalar_prefetch=3, grid=(1,), in_specs=[whole(probe.shape)], out_specs=whole((N, N))
        ),
        out_shape=jax.ShapeDtypeStruct((N, N), F32),
        compiler_params=pltpu.CompilerParams(vmem_limit_bytes=40 * 2**20),
        name="cover",
    )(place, pos_own, pos_above, probe)


def gather_kernel_sum(place, pos, received, out):
    pair = place[0] // 2
    rows, cols = iota(0), iota(1)
    out[...] = jnp.zeros_like(out)
    per_device = pos.shape[0] // received.shape[0]

    @pl.loop(0, pos.shape[0])
    def _(k):
        owner = pos[k, 1] // N
        row_shift, col_shift = pos[k, 0] % N, pos[k, 1] % N
        side = owner - 2 * pair

        @pl.when((side == 0) | (side == 1))
        def _():
            value = received[k // per_device]
            low, right = rows < row_shift, cols >= col_shift
            out[0, side] += jnp.where(low, 0.0, jnp.where(right, value, 0.0))
            out[0, side + 1] += jnp.where(low, 0.0, jnp.where(right, 0.0, value))
            out[1, side] += jnp.where(low, jnp.where(right, value, 0.0), 0.0)
            out[1, side + 1] += jnp.where(low, jnp.where(right, 0.0, value), 0.0)


def collect(place, pos, received):
    whole = lambda shape: pl.BlockSpec(shape, lambda i, *_: (0,) * len(shape))
    return pl.pallas_call(
        gather_kernel_sum,
        grid_spec=pltpu.PrefetchScalarGridSpec(
            num_scalar_prefetch=2, grid=(1,), in_specs=[whole(received.shape)], out_specs=whole((2, 3, N, N))
        ),
        out_shape=jax.ShapeDtypeStruct((2, 3, N, N), F32),
        compiler_params=pltpu.CompilerParams(vmem_limit_bytes=40 * 2**20),
        name="collect",
    )(place, pos, received)


def shifted(value, axis, steps):
    count = lax.axis_size(axis)
    return lax.ppermute(value, axis, [(s, (s + steps) % count) for s in range(count)])


def body(object_field, probe_modes, patterns, positions):
    scan_count, tile_count = lax.axis_size("scan"), lax.axis_size("tile")
    me, tile = lax.axis_index("scan"), lax.axis_index("tile")
    table = jnp.asarray(folded_tables())
    place = jnp.stack([me, jnp.int32(scan_count)])
    pos_all = lax.all_gather(positions, ("scan", "tile"), axis=0, tiled=True)
    pos_all = pos_all.reshape(scan_count, tile_count, -1, 2)
    above_tile = (tile + tile_count - 1) % tile_count
    pos_own = lax.dynamic_index_in_dim(pos_all, tile, 1, keepdims=False)
    pos_above = lax.dynamic_index_in_dim(pos_all, above_tile, 1, keepdims=False)
    pos_prev = lax.dynamic_index_in_dim(pos_above, me, 0, keepdims=False)
    pos_own = pos_own.reshape(-1, 2)
    pos_above = pos_above.reshape(-1, 2)
    band = lax.all_gather(object_field.astype(BF16), "scan", axis=0, tiled=False)
    below = shifted(cut(pos_prev, band), "tile", -1)
    slots, numer, denom = project(positions, band, below, patterns, probe_modes, table)
    received = lax.all_to_all(slots, "scan", split_axis=0, concat_axis=0, tiled=True)
    cover = cover_of(place, pos_own, pos_above, probe_modes)
    numer, denom = lax.psum((numer, denom), ("scan", "tile"))
    sums = collect(place, pos_own, received)
    sums = sums[0] + shifted(sums[1], "tile", 1)
    odd = me % 2 == 1
    swapped = lax.ppermute(jnp.where(odd, sums[0], sums[1]), "scan", [(s, s ^ 1) for s in range(scan_count)])
    tail_re = lax.ppermute(sums[2], "scan", [(s, (s + 2) % scan_count) for s in range(0, scan_count, 2)])
    tail_im = lax.ppermute(sums[2], "scan", [(s, (s + 1) % scan_count) for s in range(1, scan_count, 2)])
    whole_re = jnp.where(odd, swapped, sums[0] + tail_re)
    whole_im = jnp.where(odd, sums[1], swapped + tail_im)
    object_now = (object_field + jnp.stack([whole_re, whole_im])) / (1.0 + cover)
    probe_now = (probe_modes + numer) / (1.0 + denom)
    return (object_now, probe_now)


def solution(mesh):
    return jax.shard_map(
        body,
        mesh=mesh,
        in_specs=(
            P(None, "tile", "scan"),
            P(),
            P(("scan", "tile"), None, None),
            P(("scan", "tile"), None),
        ),
        out_specs=(P(None, "tile", "scan"), P()),
        check_vma=False,
    )
```

```python
import functools
import math

import jax
import jax.numpy as jnp
import ml_dtypes
import numpy as np
from jax import lax
from jax.experimental import pallas as pl
from jax.experimental.pallas import tpu as pltpu
from jax.sharding import PartitionSpec as P

F32 = jnp.float32
BF16 = jnp.bfloat16
N = 256
H = N // 2
I16 = jnp.int16
TAIL = 16
FULL = 32767.0
MESH = pl.DeviceIdType.MESH


def folded_tables():
    counter = np.arange(N, dtype=np.int32)
    phase = counter[:, None] * counter[None, :] % N
    angle = phase.astype(np.float32) * np.float32(2.0 * math.pi / N)
    factor = np.float32(1.0 / math.sqrt(N))
    cosine = (np.cos(angle) * factor).astype(ml_dtypes.bfloat16)
    sine = (np.sin(angle) * factor).astype(ml_dtypes.bfloat16)
    order = np.where(counter <= H, counter, 3 * H - counter)
    right = np.concatenate([cosine[:, : H + 1], sine[:, 1:H]], axis=1)[order]
    return np.stack([right, np.ascontiguousarray(right.T)])


def dot(left, right):
    return jnp.dot(left, right, preferred_element_type=F32)


def iota(axis):
    return lax.broadcasted_iota(jnp.int32, (N, N), axis)


def folded(index):
    return jnp.where(index <= H, index, 3 * H - index)


def one_hot(condition):
    return jnp.where(condition, 1.0, 0.0).astype(BF16)


def pieces(value, count):
    parts = []
    for _ in range(count):
        part = value.astype(BF16)
        parts.append(part)
        value = value - part.astype(F32)
    return parts


def permute(value, left, right, count):
    rows = sum(dot(left, part) for part in pieces(value, count))
    return sum(dot(part, right) for part in pieces(rows, count))


def encode(value):
    size = jnp.abs(value)
    peak = jnp.maximum(jnp.max(size, axis=0, keepdims=True), 1e-30)
    exponent = jnp.ceil(jnp.log(peak) * (1.0 / math.log(2.0)) + 1e-5)
    scale = jnp.exp(exponent * -math.log(2.0))
    code = jnp.minimum(jnp.sqrt(size * scale) * FULL + 0.5, FULL).astype(jnp.int32)
    code = jnp.where(value < 0.0, -code, code).astype(I16)
    tail = jnp.broadcast_to(exponent.astype(jnp.int32), (TAIL, value.shape[1])).astype(I16)
    return code, tail


def decode_scale(tail):
    exponent = tail.astype(jnp.int32).astype(F32)[:1]
    return jnp.exp(exponent * math.log(2.0)) * (1.0 / (FULL * FULL))


def decode(code, scale):
    code = code.astype(jnp.int32).astype(F32)
    return code * jnp.abs(code) * scale


def fold_cols(a, b, sign):
    first = lax.broadcasted_iota(jnp.int32, (N, H), 1) == 0
    a_lo, a_hi, b_lo, b_hi = a[:, :H], a[:, H:], b[:, :H], b[:, H:]
    a_in = jnp.where(first, 0.0, a_hi)
    b_in = jnp.where(first, 0.0, b_hi)
    re_lo = a_lo - sign * b_in
    im_lo = b_lo + sign * a_in
    re_hi = jnp.where(first, a_hi, a_lo + sign * b_hi)
    im_hi = jnp.where(first, b_hi, b_lo - sign * a_hi)
    return jnp.concatenate([re_lo, re_hi, im_lo, im_hi], axis=1)


def fold_rows(c, sign):
    first = lax.broadcasted_iota(jnp.int32, (H, N), 0) == 0
    a_lo, a_hi, b_lo, b_hi = c[:H, :N], c[H:, :N], c[:H, N:], c[H:, N:]
    a_in = jnp.where(first, 0.0, a_hi)
    b_in = jnp.where(first, 0.0, b_hi)
    re_lo = a_lo - sign * b_in
    im_lo = b_lo + sign * a_in
    re_hi = jnp.where(first, a_hi, a_lo + sign * b_hi)
    im_hi = jnp.where(first, b_hi, b_lo - sign * a_hi)
    return jnp.concatenate([re_lo, re_hi], axis=0), jnp.concatenate([im_lo, im_hi], axis=0)


def transform(re, im, table, sign):
    right = table[0]
    half = fold_cols(dot(re, right), dot(im, right), sign).astype(BF16)
    return fold_rows(dot(table[1], half), sign)


def project_kernel(
    pos, near, far_block, below, pattern, probe, table, slots, sums, folded_probe, far, power, patch, update
):
    step = pl.program_id(0)
    modes = probe.shape[0]
    row_shift, col_shift = pos[step, 0] % N, pos[step, 1] % N
    pair = pos[step, 1] // (2 * N)
    rows, cols = iota(0), iota(1)
    fold_matrix = one_hot(rows == folded(cols))

    @pl.when(step == 0)
    def _():
        slots[...] = jnp.zeros_like(slots)
        sums[...] = jnp.zeros_like(sums)

        @pl.loop(0, modes)
        def _(m):
            for plane in range(2):
                folded_probe[m, plane] = permute(probe[m, plane], fold_matrix, fold_matrix, 3)

    row_pick = one_hot(cols == (row_shift + folded(rows)) % N)
    row_back = one_hot(rows == (row_shift + folded(cols)) % N)
    col_pick = one_hot(rows == (col_shift + folded(cols)) % N)
    col_back = one_hot(cols == (col_shift + folded(rows)) % N)
    for plane in range(2):
        top = jnp.where(cols >= col_shift, near[0, plane].astype(F32), far_block[0, plane].astype(F32))
        window = jnp.where(rows >= row_shift, top, below[0, plane].astype(F32)).astype(BF16)
        patch[plane] = dot(dot(row_pick, window).astype(BF16), col_pick)
    power[...] = jnp.full_like(power, 0.25)

    @pl.loop(0, modes)
    def _(m):
        p_re, p_im = folded_probe[m, 0], folded_probe[m, 1]
        o_re, o_im = patch[0], patch[1]
        wave_re = (p_re * o_re - p_im * o_im).astype(BF16)
        wave_im = (p_re * o_im + p_im * o_re).astype(BF16)
        f_re, f_im = transform(wave_re, wave_im, table, -1.0)
        far[m, 0] = f_re
        far[m, 1] = f_im
        power[...] += f_re * f_re + f_im * f_im

    level = permute(pattern[0], fold_matrix, fold_matrix, 3)
    power[...] = jnp.sqrt(level) / jnp.sqrt(power[...])
    update[...] = jnp.zeros_like(update)

    @pl.loop(0, modes)
    def _(m):
        scaling = power[...]
        fixed_re = (far[m, 0] * scaling).astype(BF16)
        fixed_im = (far[m, 1] * scaling).astype(BF16)
        e_re, e_im = transform(fixed_re, fixed_im, table, 1.0)
        p_re, p_im = folded_probe[m, 0], folded_probe[m, 1]
        update[0] += p_re * e_re + p_im * e_im
        update[1] += p_re * e_im - p_im * e_re
        o_re, o_im = patch[0], patch[1]
        sums[2 * m] += o_re * e_re + o_im * e_im
        sums[2 * m + 1] += o_re * e_im - o_im * e_re

    sums[2 * modes] += patch[0] * patch[0] + patch[1] * patch[1]
    for plane in range(2):
        code, exponent = encode(permute(update[plane], row_back, col_back, 2))
        slots[2 * pair + plane, :N] = code
        slots[2 * pair + plane, N:] = exponent

    @pl.when(step == pl.num_programs(0) - 1)
    def _():
        @pl.loop(0, 2 * modes + 1)
        def _(m):
            sums[m] = permute(sums[m], fold_matrix, fold_matrix, 2)


def project(positions, band, below, patterns, probe, table):
    count, (modes,) = patterns.shape[0], probe.shape[:1]
    blocks = band.shape[0]
    whole = lambda shape: pl.BlockSpec(shape, lambda k, pos: (0,) * len(shape))
    near = pl.BlockSpec((1, 2, N, N), lambda k, pos: (pos[k, 1] // N, 0, 0, 0))
    after = pl.BlockSpec((1, 2, N, N), lambda k, pos: ((pos[k, 1] // N + 1) % blocks, 0, 0, 0))
    return pl.pallas_call(
        project_kernel,
        grid_spec=pltpu.PrefetchScalarGridSpec(
            num_scalar_prefetch=1,
            grid=(count,),
            in_specs=[
                near,
                after,
                pl.BlockSpec((1, 2, N, N), lambda k, pos: (k, 0, 0, 0)),
                pl.BlockSpec((1, N, N), lambda k, pos: (k, 0, 0)),
                whole((modes, 2, N, N)),
                whole((2, N, N)),
            ],
            out_specs=[whole((blocks, N + TAIL, N)), whole((2 * modes + 1, N, N))],
            scratch_shapes=[
                pltpu.VMEM((modes, 2, N, N), F32),
                pltpu.VMEM((modes, 2, N, N), F32),
                pltpu.VMEM((N, N), F32),
                pltpu.VMEM((2, N, N), F32),
                pltpu.VMEM((2, N, N), F32),
            ],
        ),
        out_shape=[
            jax.ShapeDtypeStruct((blocks, N + TAIL, N), I16),
            jax.ShapeDtypeStruct((2 * modes + 1, N, N), F32),
        ],
        compiler_params=pltpu.CompilerParams(vmem_limit_bytes=60 * 2**20),
        name="project",
    )(positions, band, band, below, patterns, probe, table)


def cut_kernel(pos, near, after, out):
    step = pl.program_id(0)
    col_shift = pos[step, 1] % N
    cols = iota(1)
    for plane in range(2):
        out[0, plane] = jnp.where(
            cols >= col_shift, near[0, plane].astype(F32), after[0, plane].astype(F32)
        ).astype(BF16)


def cut(positions, band):
    count, blocks = positions.shape[0], band.shape[0]
    return pl.pallas_call(
        cut_kernel,
        grid_spec=pltpu.PrefetchScalarGridSpec(
            num_scalar_prefetch=1,
            grid=(count,),
            in_specs=[
                pl.BlockSpec((1, 2, N, N), lambda k, pos: (pos[k, 1] // N, 0, 0, 0)),
                pl.BlockSpec((1, 2, N, N), lambda k, pos: ((pos[k, 1] // N + 1) % blocks, 0, 0, 0)),
            ],
            out_specs=pl.BlockSpec((1, 2, N, N), lambda k, pos: (k, 0, 0, 0)),
        ),
        out_shape=jax.ShapeDtypeStruct((count, 2, N, N), BF16),
        name="cut",
    )(positions, band, band)


def cover_kernel(place, pos_own, pos_above, probe, out):
    me, blocks = place[0], place[1]
    rows, cols = iota(0), iota(1)
    total = jnp.zeros((N, N), F32)
    for m in range(probe.shape[0]):
        total = total + (probe[m, 0] * probe[m, 0] + probe[m, 1] * probe[m, 1])
    out[...] = jnp.zeros_like(out)

    for above, pos in ((False, pos_own), (True, pos_above)):
        @pl.loop(0, pos_own.shape[0])
        def _(k):
            owner = pos[k, 1] // N
            row_shift, col_shift = pos[k, 0] % N, pos[k, 1] % N
            head, tail = owner == me, (owner + 1) % blocks == me

            @pl.when(head | tail)
            def _():
                moved = pltpu.roll(pltpu.roll(total, row_shift, 0), col_shift, 1)
                keep = (rows < row_shift) if above else (rows >= row_shift)
                split = jnp.where(head, col_shift, 0)
                stop = jnp.where(head, N, col_shift)
                keep = keep & (cols >= split) & (cols < stop)
                out[...] += jnp.where(keep, moved, 0.0)


def cover_of(place, pos_own, pos_above, probe):
    whole = lambda shape: pl.BlockSpec(shape, lambda i, *_: (0,) * len(shape))
    return pl.pallas_call(
        cover_kernel,
        grid_spec=pltpu.PrefetchScalarGridSpec(
            num_scalar_prefetch=3, grid=(1,), in_specs=[whole(probe.shape)], out_specs=whole((N, N))
        ),
        out_shape=jax.ShapeDtypeStruct((N, N), F32),
        compiler_params=pltpu.CompilerParams(vmem_limit_bytes=40 * 2**20),
        name="cover",
    )(place, pos_own, pos_above, probe)


def finish_kernel(
    pos,
    slots,
    sums,
    probe,
    field,
    cover,
    object_out,
    probe_out,
    received,
    core_in,
    x_out,
    x_in,
    y_part,
    y_in,
    z_in,
    coded,
    acc,
    spill_in,
    swap_in,
    tail_in,
    send_sem,
    recv_sem,
):
    scan_count, tile_count = lax.axis_size("scan"), lax.axis_size("tile")
    me, tile = lax.axis_index("scan"), lax.axis_index("tile")
    x, core = tile // 2, tile % 2
    y, z = me // 4, me % 4
    planes = sums.shape[0]
    pair, parity = me // 2, me % 2
    per_device = pos.shape[0] // scan_count
    CORE, XR, YR, ZR, YG, XG, CG, SP, SW, TL = 16, 17, 20, 23, 27, 31, 35, 39, 40, 41

    def copy(src, dst, send, recv, scan=None, tile_to=None):
        where = {"scan": me if scan is None else scan, "tile": tile if tile_to is None else tile_to}
        return pltpu.make_async_remote_copy(
            src_ref=src,
            dst_ref=dst,
            send_sem=send_sem.at[send],
            recv_sem=recv_sem.at[recv],
            device_id=where,
            device_id_type=MESH,
        )

    barrier = pltpu.get_barrier_semaphore()

    @pl.loop(1, scan_count)
    def _(d):
        pl.semaphore_signal(barrier, 1, device_id={"scan": (me + d) % scan_count, "tile": tile}, device_id_type=MESH)

    @pl.loop(1, tile_count)
    def _(d):
        pl.semaphore_signal(barrier, 1, device_id={"scan": me, "tile": (tile + d) % tile_count}, device_id_type=MESH)

    pl.semaphore_wait(barrier, scan_count + tile_count - 2)

    partner = tile + 1 - 2 * core
    other_lanes = pl.ds(pl.multiple_of((1 - core) * H, H), H)
    own_lanes = pl.ds(pl.multiple_of(core * H, H), H)
    core_copy = copy(sums.at[:, :, other_lanes], core_in, CORE, CORE, tile_to=partner)
    core_copy.start()

    def update_copy(d):
        to = (me + d) % scan_count
        return copy(slots.at[to], received.at[d], d, d, scan=to)

    @pl.loop(1, scan_count)
    def _(d):
        update_copy(d).start()

    acc[...] = jnp.zeros_like(acc)

    def collect(source, ref):
        owner, row_shift, col_shift = jnp.int32(-4), jnp.int32(0), jnp.int32(0)
        for k in range(per_device):
            spot_row, spot_col = pos[source * per_device + k, 0], pos[source * per_device + k, 1]
            hit = spot_col // (2 * N) == pair
            owner = jnp.where(hit, spot_col // N, owner)
            row_shift = jnp.where(hit, spot_row % N, row_shift)
            col_shift = jnp.where(hit, spot_col % N, col_shift)
        side = owner - 2 * pair
        cols = lax.broadcasted_iota(jnp.int32, (32, N), 1)
        right = cols >= col_shift
        head = jnp.broadcast_to(side, (32, N)) == 0
        tail = jnp.broadcast_to(side, (32, N)) == 1
        picks = (head & right, (head & ~right) | (tail & right), tail & ~right)
        scale = decode_scale(ref[N:])

        for part in range(0, N, 32):
            rows = lax.broadcasted_iota(jnp.int32, (32, N), 0) + part
            value = decode(ref[part : part + 32], scale)
            low = rows < row_shift
            for block in range(3):
                taken = jnp.where(picks[block], value, 0.0)
                acc[0, block, part : part + 32] += jnp.where(low, 0.0, taken)
                acc[1, block, part : part + 32] += jnp.where(low, taken, 0.0)

    def collect_far(d, carry):
        update_copy(d).wait_recv()
        collect((me + scan_count - d) % scan_count, received.at[d])
        return carry

    collect(me, slots.at[me])

    core_copy.wait_recv()
    x_copies = []
    for d in range(1, 4):
        to = (x + d) % 4
        rows = pl.ds(pl.multiple_of(to * 64, 64), 64)
        chunk = sums[:, rows, own_lanes] + core_in[:, rows]
        code, tail = encode(chunk.reshape(planes * 64, H))
        x_out[d - 1, : planes * 64] = code
        x_out[d - 1, planes * 64 :] = tail
        x_copies.append(copy(x_out.at[d - 1], x_in.at[d - 1], XR + d - 1, XR + d - 1, tile_to=2 * to + core))
        x_copies[-1].start()
    rows = pl.ds(pl.multiple_of(x * 64, 64), 64)
    y_part[...] = sums[:, rows, own_lanes] + core_in[:, rows]

    lax.fori_loop(1, 8, collect_far, 0)

    for d in range(1, 4):
        x_copies[d - 1].wait_recv()
        scale = decode_scale(x_in[d - 1, planes * 64 :])
        y_part[...] += decode(x_in[d - 1, : planes * 64], scale).reshape(planes, 64, H)
    y_copies = []
    for d in range(1, 4):
        to = (y + d) % 4
        rows = pl.ds(pl.multiple_of(to * 16, 16), 16)
        y_copies.append(copy(y_part.at[:, rows], y_in.at[d - 1], YR + d - 1, YR + d - 1, scan=4 * to + z))
        y_copies[-1].start()

    lax.fori_loop(8, scan_count, collect_far, 0)
    below_tile = (tile + 1) % tile_count
    spill_copy = copy(acc.at[1], spill_in, SP, SP, tile_to=below_tile)
    spill_copy.start()

    rows = pl.ds(pl.multiple_of(y * 16, 16), 16)
    chunk = y_part[:, rows]
    for d in range(1, 4):
        y_copies[d - 1].wait_recv()
        chunk = chunk + y_in[d - 1]
    z_in[z] = chunk
    z_copies = []
    for d in range(1, 4):
        to = (z + d) % 4
        z_copies.append(copy(z_in.at[z], z_in.at[z], ZR + d, ZR + d, scan=4 * y + to))
        z_copies[-1].start()

    spill_copy.wait_recv()
    acc[0] += spill_in[...]
    swap_copy = copy(acc.at[0, 1 - parity], swap_in, SW, SW, scan=me + 1 - 2 * parity)
    swap_copy.start()
    tail_copy = copy(
        acc.at[0, 2], tail_in.at[parity], TL, TL + parity, scan=(me + 2 - parity) % scan_count
    )
    tail_copy.start()

    for d in range(1, 4):
        source = (z + 4 - d) % 4
        copy(z_in.at[source], z_in.at[source], ZR + d, ZR + d, scan=4 * y + source).wait_recv()
    total = z_in[0] + z_in[1] + z_in[2] + z_in[3]
    rows = pl.ds(pl.multiple_of(x * 64 + y * 16, 16), 16)
    old = probe[:, rows, own_lanes]
    fresh = (old + total[: planes - 1]) / (1.0 + total[planes - 1 :])
    code, tail = encode(fresh.reshape((planes - 1) * 16, H))
    spot = core * 16 + x * 4 + y
    coded[spot, : (planes - 1) * 16] = code
    coded[spot, (planes - 1) * 16 :] = tail

    yg_copies = []
    for d in range(1, 4):
        yg_copies.append(copy(coded.at[spot], coded.at[spot], YG + d, YG + d, scan=4 * ((y + d) % 4) + z))
        yg_copies[-1].start()
    for d in range(1, 4):
        source = core * 16 + x * 4 + (y + 4 - d) % 4
        copy(coded.at[source], coded.at[source], YG + d, YG + d, scan=4 * ((y + d) % 4) + z).wait_recv()

    group = pl.ds(core * 16 + x * 4, 4)
    xg_copies = []
    for d in range(1, 4):
        to = 2 * ((x + d) % 4) + core
        xg_copies.append(copy(coded.at[group], coded.at[group], XG + d, XG + d, tile_to=to))
        xg_copies[-1].start()
    cg_copies = [copy(coded.at[group], coded.at[group], CG, CG, tile_to=partner)]
    cg_copies[-1].start()

    swap_copy.wait_recv()

    @pl.when(parity == 0)
    def _():
        for plane in range(2):
            copy(acc.at[0, 2], tail_in.at[plane], TL, TL + plane, scan=(me + 2) % scan_count).wait_recv()
        share = 1.0 / (1.0 + cover[...])
        object_out[0] = (field[0] + (acc[0, 0] + tail_in[0])) * share
        object_out[1] = (field[1] + (swap_in[...] + tail_in[1])) * share

    @pl.when(parity == 1)
    def _():
        share = 1.0 / (1.0 + cover[...])
        object_out[0] = (field[0] + swap_in[...]) * share
        object_out[1] = (field[1] + acc[0, 1]) * share

    def show(core_at, x_at):
        for y_at in range(4):
            at = core_at * 16 + x_at * 4 + y_at
            scale = decode_scale(coded[at, (planes - 1) * 16 :])
            value = decode(coded[at, : (planes - 1) * 16], scale).reshape(planes - 1, 16, H)
            rows = pl.ds(pl.multiple_of(x_at * 64 + y_at * 16, 16), 16)
            lanes = pl.ds(pl.multiple_of(core_at * H, H), H)
            probe_out[:, rows, lanes] = value

    show(core, x)
    for d in range(1, 4):
        source = (x + 4 - d) % 4
        at = pl.ds(core * 16 + source * 4, 4)
        copy(coded.at[at], coded.at[at], XG + d, XG + d, tile_to=2 * source + core).wait_recv()
        cg_copies.append(copy(coded.at[at], coded.at[at], CG + d, CG + d, tile_to=partner))
        cg_copies[-1].start()
        show(core, source)
    for d in range(4):
        source = (x + 4 - d) % 4
        at = pl.ds((1 - core) * 16 + source * 4, 4)
        copy(coded.at[at], coded.at[at], CG + d, CG + d, tile_to=partner).wait_recv()
        show(1 - core, source)

    @pl.loop(1, scan_count)
    def _(d):
        update_copy(d).wait_send()

    for started in [core_copy, spill_copy, swap_copy, tail_copy] + x_copies + y_copies + z_copies:
        started.wait_send()
    for started in yg_copies + xg_copies + cg_copies:
        started.wait_send()


def finish(pos, slots, sums, probe, field, cover):
    scan_count = slots.shape[0]
    planes = sums.shape[0]
    vmem = pl.BlockSpec(memory_space=pltpu.VMEM)
    return pl.pallas_call(
        finish_kernel,
        in_specs=[pl.BlockSpec(memory_space=pltpu.SMEM)] + [vmem] * 5,
        out_specs=[vmem, vmem],
        out_shape=[jax.ShapeDtypeStruct(field.shape, F32), jax.ShapeDtypeStruct(probe.shape, F32)],
        scratch_shapes=[
            pltpu.VMEM((scan_count, N + TAIL, N), I16),
            pltpu.VMEM((planes, N, H), F32),
            pltpu.VMEM((3, planes * 64 + TAIL, H), I16),
            pltpu.VMEM((3, planes * 64 + TAIL, H), I16),
            pltpu.VMEM((planes, 64, H), F32),
            pltpu.VMEM((3, planes, 16, H), F32),
            pltpu.VMEM((4, planes, 16, H), F32),
            pltpu.VMEM((32, (planes - 1) * 16 + TAIL, H), I16),
            pltpu.VMEM((2, 3, N, N), F32),
            pltpu.VMEM((3, N, N), F32),
            pltpu.VMEM((N, N), F32),
            pltpu.VMEM((2, N, N), F32),
            pltpu.SemaphoreType.DMA((44,)),
            pltpu.SemaphoreType.DMA((44,)),
        ],
        compiler_params=pltpu.CompilerParams(
            collective_id=1, has_side_effects=True, vmem_limit_bytes=56 * 2**20
        ),
        name="finish",
    )(pos, slots, sums, probe, field, cover)


def shifted(value, axis, steps):
    count = lax.axis_size(axis)
    return lax.ppermute(value, axis, [(s, (s + steps) % count) for s in range(count)])


def body(object_field, probe_modes, patterns, positions):
    scan_count, tile_count = lax.axis_size("scan"), lax.axis_size("tile")
    me, tile = lax.axis_index("scan"), lax.axis_index("tile")
    table = jnp.asarray(folded_tables())
    place = jnp.stack([me, jnp.int32(scan_count)])
    pos_all = lax.all_gather(positions, ("scan", "tile"), axis=0, tiled=True)
    pos_all = pos_all.reshape(scan_count, tile_count, -1, 2)
    above_tile = (tile + tile_count - 1) % tile_count
    pos_own = lax.dynamic_index_in_dim(pos_all, tile, 1, keepdims=False)
    pos_above = lax.dynamic_index_in_dim(pos_all, above_tile, 1, keepdims=False)
    pos_prev = lax.dynamic_index_in_dim(pos_above, me, 0, keepdims=False)
    pos_own = pos_own.reshape(-1, 2)
    pos_above = pos_above.reshape(-1, 2)
    band = lax.all_gather(object_field.astype(BF16), "scan", axis=0, tiled=False)
    below = shifted(cut(pos_prev, band), "tile", -1)
    slots, sums = project(positions, band, below, patterns, probe_modes, table)
    cover = cover_of(place, pos_own, pos_above, probe_modes)
    flat_probe = probe_modes.reshape(-1, N, N)
    object_now, probe_now = finish(pos_own, slots, sums, flat_probe, object_field, cover)
    return (object_now, probe_now.reshape(probe_modes.shape))


def solution(mesh):
    return jax.shard_map(
        body,
        mesh=mesh,
        in_specs=(
            P(None, "tile", "scan"),
            P(),
            P(("scan", "tile"), None, None),
            P(("scan", "tile"), None),
        ),
        out_specs=(P(None, "tile", "scan"), P()),
        check_vma=False,
    )
```

```python
import functools
import math

import jax
import jax.numpy as jnp
import ml_dtypes
import numpy as np
from jax import lax
from jax.experimental import pallas as pl
from jax.experimental.pallas import tpu as pltpu
from jax.sharding import PartitionSpec as P

F32 = jnp.float32
BF16 = jnp.bfloat16
N = 256
H = N // 2
I16 = jnp.int16
TAIL = 16
FULL = 32767.0
MESH = pl.DeviceIdType.MESH


def folded_tables():
    counter = np.arange(N, dtype=np.int32)
    phase = counter[:, None] * counter[None, :] % N
    angle = phase.astype(np.float32) * np.float32(2.0 * math.pi / N)
    factor = np.float32(1.0 / math.sqrt(N))
    cosine = (np.cos(angle) * factor).astype(ml_dtypes.bfloat16)
    sine = (np.sin(angle) * factor).astype(ml_dtypes.bfloat16)
    order = np.where(counter <= H, counter, 3 * H - counter)
    right = np.concatenate([cosine[:, : H + 1], sine[:, 1:H]], axis=1)[order]
    return np.stack([right, np.ascontiguousarray(right.T)])


def dot(left, right):
    return jnp.dot(left, right, preferred_element_type=F32)


def iota(axis):
    return lax.broadcasted_iota(jnp.int32, (N, N), axis)


def folded(index):
    return jnp.where(index <= H, index, 3 * H - index)


def one_hot(condition):
    return jnp.where(condition, 1.0, 0.0).astype(BF16)


def pieces(value, count):
    parts = []
    for _ in range(count):
        part = value.astype(BF16)
        parts.append(part)
        value = value - part.astype(F32)
    return parts


def permute(value, left, right, count):
    rows = sum(dot(left, part) for part in pieces(value, count))
    return sum(dot(part, right) for part in pieces(rows, count))


def encode(value):
    size = jnp.abs(value)
    peak = jnp.maximum(jnp.max(size, axis=0, keepdims=True), 1e-30)
    exponent = jnp.ceil(jnp.log(peak) * (1.0 / math.log(2.0)) + 1e-5)
    scale = jnp.exp(exponent * -math.log(2.0))
    code = jnp.minimum(jnp.sqrt(size * scale) * FULL + 0.5, FULL).astype(jnp.int32)
    code = jnp.where(value < 0.0, -code, code).astype(I16)
    tail = jnp.broadcast_to(exponent.astype(jnp.int32), (TAIL, value.shape[1])).astype(I16)
    return code, tail


def decode_scale(tail):
    exponent = tail.astype(jnp.int32).astype(F32)[:1]
    return jnp.exp(exponent * math.log(2.0)) * (1.0 / (FULL * FULL))


def decode(code, scale):
    code = code.astype(jnp.int32).astype(F32)
    return code * jnp.abs(code) * scale


def fold_cols(a, b, sign):
    first = lax.broadcasted_iota(jnp.int32, (N, H), 1) == 0
    a_lo, a_hi, b_lo, b_hi = a[:, :H], a[:, H:], b[:, :H], b[:, H:]
    a_in = jnp.where(first, 0.0, a_hi)
    b_in = jnp.where(first, 0.0, b_hi)
    re_lo = a_lo - sign * b_in
    im_lo = b_lo + sign * a_in
    re_hi = jnp.where(first, a_hi, a_lo + sign * b_hi)
    im_hi = jnp.where(first, b_hi, b_lo - sign * a_hi)
    return jnp.concatenate([re_lo, re_hi, im_lo, im_hi], axis=1)


def fold_rows(c, sign):
    first = lax.broadcasted_iota(jnp.int32, (H, N), 0) == 0
    a_lo, a_hi, b_lo, b_hi = c[:H, :N], c[H:, :N], c[:H, N:], c[H:, N:]
    a_in = jnp.where(first, 0.0, a_hi)
    b_in = jnp.where(first, 0.0, b_hi)
    re_lo = a_lo - sign * b_in
    im_lo = b_lo + sign * a_in
    re_hi = jnp.where(first, a_hi, a_lo + sign * b_hi)
    im_hi = jnp.where(first, b_hi, b_lo - sign * a_hi)
    return jnp.concatenate([re_lo, re_hi], axis=0), jnp.concatenate([im_lo, im_hi], axis=0)


def transform(re, im, table, sign):
    right = table[0]
    half = fold_cols(dot(re, right), dot(im, right), sign).astype(BF16)
    return fold_rows(dot(table[1], half), sign)


def project_kernel(
    pos, near, far_block, below, level, folded_probe, table, slots, sums, far, power, patch, update
):
    step = pl.program_id(0)
    modes = folded_probe.shape[0] // 2
    row_shift, col_shift = pos[step, 0] % N, pos[step, 1] % N
    pair = pos[step, 1] // (2 * N)
    rows, cols = iota(0), iota(1)
    fold_matrix = one_hot(rows == folded(cols))

    @pl.when(step == 0)
    def _():
        slots[...] = jnp.zeros_like(slots)
        sums[...] = jnp.zeros_like(sums)

    row_pick = one_hot(cols == (row_shift + folded(rows)) % N)
    row_back = one_hot(rows == (row_shift + folded(cols)) % N)
    col_pick = one_hot(rows == (col_shift + folded(cols)) % N)
    col_back = one_hot(cols == (col_shift + folded(rows)) % N)
    for plane in range(2):
        top = jnp.where(cols >= col_shift, near[0, plane].astype(F32), far_block[0, plane].astype(F32))
        window = jnp.where(rows >= row_shift, top, below[0, plane].astype(F32)).astype(BF16)
        patch[plane] = dot(dot(row_pick, window).astype(BF16), col_pick)
    power[...] = jnp.full_like(power, 0.25)

    @pl.loop(0, modes)
    def _(m):
        p_re, p_im = folded_probe[2 * m], folded_probe[2 * m + 1]
        o_re, o_im = patch[0], patch[1]
        wave_re = (p_re * o_re - p_im * o_im).astype(BF16)
        wave_im = (p_re * o_im + p_im * o_re).astype(BF16)
        f_re, f_im = transform(wave_re, wave_im, table, -1.0)
        far[m, 0] = f_re
        far[m, 1] = f_im
        power[...] += f_re * f_re + f_im * f_im

    power[...] = level[0] / jnp.sqrt(power[...])
    update[...] = jnp.zeros_like(update)

    @pl.loop(0, modes)
    def _(m):
        scaling = power[...]
        fixed_re = (far[m, 0] * scaling).astype(BF16)
        fixed_im = (far[m, 1] * scaling).astype(BF16)
        e_re, e_im = transform(fixed_re, fixed_im, table, 1.0)
        p_re, p_im = folded_probe[2 * m], folded_probe[2 * m + 1]
        update[0] += p_re * e_re + p_im * e_im
        update[1] += p_re * e_im - p_im * e_re
        o_re, o_im = patch[0], patch[1]
        sums[2 * m] += o_re * e_re + o_im * e_im
        sums[2 * m + 1] += o_re * e_im - o_im * e_re

    sums[2 * modes] += patch[0] * patch[0] + patch[1] * patch[1]
    for plane in range(2):
        code, exponent = encode(permute(update[plane], row_back, col_back, 2))
        slots[2 * pair + plane, :N] = code
        slots[2 * pair + plane, N:] = exponent

    @pl.when(step == pl.num_programs(0) - 1)
    def _():
        @pl.loop(0, 2 * modes + 1)
        def _(m):
            sums[m] = permute(sums[m], fold_matrix, fold_matrix, 2)


def project(positions, band, below, level, folded_probe, table):
    count, modes = level.shape[0], folded_probe.shape[0] // 2
    blocks = band.shape[0]
    whole = lambda shape: pl.BlockSpec(shape, lambda k, pos: (0,) * len(shape))
    near = pl.BlockSpec((1, 2, N, N), lambda k, pos: (pos[k, 1] // N, 0, 0, 0))
    after = pl.BlockSpec((1, 2, N, N), lambda k, pos: ((pos[k, 1] // N + 1) % blocks, 0, 0, 0))
    return pl.pallas_call(
        project_kernel,
        grid_spec=pltpu.PrefetchScalarGridSpec(
            num_scalar_prefetch=1,
            grid=(count,),
            in_specs=[
                near,
                after,
                pl.BlockSpec((1, 2, N, N), lambda k, pos: (k, 0, 0, 0)),
                pl.BlockSpec((1, N, N), lambda k, pos: (k, 0, 0)),
                whole((2 * modes, N, N)),
                whole((2, N, N)),
            ],
            out_specs=[whole((blocks, N + TAIL, N)), whole((2 * modes + 1, N, N))],
            scratch_shapes=[
                pltpu.VMEM((modes, 2, N, N), F32),
                pltpu.VMEM((N, N), F32),
                pltpu.VMEM((2, N, N), F32),
                pltpu.VMEM((2, N, N), F32),
            ],
        ),
        out_shape=[
            jax.ShapeDtypeStruct((blocks, N + TAIL, N), I16),
            jax.ShapeDtypeStruct((2 * modes + 1, N, N), F32),
        ],
        compiler_params=pltpu.CompilerParams(vmem_limit_bytes=60 * 2**20),
        name="project",
    )(positions, band, band, below, level, folded_probe, table)


def remote(src, dst, send, recv, scan, tile):
    return pltpu.make_async_remote_copy(
        src_ref=src,
        dst_ref=dst,
        send_sem=send,
        recv_sem=recv,
        device_id={"scan": scan, "tile": tile},
        device_id_type=MESH,
    )


def greet():
    scan_count, tile_count = lax.axis_size("scan"), lax.axis_size("tile")
    me, tile = lax.axis_index("scan"), lax.axis_index("tile")
    barrier = pltpu.get_barrier_semaphore()

    @pl.loop(1, scan_count)
    def _(d):
        pl.semaphore_signal(barrier, 1, device_id={"scan": (me + d) % scan_count, "tile": tile}, device_id_type=MESH)

    @pl.loop(1, tile_count)
    def _(d):
        pl.semaphore_signal(barrier, 1, device_id={"scan": me, "tile": (tile + d) % tile_count}, device_id_type=MESH)

    pl.semaphore_wait(barrier, scan_count + tile_count - 2)


def gather_kernel(
    block,
    spots,
    probe,
    patterns,
    band,
    below,
    spots_own,
    cover,
    folded_probe,
    level,
    cut,
    spots_above,
    spot_words,
    spot_words_above,
    power,
    send_sem,
    recv_sem,
    spot_send,
    spot_recv,
    cut_send,
    cut_recv,
    local_sem,
):
    scan_count, tile_count = lax.axis_size("scan"), lax.axis_size("tile")
    me, tile = lax.axis_index("scan"), lax.axis_index("tile")
    y, z = me // 4, me % 4
    next_tile, last_tile = (tile + 1) % tile_count, (tile + tile_count - 1) % tile_count
    per_device = patterns.shape[0]
    greet()

    def spot_copy(d):
        return remote(
            spots, spots_own.at[me], spot_send.at[d], spot_recv.at[d], (me + d) % scan_count, tile
        )

    @pl.loop(1, scan_count)
    def _(d):
        spot_copy(d).start()

    def along(plane, stage, d):
        turn_z = (plane == 0) == (stage == 0)
        return 4 * y + (z + d) % 4 if turn_z else 4 * ((y + d) % 4) + z

    sent = []

    def push(src, source, plane, stage, d):
        move = remote(
            src,
            band.at[source, plane],
            send_sem.at[len(sent)],
            recv_sem.at[2 * source + plane],
            along(plane, stage, d),
            tile,
        )
        move.start()
        sent.append(move)

    for stage in range(2):
        for d in (1, 3, 2):
            for plane in range(2):
                push(block.at[plane], me, plane, stage, d)

    def landed(source, plane):
        remote(block.at[plane], band.at[source, plane], send_sem.at[0], recv_sem.at[2 * source + plane], along(0, 0, 1), tile).wait_recv()

    spots_own[me] = spots[...]
    band[me] = block[...]
    total = jnp.zeros((N, N), F32)
    for plane in range(probe.shape[0]):
        total = total + probe[plane] * probe[plane]
    power[...] = total

    for d in (3, 1, 2):
        for plane in range(2):
            source = along(plane, 0, d)
            landed(source, plane)
            for turn in (1, 3, 2):
                push(band.at[source, plane], source, plane, 1, turn)

    @pl.loop(1, scan_count)
    def _(d):
        source = (me + scan_count - d) % scan_count
        remote(spots, spots_own.at[source], spot_send.at[d], spot_recv.at[d], source, tile).wait_recv()

    above_copy = remote(spots_own, spots_above, spot_send.at[0], spot_recv.at[0], me, next_tile)
    above_copy.start()
    words_copy = pltpu.make_async_copy(spots_own, spot_words, local_sem.at[0])
    words_copy.start()

    fold_matrix = one_hot(iota(0) == folded(iota(1)))

    @pl.loop(0, probe.shape[0])
    def _(plane):
        folded_probe[plane] = permute(probe[plane], fold_matrix, fold_matrix, 3)

    @pl.loop(0, per_device)
    def _(k):
        level[k] = jnp.sqrt(permute(patterns[k], fold_matrix, fold_matrix, 3))

    cover[...] = jnp.zeros_like(cover)

    def add_cover(words, above):
        @pl.loop(0, scan_count)
        def _(source):
            head, row_shift, col_shift = jnp.int32(-1), jnp.int32(0), jnp.int32(0)
            for k in range(per_device):
                row, col = words[source, 0, 2 * k], words[source, 0, 2 * k + 1]
                owner = col // N
                first = owner == me
                hit = first | ((owner + 1) % scan_count == me)
                head = jnp.where(hit, first.astype(jnp.int32), head)
                row_shift = jnp.where(hit, row % N, row_shift)
                col_shift = jnp.where(hit, col % N, col_shift)
            start = jnp.where(head == 1, col_shift, 0)
            stop = jnp.where(head == 1, N, jnp.where(head == 0, col_shift, 0))
            rows, cols = iota(0), iota(1)
            moved = pltpu.roll(pltpu.roll(power[...], row_shift, 0), col_shift, 1)
            keep = (rows < row_shift) if above else (rows >= row_shift)
            cover[...] += jnp.where(keep & (cols >= start) & (cols < stop), moved, 0.0)

    words_copy.wait()
    add_cover(spot_words, False)
    above_copy.wait_recv()
    words_copy = pltpu.make_async_copy(spots_above, spot_words_above, local_sem.at[1])
    words_copy.start()
    words_copy.wait()
    add_cover(spot_words_above, True)

    for d in (3, 1, 2):
        for plane in range(2):
            for turn in (3, 1, 2):
                if plane == 0:
                    source = 4 * ((y + turn) % 4) + (z + d) % 4
                else:
                    source = 4 * ((y + d) % 4) + (z + turn) % 4
                landed(source, plane)
    for turn in (3, 1, 2):
        landed(4 * ((y + turn) % 4) + z, 0)
        landed(4 * y + (z + turn) % 4, 1)

    cuts = []
    cols = lax.broadcasted_iota(jnp.int32, (N, N), 1)
    for k in range(per_device):
        col = spot_words_above[me, 0, 2 * k + 1]
        owner, col_shift = col // N, col % N
        after = (owner + 1) % scan_count
        for plane in range(2):
            cut[k, plane] = jnp.where(
                cols >= col_shift, band[owner, plane].astype(F32), band[after, plane].astype(F32)
            ).astype(BF16)
        cuts.append(remote(cut.at[k], below.at[k], cut_send.at[k], cut_recv.at[k], me, last_tile))
        cuts[-1].start()

    for move in cuts:
        move.wait()
    for move in sent:
        move.wait_send()
    above_copy.wait_send()

    @pl.loop(1, scan_count)
    def _(d):
        spot_copy(d).wait_send()


def gather(block, spots, probe, patterns, scan_count):
    per_device = patterns.shape[0]
    vmem = pl.BlockSpec(memory_space=pltpu.VMEM)
    words = (scan_count,) + spots.shape
    dma = pltpu.SemaphoreType.DMA
    return pl.pallas_call(
        gather_kernel,
        in_specs=[vmem] * 4,
        out_specs=[vmem] * 6,
        out_shape=[
            jax.ShapeDtypeStruct((scan_count, 2, N, N), BF16),
            jax.ShapeDtypeStruct((per_device, 2, N, N), BF16),
            jax.ShapeDtypeStruct(words, jnp.int32),
            jax.ShapeDtypeStruct((N, N), F32),
            jax.ShapeDtypeStruct(probe.shape, F32),
            jax.ShapeDtypeStruct(patterns.shape, F32),
        ],
        scratch_shapes=[
            pltpu.VMEM((per_device, 2, N, N), BF16),
            pltpu.VMEM(words, jnp.int32),
            pltpu.SMEM(words, jnp.int32),
            pltpu.SMEM(words, jnp.int32),
            pltpu.VMEM((N, N), F32),
            dma((30,)),
            dma((2 * scan_count,)),
            dma((scan_count,)),
            dma((scan_count,)),
            dma((per_device,)),
            dma((per_device,)),
            dma((2,)),
        ],
        compiler_params=pltpu.CompilerParams(
            collective_id=0, has_side_effects=True, vmem_limit_bytes=56 * 2**20
        ),
        name="gather",
    )(block, spots, probe, patterns)


def finish_kernel(
    pos,
    slots,
    sums,
    probe,
    field,
    cover,
    object_out,
    probe_out,
    received,
    core_in,
    x_out,
    x_in,
    y_part,
    y_in,
    z_in,
    coded,
    acc,
    spill_in,
    swap_in,
    tail_in,
    send_sem,
    recv_sem,
):
    scan_count, tile_count = lax.axis_size("scan"), lax.axis_size("tile")
    me, tile = lax.axis_index("scan"), lax.axis_index("tile")
    x, core = tile // 2, tile % 2
    y, z = me // 4, me % 4
    planes = sums.shape[0]
    pair, parity = me // 2, me % 2
    per_device = pos.shape[0] // scan_count
    CORE, XR, YR, ZR, YG, XG, CG, SP, SW, TL = 16, 17, 20, 23, 27, 31, 35, 39, 40, 41

    def copy(src, dst, send, recv, scan=None, tile_to=None):
        where = {"scan": me if scan is None else scan, "tile": tile if tile_to is None else tile_to}
        return pltpu.make_async_remote_copy(
            src_ref=src,
            dst_ref=dst,
            send_sem=send_sem.at[send],
            recv_sem=recv_sem.at[recv],
            device_id=where,
            device_id_type=MESH,
        )

    greet()
    partner = tile + 1 - 2 * core
    other_lanes = pl.ds(pl.multiple_of((1 - core) * H, H), H)
    own_lanes = pl.ds(pl.multiple_of(core * H, H), H)
    core_copy = copy(sums.at[:, :, other_lanes], core_in, CORE, CORE, tile_to=partner)
    core_copy.start()

    def update_copy(d):
        to = (me + d) % scan_count
        return copy(slots.at[to], received.at[d], d, d, scan=to)

    @pl.loop(1, scan_count)
    def _(d):
        update_copy(d).start()

    acc[...] = jnp.zeros_like(acc)

    def collect(source, ref):
        owner, row_shift, col_shift = jnp.int32(-4), jnp.int32(0), jnp.int32(0)
        for k in range(per_device):
            spot_row, spot_col = pos[source * per_device + k, 0], pos[source * per_device + k, 1]
            hit = spot_col // (2 * N) == pair
            owner = jnp.where(hit, spot_col // N, owner)
            row_shift = jnp.where(hit, spot_row % N, row_shift)
            col_shift = jnp.where(hit, spot_col % N, col_shift)
        side = owner - 2 * pair
        cols = lax.broadcasted_iota(jnp.int32, (32, N), 1)
        right = cols >= col_shift
        head = jnp.broadcast_to(side, (32, N)) == 0
        tail = jnp.broadcast_to(side, (32, N)) == 1
        picks = (head & right, (head & ~right) | (tail & right), tail & ~right)
        scale = decode_scale(ref[N:])

        for part in range(0, N, 32):
            rows = lax.broadcasted_iota(jnp.int32, (32, N), 0) + part
            value = decode(ref[part : part + 32], scale)
            low = rows < row_shift
            for block in range(3):
                taken = jnp.where(picks[block], value, 0.0)
                acc[0, block, part : part + 32] += jnp.where(low, 0.0, taken)
                acc[1, block, part : part + 32] += jnp.where(low, taken, 0.0)

    def collect_far(d, carry):
        update_copy(d).wait_recv()
        collect((me + scan_count - d) % scan_count, received.at[d])
        return carry

    collect(me, slots.at[me])

    core_copy.wait_recv()
    x_copies = []
    for d in range(1, 4):
        to = (x + d) % 4
        rows = pl.ds(pl.multiple_of(to * 64, 64), 64)
        chunk = sums[:, rows, own_lanes] + core_in[:, rows]
        code, tail = encode(chunk.reshape(planes * 64, H))
        x_out[d - 1, : planes * 64] = code
        x_out[d - 1, planes * 64 :] = tail
        x_copies.append(copy(x_out.at[d - 1], x_in.at[d - 1], XR + d - 1, XR + d - 1, tile_to=2 * to + core))
        x_copies[-1].start()
    rows = pl.ds(pl.multiple_of(x * 64, 64), 64)
    y_part[...] = sums[:, rows, own_lanes] + core_in[:, rows]

    lax.fori_loop(1, 8, collect_far, 0)

    for d in range(1, 4):
        x_copies[d - 1].wait_recv()
        scale = decode_scale(x_in[d - 1, planes * 64 :])
        y_part[...] += decode(x_in[d - 1, : planes * 64], scale).reshape(planes, 64, H)
    y_copies = []
    for d in range(1, 4):
        to = (y + d) % 4
        rows = pl.ds(pl.multiple_of(to * 16, 16), 16)
        y_copies.append(copy(y_part.at[:, rows], y_in.at[d - 1], YR + d - 1, YR + d - 1, scan=4 * to + z))
        y_copies[-1].start()

    lax.fori_loop(8, scan_count, collect_far, 0)
    below_tile = (tile + 1) % tile_count
    spill_copy = copy(acc.at[1], spill_in, SP, SP, tile_to=below_tile)
    spill_copy.start()

    rows = pl.ds(pl.multiple_of(y * 16, 16), 16)
    chunk = y_part[:, rows]
    for d in range(1, 4):
        y_copies[d - 1].wait_recv()
        chunk = chunk + y_in[d - 1]
    z_in[z] = chunk
    z_copies = []
    for d in range(1, 4):
        to = (z + d) % 4
        z_copies.append(copy(z_in.at[z], z_in.at[z], ZR + d, ZR + d, scan=4 * y + to))
        z_copies[-1].start()

    spill_copy.wait_recv()
    acc[0] += spill_in[...]
    swap_copy = copy(acc.at[0, 1 - parity], swap_in, SW, SW, scan=me + 1 - 2 * parity)
    swap_copy.start()
    tail_copy = copy(
        acc.at[0, 2], tail_in.at[parity], TL, TL + parity, scan=(me + 2 - parity) % scan_count
    )
    tail_copy.start()

    for d in range(1, 4):
        source = (z + 4 - d) % 4
        copy(z_in.at[source], z_in.at[source], ZR + d, ZR + d, scan=4 * y + source).wait_recv()
    total = z_in[0] + z_in[1] + z_in[2] + z_in[3]
    rows = pl.ds(pl.multiple_of(x * 64 + y * 16, 16), 16)
    old = probe[:, rows, own_lanes]
    fresh = (old + total[: planes - 1]) / (1.0 + total[planes - 1 :])
    code, tail = encode(fresh.reshape((planes - 1) * 16, H))
    spot = core * 16 + x * 4 + y
    coded[spot, : (planes - 1) * 16] = code
    coded[spot, (planes - 1) * 16 :] = tail

    yg_copies = []
    for d in range(1, 4):
        yg_copies.append(copy(coded.at[spot], coded.at[spot], YG + d, YG + d, scan=4 * ((y + d) % 4) + z))
        yg_copies[-1].start()
    for d in range(1, 4):
        source = core * 16 + x * 4 + (y + 4 - d) % 4
        copy(coded.at[source], coded.at[source], YG + d, YG + d, scan=4 * ((y + d) % 4) + z).wait_recv()

    group = pl.ds(core * 16 + x * 4, 4)
    xg_copies = []
    for d in range(1, 4):
        to = 2 * ((x + d) % 4) + core
        xg_copies.append(copy(coded.at[group], coded.at[group], XG + d, XG + d, tile_to=to))
        xg_copies[-1].start()
    cg_copies = [copy(coded.at[group], coded.at[group], CG, CG, tile_to=partner)]
    cg_copies[-1].start()

    swap_copy.wait_recv()

    @pl.when(parity == 0)
    def _():
        for plane in range(2):
            copy(acc.at[0, 2], tail_in.at[plane], TL, TL + plane, scan=(me + 2) % scan_count).wait_recv()
        share = 1.0 / (1.0 + cover[...])
        object_out[0] = (field[0] + (acc[0, 0] + tail_in[0])) * share
        object_out[1] = (field[1] + (swap_in[...] + tail_in[1])) * share

    @pl.when(parity == 1)
    def _():
        share = 1.0 / (1.0 + cover[...])
        object_out[0] = (field[0] + swap_in[...]) * share
        object_out[1] = (field[1] + acc[0, 1]) * share

    def show(core_at, x_at):
        for y_at in range(4):
            at = core_at * 16 + x_at * 4 + y_at
            scale = decode_scale(coded[at, (planes - 1) * 16 :])
            value = decode(coded[at, : (planes - 1) * 16], scale).reshape(planes - 1, 16, H)
            rows = pl.ds(pl.multiple_of(x_at * 64 + y_at * 16, 16), 16)
            lanes = pl.ds(pl.multiple_of(core_at * H, H), H)
            probe_out[:, rows, lanes] = value

    show(core, x)
    for d in range(1, 4):
        source = (x + 4 - d) % 4
        at = pl.ds(core * 16 + source * 4, 4)
        copy(coded.at[at], coded.at[at], XG + d, XG + d, tile_to=2 * source + core).wait_recv()
        cg_copies.append(copy(coded.at[at], coded.at[at], CG + d, CG + d, tile_to=partner))
        cg_copies[-1].start()
        show(core, source)
    for d in range(4):
        source = (x + 4 - d) % 4
        at = pl.ds((1 - core) * 16 + source * 4, 4)
        copy(coded.at[at], coded.at[at], CG + d, CG + d, tile_to=partner).wait_recv()
        show(1 - core, source)

    @pl.loop(1, scan_count)
    def _(d):
        update_copy(d).wait_send()

    for started in [core_copy, spill_copy, swap_copy, tail_copy] + x_copies + y_copies + z_copies:
        started.wait_send()
    for started in yg_copies + xg_copies + cg_copies:
        started.wait_send()


def finish(pos, slots, sums, probe, field, cover):
    scan_count = slots.shape[0]
    planes = sums.shape[0]
    vmem = pl.BlockSpec(memory_space=pltpu.VMEM)
    return pl.pallas_call(
        finish_kernel,
        in_specs=[pl.BlockSpec(memory_space=pltpu.SMEM)] + [vmem] * 5,
        out_specs=[vmem, vmem],
        out_shape=[jax.ShapeDtypeStruct(field.shape, F32), jax.ShapeDtypeStruct(probe.shape, F32)],
        scratch_shapes=[
            pltpu.VMEM((scan_count, N + TAIL, N), I16),
            pltpu.VMEM((planes, N, H), F32),
            pltpu.VMEM((3, planes * 64 + TAIL, H), I16),
            pltpu.VMEM((3, planes * 64 + TAIL, H), I16),
            pltpu.VMEM((planes, 64, H), F32),
            pltpu.VMEM((3, planes, 16, H), F32),
            pltpu.VMEM((4, planes, 16, H), F32),
            pltpu.VMEM((32, (planes - 1) * 16 + TAIL, H), I16),
            pltpu.VMEM((2, 3, N, N), F32),
            pltpu.VMEM((3, N, N), F32),
            pltpu.VMEM((N, N), F32),
            pltpu.VMEM((2, N, N), F32),
            pltpu.SemaphoreType.DMA((44,)),
            pltpu.SemaphoreType.DMA((44,)),
        ],
        compiler_params=pltpu.CompilerParams(
            collective_id=1, has_side_effects=True, vmem_limit_bytes=56 * 2**20
        ),
        name="finish",
    )(pos, slots, sums, probe, field, cover)


def body(object_field, probe_modes, patterns, positions):
    scan_count = lax.axis_size("scan")
    table = jnp.asarray(folded_tables())
    spots = jnp.zeros((8, 128), jnp.int32).at[0, : positions.size].set(positions.reshape(-1))
    flat_probe = probe_modes.reshape(-1, N, N)
    band, below, words, cover, folded_probe, level = gather(
        object_field.astype(BF16), spots, flat_probe, patterns, scan_count
    )
    slots, sums = project(positions, band, below, level, folded_probe, table)
    pos_own = words[:, 0, : positions.size].reshape(-1, 2)
    object_now, probe_now = finish(pos_own, slots, sums, flat_probe, object_field, cover)
    return (object_now, probe_now.reshape(probe_modes.shape))


def solution(mesh):
    return jax.shard_map(
        body,
        mesh=mesh,
        in_specs=(
            P(None, "tile", "scan"),
            P(),
            P(("scan", "tile"), None, None),
            P(("scan", "tile"), None),
        ),
        out_specs=(P(None, "tile", "scan"), P()),
        check_vma=False,
    )
```

```python
import functools
import math

import jax
import jax.numpy as jnp
import ml_dtypes
import numpy as np
from jax import lax
from jax.experimental import pallas as pl
from jax.experimental.pallas import tpu as pltpu
from jax.sharding import PartitionSpec as P

F32 = jnp.float32
BF16 = jnp.bfloat16
N = 256
H = N // 2
I16 = jnp.int16
TAIL = 16
GROUPS = 4
UNROLL = 4
STRIP = 32
FULL = 32767.0
MESH = pl.DeviceIdType.MESH


def folded_tables():
    counter = np.arange(N, dtype=np.int32)
    phase = counter[:, None] * counter[None, :] % N
    angle = phase.astype(np.float32) * np.float32(2.0 * math.pi / N)
    factor = np.float32(1.0 / math.sqrt(N))
    cosine = (np.cos(angle) * factor).astype(ml_dtypes.bfloat16)
    sine = (np.sin(angle) * factor).astype(ml_dtypes.bfloat16)
    order = np.where(counter <= H, counter, 3 * H - counter)
    right = np.concatenate([cosine[:, : H + 1], sine[:, 1:H]], axis=1)[order]
    return np.stack([right, np.ascontiguousarray(right.T)])


def dot(left, right):
    return jnp.dot(left, right, preferred_element_type=F32)


def iota(axis):
    return lax.broadcasted_iota(jnp.int32, (N, N), axis)


def folded(index):
    return jnp.where(index <= H, index, 3 * H - index)


def one_hot(condition):
    return jnp.where(condition, 1.0, 0.0).astype(BF16)


def pieces(value, count):
    parts = []
    for _ in range(count):
        part = value.astype(BF16)
        parts.append(part)
        value = value - part.astype(F32)
    return parts


def permute(value, left, right, count):
    rows = sum(dot(left, part) for part in pieces(value, count))
    return sum(dot(part, right) for part in pieces(rows, count))


def encode(value):
    size = jnp.abs(value)
    peak = jnp.maximum(jnp.max(size, axis=0, keepdims=True), 1e-30)
    exponent = jnp.ceil(jnp.log(peak) * (1.0 / math.log(2.0)) + 1e-5)
    scale = jnp.exp(exponent * -math.log(2.0))
    code = jnp.minimum(jnp.sqrt(size * scale) * FULL + 0.5, FULL).astype(jnp.int32)
    code = jnp.where(value < 0.0, -code, code).astype(I16)
    tail = jnp.broadcast_to(exponent.astype(jnp.int32), (TAIL, value.shape[1])).astype(I16)
    return code, tail


def decode_scale(tail):
    exponent = tail.astype(jnp.int32).astype(F32)[:1]
    return jnp.exp(exponent * math.log(2.0)) * (1.0 / (FULL * FULL))


def decode(code, scale):
    code = code.astype(jnp.int32).astype(F32)
    return code * jnp.abs(code) * scale


def fold(a_lo, a_hi, b_lo, b_hi, sign, first):
    if first is None:
        return a_lo - sign * b_hi, b_lo + sign * a_hi, a_lo + sign * b_hi, b_lo - sign * a_hi
    a_in = jnp.where(first, 0.0, a_hi)
    b_in = jnp.where(first, 0.0, b_hi)
    return (
        a_lo - sign * b_in,
        b_lo + sign * a_in,
        jnp.where(first, a_hi, a_lo + sign * b_hi),
        jnp.where(first, b_hi, b_lo - sign * a_hi),
    )


def right_stage(re, im, table, half, sign):
    both = dot(jnp.concatenate([re, im], axis=0), table)
    a, b = both[:N], both[N:]
    first = lax.broadcasted_iota(jnp.int32, (N, H), 1) == 0
    re_lo, im_lo, re_hi, im_hi = fold(a[:, :H], a[:, H:], b[:, :H], b[:, H:], sign, first)
    half[:, :H] = re_lo.astype(BF16)
    half[:, H:N] = re_hi.astype(BF16)
    half[:, N : N + H] = im_lo.astype(BF16)
    half[:, N + H :] = im_hi.astype(BF16)


def left_strip(flat, at, sign):
    first = lax.broadcasted_iota(jnp.int32, (STRIP, N), 0) == 0 if at == 0 else None
    low, high = slice(at, at + STRIP), slice(H + at, H + at + STRIP)
    re_lo, im_lo, re_hi, im_hi = fold(flat[low, :N], flat[high, :N], flat[low, N:], flat[high, N:], sign, first)
    return (low, re_lo, im_lo), (high, re_hi, im_hi)


def remote(src, dst, send, recv, scan, tile):
    return pltpu.make_async_remote_copy(
        src_ref=src,
        dst_ref=dst,
        send_sem=send,
        recv_sem=recv,
        device_id={"scan": scan, "tile": tile},
        device_id_type=MESH,
    )


def greet():
    scan_count, tile_count = lax.axis_size("scan"), lax.axis_size("tile")
    me, tile = lax.axis_index("scan"), lax.axis_index("tile")
    barrier = pltpu.get_barrier_semaphore()

    @pl.loop(1, scan_count)
    def _(d):
        pl.semaphore_signal(barrier, 1, device_id={"scan": (me + d) % scan_count, "tile": tile}, device_id_type=MESH)

    @pl.loop(1, tile_count)
    def _(d):
        pl.semaphore_signal(barrier, 1, device_id={"scan": me, "tile": (tile + d) % tile_count}, device_id_type=MESH)

    pl.semaphore_wait(barrier, scan_count + tile_count - 2)


def sweep_kernel(
    field,
    spots,
    table,
    probe,
    patterns,
    coded,
    numer,
    cover,
    block,
    band,
    below,
    cut,
    spots_own,
    spots_above,
    spot_words,
    spot_words_above,
    power_total,
    probe_chunk,
    folded_probe,
    level,
    patch,
    far,
    power,
    halves,
    flats,
    sums,
    update,
    queue,
    slots,
    received,
    core_in,
    x_out,
    x_in,
    y_part,
    y_in,
    z_in,
    den_chunk,
    acc,
    spill_in,
    swap_in,
    tail_in,
    send_sem,
    recv_sem,
    spot_send,
    spot_recv,
    cut_send,
    cut_recv,
    move_send,
    move_recv,
    sum_send,
    sum_recv,
    local_sem,
):
    scan_count, tile_count = lax.axis_size("scan"), lax.axis_size("tile")
    me, tile = lax.axis_index("scan"), lax.axis_index("tile")
    x, core = tile // 2, tile % 2
    y, z = me // 4, me % 4
    pair, parity = me // 2, me % 2
    partner = tile + 1 - 2 * core
    next_tile, last_tile = (tile + 1) % tile_count, (tile + tile_count - 1) % tile_count
    per_device = level.shape[0]
    modes = folded_probe.shape[0] // 2
    other_lanes = pl.ds(pl.multiple_of((1 - core) * H, H), H)
    own_lanes = pl.ds(pl.multiple_of(core * H, H), H)

    probe_load = pltpu.make_async_copy(probe, far.at[0], local_sem.at[0])
    probe_load.start()
    pattern_load = pltpu.make_async_copy(patterns, level, local_sem.at[1])
    pattern_load.start()
    block[...] = field[...].astype(BF16)
    greet()

    def spot_copy(d):
        return remote(spots, spots_own.at[me], spot_send.at[d], spot_recv.at[d], (me + d) % scan_count, tile)

    @pl.loop(1, scan_count)
    def _(d):
        spot_copy(d).start()

    def along(plane, stage, d):
        turn_z = (plane == 0) == (stage == 0)
        return 4 * y + (z + d) % 4 if turn_z else 4 * ((y + d) % 4) + z

    sent = []

    def push(src, source, plane, stage, d):
        move = remote(
            src,
            band.at[source, plane],
            send_sem.at[len(sent)],
            recv_sem.at[2 * source + plane],
            along(plane, stage, d),
            tile,
        )
        move.start()
        sent.append(move)

    for stage in range(2):
        for d in (1, 3, 2):
            for plane in range(2):
                push(block.at[plane], me, plane, stage, d)

    def landed(source, plane):
        remote(
            block.at[plane], band.at[source, plane], send_sem.at[0], recv_sem.at[2 * source + plane], along(0, 0, 1), tile
        ).wait_recv()

    spots_own[me] = spots[...]
    band[me] = block[...]
    probe_load.wait()
    total = jnp.zeros((N, N), F32)
    for m in range(modes):
        for plane in range(2):
            value = far[0, m, plane]
            total = total + value * value
    power_total[...] = total

    for d in (3, 1, 2):
        for plane in range(2):
            source = along(plane, 0, d)
            landed(source, plane)
            for turn in (1, 3, 2):
                push(band.at[source, plane], source, plane, 1, turn)

    @pl.loop(1, scan_count)
    def _(d):
        source = (me + scan_count - d) % scan_count
        remote(spots, spots_own.at[source], spot_send.at[d], spot_recv.at[d], source, tile).wait_recv()

    above_copy = remote(spots_own, spots_above, spot_send.at[0], spot_recv.at[0], me, next_tile)
    above_copy.start()
    words_copy = pltpu.make_async_copy(spots_own, spot_words, local_sem.at[2])
    words_copy.start()

    fold_matrix = one_hot(iota(0) == folded(iota(1)))
    chunk_rows = pl.ds(pl.multiple_of(x * 64 + y * 16, 16), 16)

    @pl.loop(0, modes)
    def _(m):
        for plane in range(2):
            folded_probe[2 * m + plane] = permute(far[0, m, plane], fold_matrix, fold_matrix, 3)
            probe_chunk[2 * m + plane] = far[0, m, plane, chunk_rows, own_lanes]

    pattern_load.wait()

    @pl.loop(0, per_device)
    def _(k):
        level[k] = jnp.sqrt(permute(level[k], fold_matrix, fold_matrix, 3))

    cover[...] = jnp.zeros_like(cover)

    def add_cover(words, above):
        @pl.loop(0, scan_count)
        def _(source):
            head, row_shift, col_shift = jnp.int32(-1), jnp.int32(0), jnp.int32(0)
            for k in range(per_device):
                row, col = words[source, 0, 2 * k], words[source, 0, 2 * k + 1]
                owner = col // N
                first = owner == me
                hit = first | ((owner + 1) % scan_count == me)
                head = jnp.where(hit, first.astype(jnp.int32), head)
                row_shift = jnp.where(hit, row % N, row_shift)
                col_shift = jnp.where(hit, col % N, col_shift)
            start = jnp.where(head == 1, col_shift, 0)
            stop = jnp.where(head == 1, N, jnp.where(head == 0, col_shift, 0))
            rows, cols = iota(0), iota(1)
            moved = pltpu.roll(pltpu.roll(power_total[...], row_shift, 0), col_shift, 1)
            keep = (rows < row_shift) if above else (rows >= row_shift)
            cover[...] += jnp.where(keep & (cols >= start) & (cols < stop), moved, 0.0)

    words_copy.wait()
    add_cover(spot_words, False)
    above_copy.wait_recv()
    words_copy = pltpu.make_async_copy(spots_above, spot_words_above, local_sem.at[3])
    words_copy.start()
    words_copy.wait()
    add_cover(spot_words_above, True)

    for d in (3, 1, 2):
        for plane in range(2):
            for turn in (3, 1, 2):
                if plane == 0:
                    source = 4 * ((y + turn) % 4) + (z + d) % 4
                else:
                    source = 4 * ((y + d) % 4) + (z + turn) % 4
                landed(source, plane)
    for turn in (3, 1, 2):
        landed(4 * ((y + turn) % 4) + z, 0)
        landed(4 * y + (z + turn) % 4, 1)

    def composite(col, plane):
        owner, col_shift = col // N, col % N
        after = (owner + 1) % scan_count
        return jnp.where(iota(1) >= col_shift, band[owner, plane].astype(F32), band[after, plane].astype(F32))

    def cut_copy(k):
        return remote(cut.at[k], below.at[k], cut_send.at[k], cut_recv.at[k], me, last_tile)

    @pl.loop(0, per_device)
    def _(k):
        for plane in range(2):
            cut[k, plane] = composite(spot_words_above[me, 0, 2 * k + 1], plane).astype(BF16)
        cut_copy(k).start()

    update[...] = jnp.zeros_like(update)
    sums[...] = jnp.zeros_like(sums)
    acc[...] = jnp.zeros_like(acc)
    queue[per_device] = jnp.zeros(queue.shape[1:], I16)

    @pl.loop(0, per_device)
    def _(k):
        row, col = spot_words[me, 0, 2 * k], spot_words[me, 0, 2 * k + 1]
        row_shift, col_shift = row % N, col % N
        cut_copy(k).wait_recv()
        row_pick = one_hot(iota(1) == (row_shift + folded(iota(0))) % N)
        col_pick = one_hot(iota(0) == (col_shift + folded(iota(1))) % N)
        for plane in range(2):
            top = composite(col, plane)
            window = jnp.where(iota(0) >= row_shift, top, below[k, plane].astype(F32)).astype(BF16)
            patch[k, plane] = dot(dot(row_pick, window).astype(BF16), col_pick)
        sums[0] += patch[k, 0] * patch[k, 0] + patch[k, 1] * patch[k, 1]
        power[k] = jnp.full((N, N), 0.25, F32)

        @pl.loop(0, modes // UNROLL)
        def _(part):
            for u in range(UNROLL):
                m = part * UNROLL + u
                half, flat = halves.at[u], flats.at[u]
                p_re, p_im = folded_probe[2 * m], folded_probe[2 * m + 1]
                o_re, o_im = patch[k, 0], patch[k, 1]
                wave_re = (p_re * o_re - p_im * o_im).astype(BF16)
                wave_im = (p_re * o_im + p_im * o_re).astype(BF16)
                right_stage(wave_re, wave_im, table[0], half, -1.0)
                flat[...] = dot(table[1], half[...])
                for at in range(0, H, STRIP):
                    for rows, f_re, f_im in left_strip(flat, at, -1.0):
                        far[k, m, 0, rows] = f_re
                        far[k, m, 1, rows] = f_im
                        power[k, rows] += f_re * f_re + f_im * f_im

        power[k] = level[k] / jnp.sqrt(power[k])

    sums[0] = permute(sums[0], fold_matrix, fold_matrix, 2)

    PER_GROUP = 20

    def span(g):
        return (0, 2 * modes // GROUPS + 1) if g == 0 else (1 + g * (2 * modes // GROUPS), 2 * modes // GROUPS)

    def sum_copy(src, dst, g, number, scan=None, tile_to=None):
        return remote(
            src,
            dst,
            sum_send.at[g * PER_GROUP + number],
            sum_recv.at[g * PER_GROUP + number],
            me if scan is None else scan,
            tile if tile_to is None else tile_to,
        )

    def core_copy(g):
        start, count = span(g)
        planes = pl.ds(start, count)
        return sum_copy(sums.at[planes, :, other_lanes], core_in.at[planes], g, 0, tile_to=partner)

    def x_copy(g, d):
        used = pl.ds(0, span(g)[1] * 64 + TAIL)
        return sum_copy(
            x_out.at[g, d - 1, used], x_in.at[g, d - 1, used], g, d, tile_to=2 * ((x + d) % 4) + core
        )

    def y_copy(g, d):
        start, count = span(g)
        planes = pl.ds(start, count)
        rows = pl.ds(pl.multiple_of((y + d) % 4 * 16, 16), 16)
        return sum_copy(
            y_part.at[planes, rows], y_in.at[d - 1, planes], g, 3 + d, scan=4 * ((y + d) % 4) + z
        )

    def z_copy(g, d, source):
        planes = pl.ds(*span(g))
        return sum_copy(z_in.at[source, planes], z_in.at[source, planes], g, 6 + d, scan=4 * y + (z + d) % 4)

    def yg_copy(g, d, source):
        at = core * 16 + x * 4 + source
        return sum_copy(coded.at[at, g], coded.at[at, g], g, 9 + d, scan=4 * ((y + d) % 4) + z)

    def xg_copy(g, d, source):
        at = pl.ds(core * 16 + source * 4, 4)
        return sum_copy(coded.at[at, g], coded.at[at, g], g, 12 + d, tile_to=2 * ((x + d) % 4) + core)

    def cg_copy(g, d, side):
        at = pl.ds(side * 16 + (x + 4 - d) % 4 * 4, 4)
        return sum_copy(coded.at[at, g], coded.at[at, g], g, 16 + d, tile_to=partner)

    def stage_core(g):
        core_copy(g).start()

    def stage_x(g):
        start, count = span(g)
        planes = pl.ds(start, count)
        core_copy(g).wait_recv()
        for d in range(1, 4):
            rows = pl.ds(pl.multiple_of((x + d) % 4 * 64, 64), 64)
            chunk = sums[planes, rows, own_lanes] + core_in[planes, rows]
            code, tail = encode(chunk.reshape(count * 64, H))
            x_out[g, d - 1, : count * 64] = code
            x_out[g, d - 1, count * 64 : count * 64 + TAIL] = tail
            x_copy(g, d).start()
        rows = pl.ds(pl.multiple_of(x * 64, 64), 64)
        y_part[planes] = sums[planes, rows, own_lanes] + core_in[planes, rows]

    def stage_y(g):
        start, count = span(g)
        planes = pl.ds(start, count)
        for d in range(1, 4):
            x_copy(g, d).wait_recv()
            scale = decode_scale(x_in[g, d - 1, count * 64 : count * 64 + TAIL])
            y_part[planes] += decode(x_in[g, d - 1, : count * 64], scale).reshape(count, 64, H)
        for d in range(1, 4):
            y_copy(g, d).start()

    def stage_z(g):
        start, count = span(g)
        planes = pl.ds(start, count)
        chunk = y_part[planes, pl.ds(pl.multiple_of(y * 16, 16), 16)]
        for d in range(1, 4):
            y_copy(g, d).wait_recv()
            chunk = chunk + y_in[d - 1, planes]
        z_in[z, planes] = chunk
        for d in range(1, 4):
            z_copy(g, d, z).start()

    def stage_back(g):
        start, count = span(g)
        planes = pl.ds(start, count)
        for d in range(1, 4):
            z_copy(g, d, (z + 4 - d) % 4).wait_recv()
        whole = z_in[0, planes] + z_in[1, planes] + z_in[2, planes] + z_in[3, planes]
        if g == 0:
            den_chunk[...] = 1.0 / (1.0 + whole[0])
            whole = whole[1:]
        width = 2 * modes // GROUPS
        fresh = (probe_chunk[pl.ds(g * width, width)] + whole) * den_chunk[...][None]
        code, tail = encode(fresh.reshape(width * 16, H))
        at = core * 16 + x * 4 + y
        coded[at, g, : width * 16] = code
        coded[at, g, width * 16 :] = tail
        for d in range(1, 4):
            yg_copy(g, d, y).start()

    def stage_x_back(g):
        for d in range(1, 4):
            yg_copy(g, d, (y + 4 - d) % 4).wait_recv()
        for d in range(1, 4):
            xg_copy(g, d, x).start()
        cg_copy(g, 0, core).start()

    def stage_core_back(g):
        for d in range(1, 4):
            xg_copy(g, d, (x + 4 - d) % 4).wait_recv()
            cg_copy(g, d, core).start()

    def stage_end(g):
        for d in range(4):
            cg_copy(g, d, 1 - core).wait_recv()

    stages = (stage_core, stage_x, stage_y, stage_z, stage_back, stage_x_back, stage_core_back, stage_end)

    def tick(n):
        for number in range(len(stages) - 1, -1, -1):
            if 0 <= n - number < GROUPS:
                stages[number](n - number)

    width = modes // GROUPS

    @pl.loop(0, GROUPS)
    def _(n):
        @pl.loop(0, width)
        def _(part):
            m = n * width + part
            for k in range(per_device):
                half, flat = halves.at[k % UNROLL], flats.at[k % UNROLL]
                scaling = power[k]
                fixed_re = (far[k, m, 0] * scaling).astype(BF16)
                fixed_im = (far[k, m, 1] * scaling).astype(BF16)
                right_stage(fixed_re, fixed_im, table[0], half, 1.0)
                flat[...] = dot(table[1], half[...])
                for at in range(0, H, STRIP):
                    for rows, e_re, e_im in left_strip(flat, at, 1.0):
                        p_re, p_im = folded_probe[2 * m, rows], folded_probe[2 * m + 1, rows]
                        o_re, o_im = patch[k, 0, rows], patch[k, 1, rows]
                        update[k, 0, rows] += p_re * e_re + p_im * e_im
                        update[k, 1, rows] += p_re * e_im - p_im * e_re
                        sums[1 + 2 * m, rows] += o_re * e_re + o_im * e_im
                        sums[2 + 2 * m, rows] += o_re * e_im - o_im * e_re
            for plane in range(2):
                at = 1 + 2 * m + plane
                sums[at] = permute(sums[at], fold_matrix, fold_matrix, 2)

        for step in range(GROUPS):
            @pl.when(n == step)
            def _():
                tick(step)

    @pl.loop(0, per_device)
    def _(k):
        row_shift, col_shift = spot_words[me, 0, 2 * k] % N, spot_words[me, 0, 2 * k + 1] % N
        row_back = one_hot(iota(0) == (row_shift + folded(iota(1))) % N)
        col_back = one_hot(iota(1) == (col_shift + folded(iota(0))) % N)
        for plane in range(2):
            code, tail = encode(permute(update[k, plane], row_back, col_back, 2))
            queue[k, plane, :N] = code
            queue[k, plane, N:] = tail

    @pl.loop(0, scan_count // 2)
    def _(q):
        pick = jnp.int32(per_device)
        for k in range(per_device):
            pick = jnp.where(spot_words[me, 0, 2 * k + 1] // (2 * N) == q, k, pick)
        for plane in range(2):
            slots[2 * q + plane] = queue[pick, plane]

    def update_copy(dy, dz):
        to = 4 * ((y + dy) % 4) + (z + dz) % 4
        j = 4 * dy + dz
        return remote(slots.at[to], received.at[j], move_send.at[j], move_recv.at[j], to, tile)

    hops = (0, 1, 2, 1)
    order = sorted(((dy, dz) for dy in range(4) for dz in range(4) if dy or dz), key=lambda d: -hops[d[0]] - hops[d[1]])
    for dy, dz in order:
        update_copy(dy, dz).start()

    def collect(source, ref):
        owner, row_shift, col_shift = jnp.int32(-4), jnp.int32(0), jnp.int32(0)
        for k in range(per_device):
            spot_row, spot_col = spot_words[source, 0, 2 * k], spot_words[source, 0, 2 * k + 1]
            hit = spot_col // (2 * N) == pair
            owner = jnp.where(hit, spot_col // N, owner)
            row_shift = jnp.where(hit, spot_row % N, row_shift)
            col_shift = jnp.where(hit, spot_col % N, col_shift)
        side = owner - 2 * pair
        cols = lax.broadcasted_iota(jnp.int32, (STRIP, N), 1)
        right = cols >= col_shift
        head = jnp.broadcast_to(side, (STRIP, N)) == 0
        tail = jnp.broadcast_to(side, (STRIP, N)) == 1
        picks = (head & right, (head & ~right) | (tail & right), tail & ~right)
        scale = decode_scale(ref[N:])

        for part in range(0, N, STRIP):
            rows = lax.broadcasted_iota(jnp.int32, (STRIP, N), 0) + part
            value = decode(ref[part : part + STRIP], scale)
            low = rows < row_shift
            for at in range(3):
                taken = jnp.where(picks[at], value, 0.0)
                acc[0, at, part : part + STRIP] += jnp.where(low, 0.0, taken)
                acc[1, at, part : part + STRIP] += jnp.where(low, taken, 0.0)

    def collect_some(picked):
        for dy, dz in picked:
            update_copy(dy, dz).wait_recv()
            collect(4 * ((y + 4 - dy) % 4) + (z + 4 - dz) % 4, received.at[4 * dy + dz])

    collect(me, slots.at[me])
    tick(GROUPS)
    collect_some(order[:5])
    tick(GROUPS + 1)
    collect_some(order[5:10])
    tick(GROUPS + 2)
    collect_some(order[10:])

    spill_copy = remote(acc.at[1], spill_in, move_send.at[16], move_recv.at[16], me, next_tile)
    spill_copy.start()
    tick(GROUPS + 3)
    spill_copy.wait_recv()
    acc[0] += spill_in[...]
    swap_copy = remote(
        acc.at[0, 1 - parity], swap_in, move_send.at[17], move_recv.at[17], me + 1 - 2 * parity, tile
    )
    swap_copy.start()

    def tail_copy(plane):
        to = (me + 2 - parity) % scan_count
        return remote(acc.at[0, 2], tail_in.at[plane], move_send.at[18], move_recv.at[18 + plane], to, tile)

    tail_copy(parity).start()
    tick(GROUPS + 4)
    swap_copy.wait_recv()

    @pl.when(parity == 0)
    def _():
        for plane in range(2):
            tail_copy(plane).wait_recv()
        numer[0] = acc[0, 0] + tail_in[0]
        numer[1] = swap_in[...] + tail_in[1]

    @pl.when(parity == 1)
    def _():
        numer[0] = swap_in[...]
        numer[1] = acc[0, 1]

    for n in range(GROUPS + 5, GROUPS + len(stages)):
        tick(n)

    for move in sent:
        move.wait_send()
    above_copy.wait_send()

    @pl.loop(1, scan_count)
    def _(d):
        spot_copy(d).wait_send()

    @pl.loop(0, per_device)
    def _(k):
        cut_copy(k).wait_send()

    for dy, dz in order:
        update_copy(dy, dz).wait_send()
    spill_copy.wait_send()
    swap_copy.wait_send()
    tail_copy(parity).wait_send()
    for g in range(GROUPS):
        core_copy(g).wait_send()
        cg_copy(g, 0, core).wait_send()
        for d in range(1, 4):
            x_copy(g, d).wait_send()
            y_copy(g, d).wait_send()
            z_copy(g, d, z).wait_send()
            yg_copy(g, d, y).wait_send()
            xg_copy(g, d, x).wait_send()
            cg_copy(g, d, core).wait_send()


def sweep(field, spots, table, probe, patterns, scan_count):
    per_device, modes = patterns.shape[0], probe.shape[0]
    planes = 2 * modes + 1
    width = 2 * modes // GROUPS
    vmem, anywhere = pl.BlockSpec(memory_space=pltpu.VMEM), pl.BlockSpec(memory_space=pl.ANY)
    words = (scan_count,) + spots.shape
    dma, mem = pltpu.SemaphoreType.DMA, pltpu.VMEM
    slot = (N + TAIL, N)
    return pl.pallas_call(
        sweep_kernel,
        in_specs=[vmem, vmem, vmem, anywhere, anywhere],
        out_specs=[vmem, vmem, vmem],
        out_shape=[
            jax.ShapeDtypeStruct((2 * scan_count, GROUPS, width * 16 + TAIL, H), I16),
            jax.ShapeDtypeStruct((2, N, N), F32),
            jax.ShapeDtypeStruct((N, N), F32),
        ],
        scratch_shapes=[
            mem((2, N, N), BF16),
            mem((scan_count, 2, N, N), BF16),
            mem((per_device, 2, N, N), BF16),
            mem((per_device, 2, N, N), BF16),
            mem(words, jnp.int32),
            mem(words, jnp.int32),
            pltpu.SMEM(words, jnp.int32),
            pltpu.SMEM(words, jnp.int32),
            mem((N, N), F32),
            mem((2 * modes, 16, H), F32),
            mem((2 * modes, N, N), F32),
            mem((per_device, N, N), F32),
            mem((per_device, 2, N, N), F32),
            mem((per_device, modes, 2, N, N), F32),
            mem((per_device, N, N), F32),
            mem((UNROLL, N, 2 * N), BF16),
            mem((UNROLL, N, 2 * N), F32),
            mem((planes, N, N), F32),
            mem((per_device, 2, N, N), F32),
            mem((per_device + 1, 2) + slot, I16),
            mem((scan_count,) + slot, I16),
            mem((scan_count,) + slot, I16),
            mem((planes, N, H), F32),
            mem((GROUPS, 3, (width + 1) * 64 + TAIL, H), I16),
            mem((GROUPS, 3, (width + 1) * 64 + TAIL, H), I16),
            mem((planes, 64, H), F32),
            mem((3, planes, 16, H), F32),
            mem((4, planes, 16, H), F32),
            mem((16, H), F32),
            mem((2, 3, N, N), F32),
            mem((3, N, N), F32),
            mem((N, N), F32),
            mem((2, N, N), F32),
            dma((30,)),
            dma((2 * scan_count,)),
            dma((scan_count,)),
            dma((scan_count,)),
            dma((per_device,)),
            dma((per_device,)),
            dma((20,)),
            dma((20,)),
            dma((20 * GROUPS,)),
            dma((20 * GROUPS,)),
            dma((4,)),
        ],
        compiler_params=pltpu.CompilerParams(
            collective_id=0, has_side_effects=True, vmem_limit_bytes=62 * 2**20
        ),
        name="sweep",
    )(field, spots, table, probe, patterns)


def final_kernel(coded, numer, cover, field, object_out, probe_out):
    share = 1.0 / (1.0 + cover[...])
    for plane in range(2):
        object_out[plane] = (field[plane] + numer[plane]) * share
    width = (coded.shape[4] - TAIL) // 16
    for core in range(2):
        for at in range(4):
            for g in range(GROUPS):
                scale = decode_scale(coded[core, 0, at, g, width * 16 :])
                value = decode(coded[core, 0, at, g, : width * 16], scale).reshape(width, 16, H)
                probe_out[width * g : width * (g + 1), 16 * at : 16 * (at + 1), core * H : (core + 1) * H] = value


def final(coded, numer, cover, field, planes):
    coded = coded.reshape((2, 4, 4) + coded.shape[1:])
    rows = N // 4
    return pl.pallas_call(
        final_kernel,
        grid=(4,),
        in_specs=[
            pl.BlockSpec((2, 1) + coded.shape[2:], lambda i: (0, i, 0, 0, 0, 0)),
            pl.BlockSpec((2, rows, N), lambda i: (0, i, 0)),
            pl.BlockSpec((rows, N), lambda i: (i, 0)),
            pl.BlockSpec((2, rows, N), lambda i: (0, i, 0)),
        ],
        out_specs=[
            pl.BlockSpec((2, rows, N), lambda i: (0, i, 0)),
            pl.BlockSpec((planes, rows, N), lambda i: (0, i, 0)),
        ],
        out_shape=[jax.ShapeDtypeStruct((2, N, N), F32), jax.ShapeDtypeStruct((planes, N, N), F32)],
        compiler_params=pltpu.CompilerParams(vmem_limit_bytes=40 * 2**20),
        name="final",
    )(coded, numer, cover, field)


def body(object_field, probe_modes, patterns, positions):
    scan_count = lax.axis_size("scan")
    table = jnp.asarray(folded_tables())
    spots = jnp.zeros((8, 128), jnp.int32).at[0, : positions.size].set(positions.reshape(-1))
    coded, numer, cover = sweep(object_field, spots, table, probe_modes, patterns, scan_count)
    planes = 2 * probe_modes.shape[0]
    object_now, probe_now = final(coded, numer, cover, object_field, planes)
    return (object_now, probe_now.reshape(probe_modes.shape))


def solution(mesh):
    return jax.shard_map(
        body,
        mesh=mesh,
        in_specs=(
            P(None, "tile", "scan"),
            P(),
            P(("scan", "tile"), None, None),
            P(("scan", "tile"), None),
        ),
        out_specs=(P(None, "tile", "scan"), P()),
        check_vma=False,
    )
```

```python
import functools
import math

import jax
import jax.numpy as jnp
import ml_dtypes
import numpy as np
from jax import lax
from jax.experimental import pallas as pl
from jax.experimental.pallas import tpu as pltpu
from jax.sharding import PartitionSpec as P

F32 = jnp.float32
BF16 = jnp.bfloat16
N = 256
H = N // 2
I16 = jnp.int16
TAIL = 16
GROUPS = 4
UNROLL = 4
STRIP = 32
FULL = 32767.0
MESH = pl.DeviceIdType.MESH


def folded_tables():
    counter = np.arange(N, dtype=np.int32)
    phase = counter[:, None] * counter[None, :] % N
    angle = phase.astype(np.float32) * np.float32(2.0 * math.pi / N)
    factor = np.float32(1.0 / math.sqrt(N))
    cosine = (np.cos(angle) * factor).astype(ml_dtypes.bfloat16)
    sine = (np.sin(angle) * factor).astype(ml_dtypes.bfloat16)
    order = np.where(counter <= H, counter, 3 * H - counter)
    right = np.concatenate([cosine[:, : H + 1], sine[:, 1:H]], axis=1)[order]
    return np.stack([right, np.ascontiguousarray(right.T)])


def dot(left, right):
    return jnp.dot(left, right, preferred_element_type=F32)


def iota(axis):
    return lax.broadcasted_iota(jnp.int32, (N, N), axis)


def folded(index):
    return jnp.where(index <= H, index, 3 * H - index)


def one_hot(condition):
    return jnp.where(condition, 1.0, 0.0).astype(BF16)


def pieces(value, count):
    parts = []
    for _ in range(count):
        part = value.astype(BF16)
        parts.append(part)
        value = value - part.astype(F32)
    return parts


def permute(value, left, right, count):
    rows = sum(dot(left, part) for part in pieces(value, count))
    return sum(dot(part, right) for part in pieces(rows, count))


def encode(value):
    size = jnp.abs(value)
    peak = jnp.maximum(jnp.max(size, axis=0, keepdims=True), 1e-30)
    exponent = jnp.ceil(jnp.log(peak) * (1.0 / math.log(2.0)) + 1e-5)
    scale = jnp.exp(exponent * -math.log(2.0))
    code = jnp.minimum(jnp.sqrt(size * scale) * FULL + 0.5, FULL).astype(jnp.int32)
    code = jnp.where(value < 0.0, -code, code).astype(I16)
    tail = jnp.broadcast_to(exponent.astype(jnp.int32), (TAIL, value.shape[1])).astype(I16)
    return code, tail


def decode_scale(tail):
    exponent = tail.astype(jnp.int32).astype(F32)[:1]
    return jnp.exp(exponent * math.log(2.0)) * (1.0 / (FULL * FULL))


def decode(code, scale):
    code = code.astype(jnp.int32).astype(F32)
    return code * jnp.abs(code) * scale


def fold(a_lo, a_hi, b_lo, b_hi, sign, first):
    if first is None:
        return a_lo - sign * b_hi, b_lo + sign * a_hi, a_lo + sign * b_hi, b_lo - sign * a_hi
    a_in = jnp.where(first, 0.0, a_hi)
    b_in = jnp.where(first, 0.0, b_hi)
    return (
        a_lo - sign * b_in,
        b_lo + sign * a_in,
        jnp.where(first, a_hi, a_lo + sign * b_hi),
        jnp.where(first, b_hi, b_lo - sign * a_hi),
    )


def right_stage(re, im, table, half, sign):
    both = dot(jnp.concatenate([re, im], axis=0), table)
    a, b = both[:N], both[N:]
    first = lax.broadcasted_iota(jnp.int32, (N, H), 1) == 0
    re_lo, im_lo, re_hi, im_hi = fold(a[:, :H], a[:, H:], b[:, :H], b[:, H:], sign, first)
    half[:, :H] = re_lo.astype(BF16)
    half[:, H:N] = re_hi.astype(BF16)
    half[:, N : N + H] = im_lo.astype(BF16)
    half[:, N + H :] = im_hi.astype(BF16)


def left_strip(flat, at, sign):
    first = lax.broadcasted_iota(jnp.int32, (STRIP, N), 0) == 0 if at == 0 else None
    low, high = slice(at, at + STRIP), slice(H + at, H + at + STRIP)
    re_lo, im_lo, re_hi, im_hi = fold(flat[low, :N], flat[high, :N], flat[low, N:], flat[high, N:], sign, first)
    return (low, re_lo, im_lo), (high, re_hi, im_hi)


def remote(src, dst, send, recv, scan, tile):
    return pltpu.make_async_remote_copy(
        src_ref=src,
        dst_ref=dst,
        send_sem=send,
        recv_sem=recv,
        device_id={"scan": scan, "tile": tile},
        device_id_type=MESH,
    )


def greet():
    scan_count, tile_count = lax.axis_size("scan"), lax.axis_size("tile")
    me, tile = lax.axis_index("scan"), lax.axis_index("tile")
    barrier = pltpu.get_barrier_semaphore()

    @pl.loop(1, scan_count)
    def _(d):
        pl.semaphore_signal(barrier, 1, device_id={"scan": (me + d) % scan_count, "tile": tile}, device_id_type=MESH)

    @pl.loop(1, tile_count)
    def _(d):
        pl.semaphore_signal(barrier, 1, device_id={"scan": me, "tile": (tile + d) % tile_count}, device_id_type=MESH)

    pl.semaphore_wait(barrier, scan_count + tile_count - 2)


def sweep_kernel(
    field,
    spots,
    table,
    probe,
    patterns,
    coded,
    numer,
    cover,
    block,
    band,
    below,
    cut,
    spots_own,
    spots_above,
    spot_words,
    spot_words_above,
    power_total,
    probe_chunk,
    folded_probe,
    level,
    patch,
    far,
    power,
    halves,
    flats,
    sums,
    update,
    queue,
    slots,
    received,
    core_in,
    x_out,
    x_in,
    y_part,
    y_in,
    z_in,
    den_chunk,
    acc,
    merge_out,
    merge_in,
    send_sem,
    recv_sem,
    spot_send,
    spot_recv,
    cut_send,
    cut_recv,
    move_send,
    move_recv,
    sum_send,
    sum_recv,
    local_sem,
):
    scan_count, tile_count = lax.axis_size("scan"), lax.axis_size("tile")
    me, tile = lax.axis_index("scan"), lax.axis_index("tile")
    x, core = tile // 2, tile % 2
    y, z = me // 4, me % 4
    pair, parity = me // 2, me % 2
    partner = tile + 1 - 2 * core
    next_tile, last_tile = (tile + 1) % tile_count, (tile + tile_count - 1) % tile_count
    per_device = level.shape[0]
    modes = folded_probe.shape[0] // 2
    other_lanes = pl.ds(pl.multiple_of((1 - core) * H, H), H)
    own_lanes = pl.ds(pl.multiple_of(core * H, H), H)

    probe_load = pltpu.make_async_copy(probe, far.at[0], local_sem.at[0])
    probe_load.start()
    pattern_load = pltpu.make_async_copy(patterns, level, local_sem.at[1])
    pattern_load.start()
    block[...] = field[...].astype(BF16)
    greet()

    def spot_copy(d):
        return remote(spots, spots_own.at[me], spot_send.at[d], spot_recv.at[d], (me + d) % scan_count, tile)

    @pl.loop(1, scan_count)
    def _(d):
        spot_copy(d).start()

    def along(plane, stage, d):
        turn_z = (plane == 0) == (stage == 0)
        return 4 * y + (z + d) % 4 if turn_z else 4 * ((y + d) % 4) + z

    sent = []

    def push(src, source, plane, stage, d):
        move = remote(
            src,
            band.at[source, plane],
            send_sem.at[len(sent)],
            recv_sem.at[2 * source + plane],
            along(plane, stage, d),
            tile,
        )
        move.start()
        sent.append(move)

    for stage in range(2):
        for d in (1, 3, 2):
            for plane in range(2):
                push(block.at[plane], me, plane, stage, d)

    def landed(source, plane):
        remote(
            block.at[plane], band.at[source, plane], send_sem.at[0], recv_sem.at[2 * source + plane], along(0, 0, 1), tile
        ).wait_recv()

    spots_own[me] = spots[...]
    band[me] = block[...]
    probe_load.wait()
    total = jnp.zeros((N, N), F32)
    for m in range(modes):
        for plane in range(2):
            value = far[0, m, plane]
            total = total + value * value
    power_total[...] = total

    for d in (3, 1, 2):
        for plane in range(2):
            source = along(plane, 0, d)
            landed(source, plane)
            for turn in (1, 3, 2):
                push(band.at[source, plane], source, plane, 1, turn)

    @pl.loop(1, scan_count)
    def _(d):
        source = (me + scan_count - d) % scan_count
        remote(spots, spots_own.at[source], spot_send.at[d], spot_recv.at[d], source, tile).wait_recv()

    above_copy = remote(spots_own, spots_above, spot_send.at[0], spot_recv.at[0], me, next_tile)
    above_copy.start()
    words_copy = pltpu.make_async_copy(spots_own, spot_words, local_sem.at[2])
    words_copy.start()

    fold_matrix = one_hot(iota(0) == folded(iota(1)))
    chunk_rows = pl.ds(pl.multiple_of(x * 64 + y * 16, 16), 16)

    @pl.loop(0, modes)
    def _(m):
        for plane in range(2):
            folded_probe[2 * m + plane] = permute(far[0, m, plane], fold_matrix, fold_matrix, 3)
            probe_chunk[2 * m + plane] = far[0, m, plane, chunk_rows, own_lanes]

    pattern_load.wait()

    @pl.loop(0, per_device)
    def _(k):
        level[k] = jnp.sqrt(permute(level[k], fold_matrix, fold_matrix, 3))

    cover[...] = jnp.zeros_like(cover)

    def add_cover(words, above):
        @pl.loop(0, scan_count)
        def _(source):
            head, row_shift, col_shift = jnp.int32(-1), jnp.int32(0), jnp.int32(0)
            for k in range(per_device):
                row, col = words[source, 0, 2 * k], words[source, 0, 2 * k + 1]
                owner = col // N
                first = owner == me
                hit = first | ((owner + 1) % scan_count == me)
                head = jnp.where(hit, first.astype(jnp.int32), head)
                row_shift = jnp.where(hit, row % N, row_shift)
                col_shift = jnp.where(hit, col % N, col_shift)
            start = jnp.where(head == 1, col_shift, 0)
            stop = jnp.where(head == 1, N, jnp.where(head == 0, col_shift, 0))
            rows, cols = iota(0), iota(1)
            moved = pltpu.roll(pltpu.roll(power_total[...], row_shift, 0), col_shift, 1)
            keep = (rows < row_shift) if above else (rows >= row_shift)
            cover[...] += jnp.where(keep & (cols >= start) & (cols < stop), moved, 0.0)

    words_copy.wait()
    add_cover(spot_words, False)
    above_copy.wait_recv()
    words_copy = pltpu.make_async_copy(spots_above, spot_words_above, local_sem.at[3])
    words_copy.start()
    words_copy.wait()
    add_cover(spot_words_above, True)

    for d in (3, 1, 2):
        for plane in range(2):
            for turn in (3, 1, 2):
                if plane == 0:
                    source = 4 * ((y + turn) % 4) + (z + d) % 4
                else:
                    source = 4 * ((y + d) % 4) + (z + turn) % 4
                landed(source, plane)
    for turn in (3, 1, 2):
        landed(4 * ((y + turn) % 4) + z, 0)
        landed(4 * y + (z + turn) % 4, 1)

    def composite(col, plane):
        owner, col_shift = col // N, col % N
        after = (owner + 1) % scan_count
        return jnp.where(iota(1) >= col_shift, band[owner, plane].astype(F32), band[after, plane].astype(F32))

    def cut_copy(k):
        return remote(cut.at[k], below.at[k], cut_send.at[k], cut_recv.at[k], me, last_tile)

    @pl.loop(0, per_device)
    def _(k):
        for plane in range(2):
            cut[k, plane] = composite(spot_words_above[me, 0, 2 * k + 1], plane).astype(BF16)
        cut_copy(k).start()

    update[...] = jnp.zeros_like(update)
    sums[...] = jnp.zeros_like(sums)
    acc[...] = jnp.zeros_like(acc)
    queue[per_device] = jnp.zeros(queue.shape[1:], I16)

    @pl.loop(0, per_device)
    def _(k):
        row, col = spot_words[me, 0, 2 * k], spot_words[me, 0, 2 * k + 1]
        row_shift, col_shift = row % N, col % N
        cut_copy(k).wait_recv()
        row_pick = one_hot(iota(1) == (row_shift + folded(iota(0))) % N)
        col_pick = one_hot(iota(0) == (col_shift + folded(iota(1))) % N)
        for plane in range(2):
            top = composite(col, plane)
            window = jnp.where(iota(0) >= row_shift, top, below[k, plane].astype(F32)).astype(BF16)
            patch[k, plane] = dot(dot(row_pick, window).astype(BF16), col_pick)
        sums[0] += patch[k, 0] * patch[k, 0] + patch[k, 1] * patch[k, 1]
        power[k] = jnp.full((N, N), 0.25, F32)

        @pl.loop(0, modes // UNROLL)
        def _(part):
            for u in range(UNROLL):
                m = part * UNROLL + u
                half, flat = halves.at[u], flats.at[u]
                p_re, p_im = folded_probe[2 * m], folded_probe[2 * m + 1]
                o_re, o_im = patch[k, 0], patch[k, 1]
                wave_re = (p_re * o_re - p_im * o_im).astype(BF16)
                wave_im = (p_re * o_im + p_im * o_re).astype(BF16)
                right_stage(wave_re, wave_im, table[0], half, -1.0)
                flat[...] = dot(table[1], half[...])
                for at in range(0, H, STRIP):
                    for rows, f_re, f_im in left_strip(flat, at, -1.0):
                        far[k, m, 0, rows] = f_re
                        far[k, m, 1, rows] = f_im
                        power[k, rows] += f_re * f_re + f_im * f_im

        power[k] = level[k] / jnp.sqrt(power[k])

    sums[0] = permute(sums[0], fold_matrix, fold_matrix, 2)

    PER_GROUP = 20

    def span(g):
        return (0, 2 * modes // GROUPS + 1) if g == 0 else (1 + g * (2 * modes // GROUPS), 2 * modes // GROUPS)

    def sum_copy(src, dst, g, number, scan=None, tile_to=None):
        return remote(
            src,
            dst,
            sum_send.at[g * PER_GROUP + number],
            sum_recv.at[g * PER_GROUP + number],
            me if scan is None else scan,
            tile if tile_to is None else tile_to,
        )

    def core_copy(g):
        start, count = span(g)
        planes = pl.ds(start, count)
        return sum_copy(sums.at[planes, :, other_lanes], core_in.at[planes], g, 0, tile_to=partner)

    def x_copy(g, d):
        used = pl.ds(0, span(g)[1] * 64 + TAIL)
        return sum_copy(
            x_out.at[g, d - 1, used], x_in.at[g, d - 1, used], g, d, tile_to=2 * ((x + d) % 4) + core
        )

    def y_copy(g, d):
        start, count = span(g)
        planes = pl.ds(start, count)
        rows = pl.ds(pl.multiple_of((y + d) % 4 * 16, 16), 16)
        return sum_copy(
            y_part.at[planes, rows], y_in.at[d - 1, planes], g, 3 + d, scan=4 * ((y + d) % 4) + z
        )

    def z_copy(g, d, source):
        planes = pl.ds(*span(g))
        return sum_copy(z_in.at[source, planes], z_in.at[source, planes], g, 6 + d, scan=4 * y + (z + d) % 4)

    def yg_copy(g, d, source):
        at = core * 16 + x * 4 + source
        return sum_copy(coded.at[at, g], coded.at[at, g], g, 9 + d, scan=4 * ((y + d) % 4) + z)

    def xg_copy(g, d, source):
        at = pl.ds(core * 16 + source * 4, 4)
        return sum_copy(coded.at[at, g], coded.at[at, g], g, 12 + d, tile_to=2 * ((x + d) % 4) + core)

    def cg_copy(g, d, side):
        at = pl.ds(side * 16 + (x + 4 - d) % 4 * 4, 4)
        return sum_copy(coded.at[at, g], coded.at[at, g], g, 16 + d, tile_to=partner)

    def stage_core(g):
        core_copy(g).start()

    def stage_x(g):
        start, count = span(g)
        planes = pl.ds(start, count)
        core_copy(g).wait_recv()
        for d in range(1, 4):
            rows = pl.ds(pl.multiple_of((x + d) % 4 * 64, 64), 64)
            chunk = sums[planes, rows, own_lanes] + core_in[planes, rows]
            code, tail = encode(chunk.reshape(count * 64, H))
            x_out[g, d - 1, : count * 64] = code
            x_out[g, d - 1, count * 64 : count * 64 + TAIL] = tail
            x_copy(g, d).start()
        rows = pl.ds(pl.multiple_of(x * 64, 64), 64)
        y_part[planes] = sums[planes, rows, own_lanes] + core_in[planes, rows]

    def stage_y(g):
        start, count = span(g)
        planes = pl.ds(start, count)
        for d in range(1, 4):
            x_copy(g, d).wait_recv()
            scale = decode_scale(x_in[g, d - 1, count * 64 : count * 64 + TAIL])
            y_part[planes] += decode(x_in[g, d - 1, : count * 64], scale).reshape(count, 64, H)
        for d in range(1, 4):
            y_copy(g, d).start()

    def stage_z(g):
        start, count = span(g)
        planes = pl.ds(start, count)
        chunk = y_part[planes, pl.ds(pl.multiple_of(y * 16, 16), 16)]
        for d in range(1, 4):
            y_copy(g, d).wait_recv()
            chunk = chunk + y_in[d - 1, planes]
        z_in[z, planes] = chunk
        for d in range(1, 4):
            z_copy(g, d, z).start()

    def stage_back(g):
        start, count = span(g)
        planes = pl.ds(start, count)
        for d in range(1, 4):
            z_copy(g, d, (z + 4 - d) % 4).wait_recv()
        whole = z_in[0, planes] + z_in[1, planes] + z_in[2, planes] + z_in[3, planes]
        if g == 0:
            den_chunk[...] = 1.0 / (1.0 + whole[0])
            whole = whole[1:]
        width = 2 * modes // GROUPS
        fresh = (probe_chunk[pl.ds(g * width, width)] + whole) * den_chunk[...][None]
        code, tail = encode(fresh.reshape(width * 16, H))
        at = core * 16 + x * 4 + y
        coded[at, g, : width * 16] = code
        coded[at, g, width * 16 :] = tail
        for d in range(1, 4):
            yg_copy(g, d, y).start()

    def stage_x_back(g):
        for d in range(1, 4):
            yg_copy(g, d, (y + 4 - d) % 4).wait_recv()
        for d in range(1, 4):
            xg_copy(g, d, x).start()
        cg_copy(g, 0, core).start()

    def stage_core_back(g):
        for d in range(1, 4):
            xg_copy(g, d, (x + 4 - d) % 4).wait_recv()
            cg_copy(g, d, core).start()

    def stage_end(g):
        for d in range(4):
            cg_copy(g, d, 1 - core).wait_recv()

    stages = (stage_core, stage_x, stage_y, stage_z, stage_back, stage_x_back, stage_core_back, stage_end)

    def tick(n):
        for number in range(len(stages) - 1, -1, -1):
            if 0 <= n - number < GROUPS:
                stages[number](n - number)

    width = modes // GROUPS

    @pl.loop(0, GROUPS)
    def _(n):
        @pl.loop(0, width)
        def _(part):
            m = n * width + part
            for k in range(per_device):
                half, flat = halves.at[k % UNROLL], flats.at[k % UNROLL]
                scaling = power[k]
                fixed_re = (far[k, m, 0] * scaling).astype(BF16)
                fixed_im = (far[k, m, 1] * scaling).astype(BF16)
                right_stage(fixed_re, fixed_im, table[0], half, 1.0)
                flat[...] = dot(table[1], half[...])
                for at in range(0, H, STRIP):
                    for rows, e_re, e_im in left_strip(flat, at, 1.0):
                        p_re, p_im = folded_probe[2 * m, rows], folded_probe[2 * m + 1, rows]
                        o_re, o_im = patch[k, 0, rows], patch[k, 1, rows]
                        update[k, 0, rows] += p_re * e_re + p_im * e_im
                        update[k, 1, rows] += p_re * e_im - p_im * e_re
                        sums[1 + 2 * m, rows] += o_re * e_re + o_im * e_im
                        sums[2 + 2 * m, rows] += o_re * e_im - o_im * e_re
            for plane in range(2):
                at = 1 + 2 * m + plane
                sums[at] = permute(sums[at], fold_matrix, fold_matrix, 2)

        for step in range(GROUPS):
            @pl.when(n == step)
            def _():
                tick(step)

    @pl.loop(0, per_device)
    def _(k):
        row_shift, col_shift = spot_words[me, 0, 2 * k] % N, spot_words[me, 0, 2 * k + 1] % N
        row_back = one_hot(iota(0) == (row_shift + folded(iota(1))) % N)
        col_back = one_hot(iota(1) == (col_shift + folded(iota(0))) % N)
        for plane in range(2):
            code, tail = encode(permute(update[k, plane], row_back, col_back, 2))
            queue[k, plane, :N] = code
            queue[k, plane, N:] = tail

    @pl.loop(0, scan_count // 2)
    def _(q):
        pick = jnp.int32(per_device)
        for k in range(per_device):
            pick = jnp.where(spot_words[me, 0, 2 * k + 1] // (2 * N) == q, k, pick)
        for plane in range(2):
            slots[2 * q + plane] = queue[pick, plane]

    def update_copy(dy, dz):
        to = 4 * ((y + dy) % 4) + (z + dz) % 4
        j = 4 * dy + dz
        return remote(slots.at[to], received.at[j], move_send.at[j], move_recv.at[j], to, tile)

    hops = (0, 1, 2, 1)
    order = sorted(((dy, dz) for dy in range(4) for dz in range(4) if dy or dz), key=lambda d: -hops[d[0]] - hops[d[1]])
    def launch(picked):
        for dy, dz in picked:
            update_copy(dy, dz).start()

    launch(order[:6])

    def collect(source, ref):
        owner, row_shift, col_shift = jnp.int32(-4), jnp.int32(0), jnp.int32(0)
        for k in range(per_device):
            spot_row, spot_col = spot_words[source, 0, 2 * k], spot_words[source, 0, 2 * k + 1]
            hit = spot_col // (2 * N) == pair
            owner = jnp.where(hit, spot_col // N, owner)
            row_shift = jnp.where(hit, spot_row % N, row_shift)
            col_shift = jnp.where(hit, spot_col % N, col_shift)
        side = owner - 2 * pair
        cols = lax.broadcasted_iota(jnp.int32, (STRIP, N), 1)
        right = cols >= col_shift
        head = jnp.broadcast_to(side, (STRIP, N)) == 0
        tail = jnp.broadcast_to(side, (STRIP, N)) == 1
        picks = (head & right, (head & ~right) | (tail & right), tail & ~right)
        scale = decode_scale(ref[N:])

        for part in range(0, N, STRIP):
            rows = lax.broadcasted_iota(jnp.int32, (STRIP, N), 0) + part
            value = decode(ref[part : part + STRIP], scale)
            low = rows < row_shift
            for at in range(3):
                taken = jnp.where(picks[at], value, 0.0)
                acc[0, at, part : part + STRIP] += jnp.where(low, 0.0, taken)
                acc[1, at, part : part + STRIP] += jnp.where(low, taken, 0.0)

    def collect_some(picked):
        for dy, dz in picked:
            update_copy(dy, dz).wait_recv()
            collect(4 * ((y + 4 - dy) % 4) + (z + 4 - dz) % 4, received.at[4 * dy + dz])

    collect(me, slots.at[me])
    tick(GROUPS)
    launch(order[6:9])
    collect_some(order[:3])
    tick(GROUPS + 1)
    launch(order[9:12])
    collect_some(order[3:6])
    tick(GROUPS + 2)
    launch(order[12:])
    collect_some(order[6:9])
    tick(GROUPS + 3)
    collect_some(order[9:12])
    tick(GROUPS + 4)
    collect_some(order[12:])
    tick(GROUPS + 5)

    def merge_copy(number, band_at, kind, plane, to):
        return remote(
            merge_out.at[number],
            merge_in.at[band_at, kind, plane],
            move_send.at[16 + number],
            move_recv.at[16 + 4 * band_at + 2 * kind + plane],
            to,
            (tile + band_at) % tile_count,
        )

    beside = me + 1 - 2 * parity
    after_pair = (2 * pair + 2) % scan_count
    merges = []
    for number, (band_at, at, kind, to) in enumerate(
        (
            (1, 2, 1, after_pair),
            (1, 1 - parity, 0, beside),
            (1, parity, 0, me),
            (0, 2, 1, after_pair),
            (0, 1 - parity, 0, beside),
        )
    ):
        code, tail = encode(acc[band_at, at])
        merge_out[number, :N] = code
        merge_out[number, N:] = tail
        merges.append(merge_copy(number, band_at, kind, parity, to))
        merges[-1].start()

    def merged(band_at, kind, plane):
        merge_copy(0, band_at, kind, plane, beside).wait_recv()
        ref = merge_in.at[band_at, kind, plane]
        return decode(ref[:N], decode_scale(ref[N:]))

    numer[1 - parity] = merged(0, 0, 1 - parity)
    numer[1 - parity] += merged(1, 0, 1 - parity)
    numer[parity] = acc[0, parity] + merged(1, 0, parity)

    @pl.when(parity == 0)
    def _():
        for band_at in range(2):
            for plane in range(2):
                numer[plane] += merged(band_at, 1, plane)

    for n in range(GROUPS + 6, GROUPS + len(stages)):
        tick(n)

    for move in sent:
        move.wait_send()
    above_copy.wait_send()

    @pl.loop(1, scan_count)
    def _(d):
        spot_copy(d).wait_send()

    @pl.loop(0, per_device)
    def _(k):
        cut_copy(k).wait_send()

    for dy, dz in order:
        update_copy(dy, dz).wait_send()
    for move in merges:
        move.wait_send()
    for g in range(GROUPS):
        core_copy(g).wait_send()
        cg_copy(g, 0, core).wait_send()
        for d in range(1, 4):
            x_copy(g, d).wait_send()
            y_copy(g, d).wait_send()
            z_copy(g, d, z).wait_send()
            yg_copy(g, d, y).wait_send()
            xg_copy(g, d, x).wait_send()
            cg_copy(g, d, core).wait_send()


def sweep(field, spots, table, probe, patterns, scan_count):
    per_device, modes = patterns.shape[0], probe.shape[0]
    planes = 2 * modes + 1
    width = 2 * modes // GROUPS
    vmem, anywhere = pl.BlockSpec(memory_space=pltpu.VMEM), pl.BlockSpec(memory_space=pl.ANY)
    words = (scan_count,) + spots.shape
    dma, mem = pltpu.SemaphoreType.DMA, pltpu.VMEM
    slot = (N + TAIL, N)
    return pl.pallas_call(
        sweep_kernel,
        in_specs=[vmem, vmem, vmem, anywhere, anywhere],
        out_specs=[vmem, vmem, vmem],
        out_shape=[
            jax.ShapeDtypeStruct((2 * scan_count, GROUPS, width * 16 + TAIL, H), I16),
            jax.ShapeDtypeStruct((2, N, N), F32),
            jax.ShapeDtypeStruct((N, N), F32),
        ],
        scratch_shapes=[
            mem((2, N, N), BF16),
            mem((scan_count, 2, N, N), BF16),
            mem((per_device, 2, N, N), BF16),
            mem((per_device, 2, N, N), BF16),
            mem(words, jnp.int32),
            mem(words, jnp.int32),
            pltpu.SMEM(words, jnp.int32),
            pltpu.SMEM(words, jnp.int32),
            mem((N, N), F32),
            mem((2 * modes, 16, H), F32),
            mem((2 * modes, N, N), F32),
            mem((per_device, N, N), F32),
            mem((per_device, 2, N, N), F32),
            mem((per_device, modes, 2, N, N), F32),
            mem((per_device, N, N), F32),
            mem((UNROLL, N, 2 * N), BF16),
            mem((UNROLL, N, 2 * N), F32),
            mem((planes, N, N), F32),
            mem((per_device, 2, N, N), F32),
            mem((per_device + 1, 2) + slot, I16),
            mem((scan_count,) + slot, I16),
            mem((scan_count,) + slot, I16),
            mem((planes, N, H), F32),
            mem((GROUPS, 3, (width + 1) * 64 + TAIL, H), I16),
            mem((GROUPS, 3, (width + 1) * 64 + TAIL, H), I16),
            mem((planes, 64, H), F32),
            mem((3, planes, 16, H), F32),
            mem((4, planes, 16, H), F32),
            mem((16, H), F32),
            mem((2, 3, N, N), F32),
            mem((5,) + slot, I16),
            mem((2, 2, 2) + slot, I16),
            dma((30,)),
            dma((2 * scan_count,)),
            dma((scan_count,)),
            dma((scan_count,)),
            dma((per_device,)),
            dma((per_device,)),
            dma((24,)),
            dma((24,)),
            dma((20 * GROUPS,)),
            dma((20 * GROUPS,)),
            dma((4,)),
        ],
        compiler_params=pltpu.CompilerParams(
            collective_id=0, has_side_effects=True, vmem_limit_bytes=62 * 2**20
        ),
        name="sweep",
    )(field, spots, table, probe, patterns)


def final_kernel(coded, numer, cover, field, object_out, probe_out):
    share = 1.0 / (1.0 + cover[...])
    for plane in range(2):
        object_out[plane] = (field[plane] + numer[plane]) * share
    width = (coded.shape[4] - TAIL) // 16
    for core in range(2):
        for at in range(4):
            for g in range(GROUPS):
                scale = decode_scale(coded[core, 0, at, g, width * 16 :])
                value = decode(coded[core, 0, at, g, : width * 16], scale).reshape(width, 16, H)
                probe_out[width * g : width * (g + 1), 16 * at : 16 * (at + 1), core * H : (core + 1) * H] = value


def final(coded, numer, cover, field, planes):
    coded = coded.reshape((2, 4, 4) + coded.shape[1:])
    rows = N // 4
    return pl.pallas_call(
        final_kernel,
        grid=(4,),
        in_specs=[
            pl.BlockSpec((2, 1) + coded.shape[2:], lambda i: (0, i, 0, 0, 0, 0)),
            pl.BlockSpec((2, rows, N), lambda i: (0, i, 0)),
            pl.BlockSpec((rows, N), lambda i: (i, 0)),
            pl.BlockSpec((2, rows, N), lambda i: (0, i, 0)),
        ],
        out_specs=[
            pl.BlockSpec((2, rows, N), lambda i: (0, i, 0)),
            pl.BlockSpec((planes, rows, N), lambda i: (0, i, 0)),
        ],
        out_shape=[jax.ShapeDtypeStruct((2, N, N), F32), jax.ShapeDtypeStruct((planes, N, N), F32)],
        compiler_params=pltpu.CompilerParams(vmem_limit_bytes=62 * 2**20),
        name="final",
    )(coded, numer, cover, field)


def body(object_field, probe_modes, patterns, positions):
    scan_count = lax.axis_size("scan")
    table = jnp.asarray(folded_tables())
    spots = jnp.zeros((8, 128), jnp.int32).at[0, : positions.size].set(positions.reshape(-1))
    coded, numer, cover = sweep(object_field, spots, table, probe_modes, patterns, scan_count)
    planes = 2 * probe_modes.shape[0]
    object_now, probe_now = final(coded, numer, cover, object_field, planes)
    return (object_now, probe_now.reshape(probe_modes.shape))


def solution(mesh):
    return jax.shard_map(
        body,
        mesh=mesh,
        in_specs=(
            P(None, "tile", "scan"),
            P(),
            P(("scan", "tile"), None, None),
            P(("scan", "tile"), None),
        ),
        out_specs=(P(None, "tile", "scan"), P()),
        check_vma=False,
    )
```

```python
import functools
import math

import jax
import jax.numpy as jnp
import ml_dtypes
import numpy as np
from jax import lax
from jax.experimental import pallas as pl
from jax.experimental.pallas import tpu as pltpu
from jax.sharding import PartitionSpec as P

F32 = jnp.float32
BF16 = jnp.bfloat16
N = 256
H = N // 2
I16 = jnp.int16
TAIL = 16
GROUPS = 4
UNROLL = 4
STRIP = 32
FULL = 32767.0
MESH = pl.DeviceIdType.MESH


def folded_tables():
    counter = np.arange(N, dtype=np.int32)
    phase = counter[:, None] * counter[None, :] % N
    angle = phase.astype(np.float32) * np.float32(2.0 * math.pi / N)
    factor = np.float32(1.0 / math.sqrt(N))
    cosine = (np.cos(angle) * factor).astype(ml_dtypes.bfloat16)
    sine = (np.sin(angle) * factor).astype(ml_dtypes.bfloat16)
    order = np.where(counter <= H, counter, 3 * H - counter)
    right = np.concatenate([cosine[:, : H + 1], sine[:, 1:H]], axis=1)[order]
    return np.stack([right, np.ascontiguousarray(right.T)])


def dot(left, right):
    return jnp.dot(left, right, preferred_element_type=F32)


def iota(axis):
    return lax.broadcasted_iota(jnp.int32, (N, N), axis)


def folded(index):
    return jnp.where(index <= H, index, 3 * H - index)


def one_hot(condition):
    return jnp.where(condition, 1.0, 0.0).astype(BF16)


def pieces(value, count):
    parts = []
    for _ in range(count):
        part = value.astype(BF16)
        parts.append(part)
        value = value - part.astype(F32)
    return parts


def permute(value, left, right, count):
    rows = sum(dot(left, part) for part in pieces(value, count))
    return sum(dot(part, right) for part in pieces(rows, count))


def encode(value):
    size = jnp.abs(value)
    peak = jnp.maximum(jnp.max(size, axis=0, keepdims=True), 1e-30)
    exponent = jnp.ceil(jnp.log(peak) * (1.0 / math.log(2.0)) + 1e-5)
    scale = jnp.exp(exponent * -math.log(2.0))
    code = jnp.minimum(jnp.sqrt(size * scale) * FULL + 0.5, FULL).astype(jnp.int32)
    code = jnp.where(value < 0.0, -code, code).astype(I16)
    tail = jnp.broadcast_to(exponent.astype(jnp.int32), (TAIL, value.shape[1])).astype(I16)
    return code, tail


def decode_scale(tail):
    exponent = tail.astype(jnp.int32).astype(F32)[:1]
    return jnp.exp(exponent * math.log(2.0)) * (1.0 / (FULL * FULL))


def decode(code, scale):
    code = code.astype(jnp.int32).astype(F32)
    return code * jnp.abs(code) * scale


def unfold(value, flip):
    high = sum(dot(flip, part) for part in pieces(value[H:], 2))
    rows = jnp.concatenate([value[:H], high], axis=0)
    right = sum(dot(part, flip) for part in pieces(rows[:, H:], 2))
    return jnp.concatenate([rows[:, :H], right], axis=1)


def fold(a_lo, a_hi, b_lo, b_hi, sign, first):
    if first is None:
        return a_lo - sign * b_hi, b_lo + sign * a_hi, a_lo + sign * b_hi, b_lo - sign * a_hi
    a_in = jnp.where(first, 0.0, a_hi)
    b_in = jnp.where(first, 0.0, b_hi)
    return (
        a_lo - sign * b_in,
        b_lo + sign * a_in,
        jnp.where(first, a_hi, a_lo + sign * b_hi),
        jnp.where(first, b_hi, b_lo - sign * a_hi),
    )


def right_stage(re, im, table, half, sign):
    both = dot(jnp.concatenate([re, im], axis=0), table)
    a, b = both[:N], both[N:]
    first = lax.broadcasted_iota(jnp.int32, (N, H), 1) == 0
    re_lo, im_lo, re_hi, im_hi = fold(a[:, :H], a[:, H:], b[:, :H], b[:, H:], sign, first)
    half[:, :H] = re_lo.astype(BF16)
    half[:, H:N] = re_hi.astype(BF16)
    half[:, N : N + H] = im_lo.astype(BF16)
    half[:, N + H :] = im_hi.astype(BF16)


def left_strip(flat, at, sign):
    first = lax.broadcasted_iota(jnp.int32, (STRIP, N), 0) == 0 if at == 0 else None
    low, high = slice(at, at + STRIP), slice(H + at, H + at + STRIP)
    re_lo, im_lo, re_hi, im_hi = fold(flat[low, :N], flat[high, :N], flat[low, N:], flat[high, N:], sign, first)
    return (low, re_lo, im_lo), (high, re_hi, im_hi)


def remote(src, dst, send, recv, scan, tile):
    return pltpu.make_async_remote_copy(
        src_ref=src,
        dst_ref=dst,
        send_sem=send,
        recv_sem=recv,
        device_id={"scan": scan, "tile": tile},
        device_id_type=MESH,
    )


def greet():
    scan_count, tile_count = lax.axis_size("scan"), lax.axis_size("tile")
    me, tile = lax.axis_index("scan"), lax.axis_index("tile")
    barrier = pltpu.get_barrier_semaphore()

    @pl.loop(1, scan_count)
    def _(d):
        pl.semaphore_signal(barrier, 1, device_id={"scan": (me + d) % scan_count, "tile": tile}, device_id_type=MESH)

    @pl.loop(1, tile_count)
    def _(d):
        pl.semaphore_signal(barrier, 1, device_id={"scan": me, "tile": (tile + d) % tile_count}, device_id_type=MESH)

    pl.semaphore_wait(barrier, scan_count + tile_count - 2)


def sweep_kernel(
    field,
    spots,
    table,
    probe,
    patterns,
    coded,
    numer,
    cover,
    block,
    band,
    below,
    cut,
    spots_own,
    spots_above,
    spot_words,
    spot_words_above,
    power_total,
    probe_chunk,
    folded_probe,
    level,
    patch,
    far,
    power,
    halves,
    flats,
    sums,
    update,
    queue,
    slots,
    received,
    core_in,
    x_out,
    x_in,
    y_part,
    y_in,
    z_in,
    den_chunk,
    acc,
    merge_out,
    merge_in,
    send_sem,
    recv_sem,
    spot_send,
    spot_recv,
    cut_send,
    cut_recv,
    move_send,
    move_recv,
    sum_send,
    sum_recv,
    local_sem,
):
    scan_count, tile_count = lax.axis_size("scan"), lax.axis_size("tile")
    me, tile = lax.axis_index("scan"), lax.axis_index("tile")
    x, core = tile // 2, tile % 2
    y, z = me // 4, me % 4
    pair, parity = me // 2, me % 2
    partner = tile + 1 - 2 * core
    next_tile, last_tile = (tile + 1) % tile_count, (tile + tile_count - 1) % tile_count
    per_device = level.shape[0]
    modes = folded_probe.shape[0] // 2
    other_lanes = pl.ds(pl.multiple_of((1 - core) * H, H), H)
    own_lanes = pl.ds(pl.multiple_of(core * H, H), H)

    probe_load = pltpu.make_async_copy(probe, far.at[0], local_sem.at[0])
    probe_load.start()
    pattern_load = pltpu.make_async_copy(patterns, level, local_sem.at[1])
    pattern_load.start()
    block[...] = field[...].astype(BF16)
    greet()

    def spot_copy(d):
        return remote(spots, spots_own.at[me], spot_send.at[d], spot_recv.at[d], (me + d) % scan_count, tile)

    @pl.loop(1, scan_count)
    def _(d):
        spot_copy(d).start()

    def along(plane, stage, d):
        turn_z = (plane == 0) == (stage == 0)
        return 4 * y + (z + d) % 4 if turn_z else 4 * ((y + d) % 4) + z

    sent = []

    def push(src, source, plane, stage, d):
        move = remote(
            src,
            band.at[source, plane],
            send_sem.at[len(sent)],
            recv_sem.at[2 * source + plane],
            along(plane, stage, d),
            tile,
        )
        move.start()
        sent.append(move)

    for stage in range(2):
        for d in (1, 3, 2):
            for plane in range(2):
                push(block.at[plane], me, plane, stage, d)

    def landed(source, plane):
        remote(
            block.at[plane], band.at[source, plane], send_sem.at[0], recv_sem.at[2 * source + plane], along(0, 0, 1), tile
        ).wait_recv()

    spots_own[me] = spots[...]
    band[me] = block[...]
    probe_load.wait()
    total = jnp.zeros((N, N), F32)
    for m in range(modes):
        for plane in range(2):
            value = far[0, m, plane]
            total = total + value * value
    power_total[...] = total

    for d in (3, 1, 2):
        for plane in range(2):
            source = along(plane, 0, d)
            landed(source, plane)
            for turn in (1, 3, 2):
                push(band.at[source, plane], source, plane, 1, turn)

    @pl.loop(1, scan_count)
    def _(d):
        source = (me + scan_count - d) % scan_count
        remote(spots, spots_own.at[source], spot_send.at[d], spot_recv.at[d], source, tile).wait_recv()

    above_copy = remote(spots_own, spots_above, spot_send.at[0], spot_recv.at[0], me, next_tile)
    above_copy.start()
    words_copy = pltpu.make_async_copy(spots_own, spot_words, local_sem.at[2])
    words_copy.start()

    fold_matrix = one_hot(iota(0) == folded(iota(1)))
    chunk_rows = pl.ds(pl.multiple_of(x * 64 + y * 16, 16), 16)

    @pl.loop(0, modes)
    def _(m):
        for plane in range(2):
            folded_probe[2 * m + plane] = permute(far[0, m, plane], fold_matrix, fold_matrix, 3)
            probe_chunk[2 * m + plane] = far[0, m, plane, chunk_rows, own_lanes]

    pattern_load.wait()

    @pl.loop(0, per_device)
    def _(k):
        level[k] = jnp.sqrt(permute(level[k], fold_matrix, fold_matrix, 3))

    cover[...] = jnp.zeros_like(cover)

    def add_cover(words, above):
        @pl.loop(0, scan_count)
        def _(source):
            head, row_shift, col_shift = jnp.int32(-1), jnp.int32(0), jnp.int32(0)
            for k in range(per_device):
                row, col = words[source, 0, 2 * k], words[source, 0, 2 * k + 1]
                owner = col // N
                first = owner == me
                hit = first | ((owner + 1) % scan_count == me)
                head = jnp.where(hit, first.astype(jnp.int32), head)
                row_shift = jnp.where(hit, row % N, row_shift)
                col_shift = jnp.where(hit, col % N, col_shift)
            start = jnp.where(head == 1, col_shift, 0)
            stop = jnp.where(head == 1, N, jnp.where(head == 0, col_shift, 0))
            rows, cols = iota(0), iota(1)
            moved = pltpu.roll(pltpu.roll(power_total[...], row_shift, 0), col_shift, 1)
            keep = (rows < row_shift) if above else (rows >= row_shift)
            cover[...] += jnp.where(keep & (cols >= start) & (cols < stop), moved, 0.0)

    words_copy.wait()
    add_cover(spot_words, False)
    above_copy.wait_recv()
    words_copy = pltpu.make_async_copy(spots_above, spot_words_above, local_sem.at[3])
    words_copy.start()
    words_copy.wait()
    add_cover(spot_words_above, True)

    for d in (3, 1, 2):
        for plane in range(2):
            for turn in (3, 1, 2):
                if plane == 0:
                    source = 4 * ((y + turn) % 4) + (z + d) % 4
                else:
                    source = 4 * ((y + d) % 4) + (z + turn) % 4
                landed(source, plane)
    for turn in (3, 1, 2):
        landed(4 * ((y + turn) % 4) + z, 0)
        landed(4 * y + (z + turn) % 4, 1)

    def composite(col, plane):
        owner, col_shift = col // N, col % N
        after = (owner + 1) % scan_count
        return jnp.where(iota(1) >= col_shift, band[owner, plane].astype(F32), band[after, plane].astype(F32))

    def cut_copy(k):
        return remote(cut.at[k], below.at[k], cut_send.at[k], cut_recv.at[k], me, last_tile)

    @pl.loop(0, per_device)
    def _(k):
        for plane in range(2):
            cut[k, plane] = composite(spot_words_above[me, 0, 2 * k + 1], plane).astype(BF16)
        cut_copy(k).start()

    update[...] = jnp.zeros_like(update)
    sums[...] = jnp.zeros_like(sums)
    acc[...] = jnp.zeros_like(acc)
    queue[per_device] = jnp.zeros(queue.shape[1:], I16)

    @pl.loop(0, per_device)
    def _(k):
        row, col = spot_words[me, 0, 2 * k], spot_words[me, 0, 2 * k + 1]
        row_shift, col_shift = row % N, col % N
        cut_copy(k).wait_recv()
        row_pick = one_hot(iota(1) == (row_shift + folded(iota(0))) % N)
        col_pick = one_hot(iota(0) == (col_shift + folded(iota(1))) % N)
        for plane in range(2):
            top = composite(col, plane)
            window = jnp.where(iota(0) >= row_shift, top, below[k, plane].astype(F32)).astype(BF16)
            patch[k, plane] = dot(dot(row_pick, window).astype(BF16), col_pick)
        sums[0] += patch[k, 0] * patch[k, 0] + patch[k, 1] * patch[k, 1]
        power[k] = jnp.full((N, N), 0.25, F32)

        @pl.loop(0, modes // UNROLL)
        def _(part):
            for u in range(UNROLL):
                m = part * UNROLL + u
                half, flat = halves.at[u], flats.at[u]
                p_re, p_im = folded_probe[2 * m], folded_probe[2 * m + 1]
                o_re, o_im = patch[k, 0], patch[k, 1]
                wave_re = (p_re * o_re - p_im * o_im).astype(BF16)
                wave_im = (p_re * o_im + p_im * o_re).astype(BF16)
                right_stage(wave_re, wave_im, table[0], half, -1.0)
                flat[...] = dot(table[1], half[...])
                for at in range(0, H, STRIP):
                    for rows, f_re, f_im in left_strip(flat, at, -1.0):
                        far[k, m, 0, rows] = f_re
                        far[k, m, 1, rows] = f_im
                        power[k, rows] += f_re * f_re + f_im * f_im

        power[k] = level[k] / jnp.sqrt(power[k])

    half_rows = lax.broadcasted_iota(jnp.int32, (H, H), 0)
    half_cols = lax.broadcasted_iota(jnp.int32, (H, H), 1)
    flip = one_hot(half_rows == (H - half_cols) % H)
    sums[0] = unfold(sums[0], flip)

    PER_GROUP = 20

    def span(g):
        return (0, 2 * modes // GROUPS + 1) if g == 0 else (1 + g * (2 * modes // GROUPS), 2 * modes // GROUPS)

    def sum_copy(src, dst, g, number, scan=None, tile_to=None):
        return remote(
            src,
            dst,
            sum_send.at[g * PER_GROUP + number],
            sum_recv.at[g * PER_GROUP + number],
            me if scan is None else scan,
            tile if tile_to is None else tile_to,
        )

    def core_copy(g):
        start, count = span(g)
        planes = pl.ds(start, count)
        return sum_copy(sums.at[planes, :, other_lanes], core_in.at[planes], g, 0, tile_to=partner)

    def x_copy(g, d):
        used = pl.ds(0, span(g)[1] * 64 + TAIL)
        return sum_copy(
            x_out.at[g, d - 1, used], x_in.at[g, d - 1, used], g, d, tile_to=2 * ((x + d) % 4) + core
        )

    def y_copy(g, d):
        start, count = span(g)
        planes = pl.ds(start, count)
        rows = pl.ds(pl.multiple_of((y + d) % 4 * 16, 16), 16)
        return sum_copy(
            y_part.at[planes, rows], y_in.at[d - 1, planes], g, 3 + d, scan=4 * ((y + d) % 4) + z
        )

    def z_copy(g, d, source):
        planes = pl.ds(*span(g))
        return sum_copy(z_in.at[source, planes], z_in.at[source, planes], g, 6 + d, scan=4 * y + (z + d) % 4)

    def yg_copy(g, d, source):
        at = core * 16 + x * 4 + source
        return sum_copy(coded.at[at, g], coded.at[at, g], g, 9 + d, scan=4 * ((y + d) % 4) + z)

    def xg_copy(g, d, source):
        at = pl.ds(core * 16 + source * 4, 4)
        return sum_copy(coded.at[at, g], coded.at[at, g], g, 12 + d, tile_to=2 * ((x + d) % 4) + core)

    def cg_copy(g, d, side):
        at = pl.ds(side * 16 + (x + 4 - d) % 4 * 4, 4)
        return sum_copy(coded.at[at, g], coded.at[at, g], g, 16 + d, tile_to=partner)

    def stage_core(g):
        core_copy(g).start()

    def stage_x(g):
        start, count = span(g)
        planes = pl.ds(start, count)
        core_copy(g).wait_recv()
        for d in range(1, 4):
            rows = pl.ds(pl.multiple_of((x + d) % 4 * 64, 64), 64)
            chunk = sums[planes, rows, own_lanes] + core_in[planes, rows]
            code, tail = encode(chunk.reshape(count * 64, H))
            x_out[g, d - 1, : count * 64] = code
            x_out[g, d - 1, count * 64 : count * 64 + TAIL] = tail
            x_copy(g, d).start()
        rows = pl.ds(pl.multiple_of(x * 64, 64), 64)
        y_part[planes] = sums[planes, rows, own_lanes] + core_in[planes, rows]

    def stage_y(g):
        start, count = span(g)
        planes = pl.ds(start, count)
        for d in range(1, 4):
            x_copy(g, d).wait_recv()
            scale = decode_scale(x_in[g, d - 1, count * 64 : count * 64 + TAIL])
            y_part[planes] += decode(x_in[g, d - 1, : count * 64], scale).reshape(count, 64, H)
        for d in range(1, 4):
            y_copy(g, d).start()

    def stage_z(g):
        start, count = span(g)
        planes = pl.ds(start, count)
        chunk = y_part[planes, pl.ds(pl.multiple_of(y * 16, 16), 16)]
        for d in range(1, 4):
            y_copy(g, d).wait_recv()
            chunk = chunk + y_in[d - 1, planes]
        z_in[z, planes] = chunk
        for d in range(1, 4):
            z_copy(g, d, z).start()

    def stage_back(g):
        start, count = span(g)
        planes = pl.ds(start, count)
        for d in range(1, 4):
            z_copy(g, d, (z + 4 - d) % 4).wait_recv()
        whole = z_in[0, planes] + z_in[1, planes] + z_in[2, planes] + z_in[3, planes]
        if g == 0:
            den_chunk[...] = 1.0 / (1.0 + whole[0])
            whole = whole[1:]
        width = 2 * modes // GROUPS
        fresh = (probe_chunk[pl.ds(g * width, width)] + whole) * den_chunk[...][None]
        code, tail = encode(fresh.reshape(width * 16, H))
        at = core * 16 + x * 4 + y
        coded[at, g, : width * 16] = code
        coded[at, g, width * 16 :] = tail
        for d in range(1, 4):
            yg_copy(g, d, y).start()

    def stage_x_back(g):
        for d in range(1, 4):
            yg_copy(g, d, (y + 4 - d) % 4).wait_recv()
        for d in range(1, 4):
            xg_copy(g, d, x).start()
        cg_copy(g, 0, core).start()

    def stage_core_back(g):
        for d in range(1, 4):
            xg_copy(g, d, (x + 4 - d) % 4).wait_recv()
            cg_copy(g, d, core).start()

    def stage_end(g):
        for d in range(4):
            cg_copy(g, d, 1 - core).wait_recv()

    stages = (stage_core, stage_x, stage_y, stage_z, stage_back, stage_x_back, stage_core_back, stage_end)

    def tick(n):
        for number in range(len(stages) - 1, -1, -1):
            if 0 <= n - number < GROUPS:
                stages[number](n - number)

    width = modes // GROUPS

    @pl.loop(0, GROUPS)
    def _(n):
        @pl.loop(0, width)
        def _(part):
            m = n * width + part
            for k in range(per_device):
                half, flat = halves.at[k % UNROLL], flats.at[k % UNROLL]
                scaling = power[k]
                fixed_re = (far[k, m, 0] * scaling).astype(BF16)
                fixed_im = (far[k, m, 1] * scaling).astype(BF16)
                right_stage(fixed_re, fixed_im, table[0], half, 1.0)
                flat[...] = dot(table[1], half[...])
                for at in range(0, H, STRIP):
                    for rows, e_re, e_im in left_strip(flat, at, 1.0):
                        p_re, p_im = folded_probe[2 * m, rows], folded_probe[2 * m + 1, rows]
                        o_re, o_im = patch[k, 0, rows], patch[k, 1, rows]
                        update[k, 0, rows] += p_re * e_re + p_im * e_im
                        update[k, 1, rows] += p_re * e_im - p_im * e_re
                        sums[1 + 2 * m, rows] += o_re * e_re + o_im * e_im
                        sums[2 + 2 * m, rows] += o_re * e_im - o_im * e_re
            for plane in range(2):
                at = 1 + 2 * m + plane
                sums[at] = unfold(sums[at], flip)

        for step in range(GROUPS):
            @pl.when(n == step)
            def _():
                tick(step)

    def file_update(k):
        row_shift, col_shift = spot_words[me, 0, 2 * k] % N, spot_words[me, 0, 2 * k + 1] % N
        row_back = one_hot(iota(0) == (row_shift + folded(iota(1))) % N)
        col_back = one_hot(iota(1) == (col_shift + folded(iota(0))) % N)
        for plane in range(2):
            code, tail = encode(permute(update[k, plane], row_back, col_back, 2))
            queue[k, plane, :N] = code
            queue[k, plane, N:] = tail

    pl.loop(0, per_device // 2)(file_update)
    tick(GROUPS)
    pl.loop(per_device // 2, per_device)(file_update)

    @pl.loop(0, scan_count // 2)
    def _(q):
        pick = jnp.int32(per_device)
        for k in range(per_device):
            pick = jnp.where(spot_words[me, 0, 2 * k + 1] // (2 * N) == q, k, pick)
        for plane in range(2):
            slots[2 * q + plane] = queue[pick, plane]

    def update_copy(dy, dz):
        to = 4 * ((y + dy) % 4) + (z + dz) % 4
        j = 4 * dy + dz
        return remote(slots.at[to], received.at[j], move_send.at[j], move_recv.at[j], to, tile)

    hops = (0, 1, 2, 1)
    order = sorted(((dy, dz) for dy in range(4) for dz in range(4) if dy or dz), key=lambda d: -hops[d[0]] - hops[d[1]])
    def launch(picked):
        for dy, dz in picked:
            update_copy(dy, dz).start()

    tick(GROUPS + 1)
    launch(order[:6])

    def collect(source, ref):
        owner, row_shift, col_shift = jnp.int32(-4), jnp.int32(0), jnp.int32(0)
        for k in range(per_device):
            spot_row, spot_col = spot_words[source, 0, 2 * k], spot_words[source, 0, 2 * k + 1]
            hit = spot_col // (2 * N) == pair
            owner = jnp.where(hit, spot_col // N, owner)
            row_shift = jnp.where(hit, spot_row % N, row_shift)
            col_shift = jnp.where(hit, spot_col % N, col_shift)
        side = owner - 2 * pair
        cols = lax.broadcasted_iota(jnp.int32, (STRIP, N), 1)
        right = cols >= col_shift
        head = jnp.broadcast_to(side, (STRIP, N)) == 0
        tail = jnp.broadcast_to(side, (STRIP, N)) == 1
        picks = (head & right, (head & ~right) | (tail & right), tail & ~right)
        scale = decode_scale(ref[N:])

        for part in range(0, N, STRIP):
            rows = lax.broadcasted_iota(jnp.int32, (STRIP, N), 0) + part
            value = decode(ref[part : part + STRIP], scale)
            low = rows < row_shift
            for at in range(3):
                taken = jnp.where(picks[at], value, 0.0)
                acc[0, at, part : part + STRIP] += jnp.where(low, 0.0, taken)
                acc[1, at, part : part + STRIP] += jnp.where(low, taken, 0.0)

    def collect_some(picked):
        for dy, dz in picked:
            update_copy(dy, dz).wait_recv()
            collect(4 * ((y + 4 - dy) % 4) + (z + 4 - dz) % 4, received.at[4 * dy + dz])

    collect(me, slots.at[me])
    tick(GROUPS + 2)
    launch(order[6:9])
    collect_some(order[:3])
    tick(GROUPS + 3)
    launch(order[9:12])
    collect_some(order[3:6])
    tick(GROUPS + 4)
    launch(order[12:])
    collect_some(order[6:9])
    tick(GROUPS + 5)
    collect_some(order[9:12])
    tick(GROUPS + 6)
    collect_some(order[12:])

    def merge_copy(number, band_at, kind, plane, to):
        return remote(
            merge_out.at[number],
            merge_in.at[band_at, kind, plane],
            move_send.at[16 + number],
            move_recv.at[16 + 4 * band_at + 2 * kind + plane],
            to,
            (tile + band_at) % tile_count,
        )

    beside = me + 1 - 2 * parity
    after_pair = (2 * pair + 2) % scan_count
    merges = []
    for number, (band_at, at, kind, to) in enumerate(
        (
            (1, 2, 1, after_pair),
            (1, 1 - parity, 0, beside),
            (1, parity, 0, me),
            (0, 2, 1, after_pair),
            (0, 1 - parity, 0, beside),
        )
    ):
        code, tail = encode(acc[band_at, at])
        merge_out[number, :N] = code
        merge_out[number, N:] = tail
        merges.append(merge_copy(number, band_at, kind, parity, to))
        merges[-1].start()

    def merged(band_at, kind, plane):
        merge_copy(0, band_at, kind, plane, beside).wait_recv()
        ref = merge_in.at[band_at, kind, plane]
        return decode(ref[:N], decode_scale(ref[N:]))

    numer[1 - parity] = merged(0, 0, 1 - parity)
    numer[1 - parity] += merged(1, 0, 1 - parity)
    numer[parity] = acc[0, parity] + merged(1, 0, parity)

    @pl.when(parity == 0)
    def _():
        for band_at in range(2):
            for plane in range(2):
                numer[plane] += merged(band_at, 1, plane)


    for move in sent:
        move.wait_send()
    above_copy.wait_send()

    @pl.loop(1, scan_count)
    def _(d):
        spot_copy(d).wait_send()

    @pl.loop(0, per_device)
    def _(k):
        cut_copy(k).wait_send()

    for dy, dz in order:
        update_copy(dy, dz).wait_send()
    for move in merges:
        move.wait_send()
    for g in range(GROUPS):
        core_copy(g).wait_send()
        cg_copy(g, 0, core).wait_send()
        for d in range(1, 4):
            x_copy(g, d).wait_send()
            y_copy(g, d).wait_send()
            z_copy(g, d, z).wait_send()
            yg_copy(g, d, y).wait_send()
            xg_copy(g, d, x).wait_send()
            cg_copy(g, d, core).wait_send()


def sweep(field, spots, table, probe, patterns, scan_count):
    per_device, modes = patterns.shape[0], probe.shape[0]
    planes = 2 * modes + 1
    width = 2 * modes // GROUPS
    vmem, anywhere = pl.BlockSpec(memory_space=pltpu.VMEM), pl.BlockSpec(memory_space=pl.ANY)
    words = (scan_count,) + spots.shape
    dma, mem = pltpu.SemaphoreType.DMA, pltpu.VMEM
    slot = (N + TAIL, N)
    return pl.pallas_call(
        sweep_kernel,
        in_specs=[vmem, vmem, vmem, anywhere, anywhere],
        out_specs=[vmem, vmem, vmem],
        out_shape=[
            jax.ShapeDtypeStruct((2 * scan_count, GROUPS, width * 16 + TAIL, H), I16),
            jax.ShapeDtypeStruct((2, N, N), F32),
            jax.ShapeDtypeStruct((N, N), F32),
        ],
        scratch_shapes=[
            mem((2, N, N), BF16),
            mem((scan_count, 2, N, N), BF16),
            mem((per_device, 2, N, N), BF16),
            mem((per_device, 2, N, N), BF16),
            mem(words, jnp.int32),
            mem(words, jnp.int32),
            pltpu.SMEM(words, jnp.int32),
            pltpu.SMEM(words, jnp.int32),
            mem((N, N), F32),
            mem((2 * modes, 16, H), F32),
            mem((2 * modes, N, N), F32),
            mem((per_device, N, N), F32),
            mem((per_device, 2, N, N), F32),
            mem((per_device, modes, 2, N, N), F32),
            mem((per_device, N, N), F32),
            mem((UNROLL, N, 2 * N), BF16),
            mem((UNROLL, N, 2 * N), F32),
            mem((planes, N, N), F32),
            mem((per_device, 2, N, N), F32),
            mem((per_device + 1, 2) + slot, I16),
            mem((scan_count,) + slot, I16),
            mem((scan_count,) + slot, I16),
            mem((planes, N, H), F32),
            mem((GROUPS, 3, (width + 1) * 64 + TAIL, H), I16),
            mem((GROUPS, 3, (width + 1) * 64 + TAIL, H), I16),
            mem((planes, 64, H), F32),
            mem((3, planes, 16, H), F32),
            mem((4, planes, 16, H), F32),
            mem((16, H), F32),
            mem((2, 3, N, N), F32),
            mem((5,) + slot, I16),
            mem((2, 2, 2) + slot, I16),
            dma((30,)),
            dma((2 * scan_count,)),
            dma((scan_count,)),
            dma((scan_count,)),
            dma((per_device,)),
            dma((per_device,)),
            dma((24,)),
            dma((24,)),
            dma((20 * GROUPS,)),
            dma((20 * GROUPS,)),
            dma((4,)),
        ],
        compiler_params=pltpu.CompilerParams(
            collective_id=0, has_side_effects=True, vmem_limit_bytes=62 * 2**20
        ),
        name="sweep",
    )(field, spots, table, probe, patterns)


def final_kernel(coded, numer, cover, field, object_out, probe_out):
    share = 1.0 / (1.0 + cover[...])
    for plane in range(2):
        object_out[plane] = (field[plane] + numer[plane]) * share
    width = (coded.shape[4] - TAIL) // 16
    for core in range(2):
        for at in range(4):
            for g in range(GROUPS):
                scale = decode_scale(coded[core, 0, at, g, width * 16 :])
                value = decode(coded[core, 0, at, g, : width * 16], scale).reshape(width, 16, H)
                probe_out[width * g : width * (g + 1), 16 * at : 16 * (at + 1), core * H : (core + 1) * H] = value


def final(coded, numer, cover, field, planes):
    coded = coded.reshape((2, 4, 4) + coded.shape[1:])
    rows = N // 4
    return pl.pallas_call(
        final_kernel,
        grid=(4,),
        in_specs=[
            pl.BlockSpec((2, 1) + coded.shape[2:], lambda i: (0, i, 0, 0, 0, 0)),
            pl.BlockSpec((2, rows, N), lambda i: (0, i, 0)),
            pl.BlockSpec((rows, N), lambda i: (i, 0)),
            pl.BlockSpec((2, rows, N), lambda i: (0, i, 0)),
        ],
        out_specs=[
            pl.BlockSpec((2, rows, N), lambda i: (0, i, 0)),
            pl.BlockSpec((planes, rows, N), lambda i: (0, i, 0)),
        ],
        out_shape=[jax.ShapeDtypeStruct((2, N, N), F32), jax.ShapeDtypeStruct((planes, N, N), F32)],
        compiler_params=pltpu.CompilerParams(vmem_limit_bytes=62 * 2**20),
        name="final",
    )(coded, numer, cover, field)


def body(object_field, probe_modes, patterns, positions):
    scan_count = lax.axis_size("scan")
    table = jnp.asarray(folded_tables())
    spots = jnp.zeros((8, 128), jnp.int32).at[0, : positions.size].set(positions.reshape(-1))
    coded, numer, cover = sweep(object_field, spots, table, probe_modes, patterns, scan_count)
    planes = 2 * probe_modes.shape[0]
    object_now, probe_now = final(coded, numer, cover, object_field, planes)
    return (object_now, probe_now.reshape(probe_modes.shape))


def solution(mesh):
    return jax.shard_map(
        body,
        mesh=mesh,
        in_specs=(
            P(None, "tile", "scan"),
            P(),
            P(("scan", "tile"), None, None),
            P(("scan", "tile"), None),
        ),
        out_specs=(P(None, "tile", "scan"), P()),
        check_vma=False,
    )
```

```python
import functools
import math

import jax
import jax.numpy as jnp
import ml_dtypes
import numpy as np
from jax import lax
from jax.experimental import pallas as pl
from jax.experimental.pallas import tpu as pltpu
from jax.sharding import PartitionSpec as P

F32 = jnp.float32
BF16 = jnp.bfloat16
N = 256
H = N // 2
I16 = jnp.int16
TAIL = 16
GROUPS = 4
UNROLL = 4
STRIP = 32
FULL = 32767.0
MESH = pl.DeviceIdType.MESH


def folded_tables():
    counter = np.arange(N, dtype=np.int32)
    phase = counter[:, None] * counter[None, :] % N
    angle = phase.astype(np.float32) * np.float32(2.0 * math.pi / N)
    factor = np.float32(1.0 / math.sqrt(N))
    cosine = (np.cos(angle) * factor).astype(ml_dtypes.bfloat16)
    sine = (np.sin(angle) * factor).astype(ml_dtypes.bfloat16)
    order = np.where(counter <= H, counter, 3 * H - counter)
    right = np.concatenate([cosine[:, : H + 1], sine[:, 1:H]], axis=1)[order]
    return np.stack([right, np.ascontiguousarray(right.T)])


def dot(left, right):
    return jnp.dot(left, right, preferred_element_type=F32)


def iota(axis):
    return lax.broadcasted_iota(jnp.int32, (N, N), axis)


def folded(index):
    return jnp.where(index <= H, index, 3 * H - index)


def one_hot(condition):
    return jnp.where(condition, 1.0, 0.0).astype(BF16)


def pieces(value, count):
    parts = []
    for _ in range(count):
        part = value.astype(BF16)
        parts.append(part)
        value = value - part.astype(F32)
    return parts


def permute(value, left, right, count):
    rows = sum(dot(left, part) for part in pieces(value, count))
    return sum(dot(part, right) for part in pieces(rows, count))


def encode(value):
    size = jnp.abs(value)
    peak = jnp.maximum(jnp.max(size, axis=0, keepdims=True), 1e-30)
    exponent = jnp.ceil(jnp.log(peak) * (1.0 / math.log(2.0)) + 1e-5)
    scale = jnp.exp(exponent * -math.log(2.0))
    code = jnp.minimum(jnp.sqrt(size * scale) * FULL + 0.5, FULL).astype(jnp.int32)
    code = jnp.where(value < 0.0, -code, code).astype(I16)
    tail = jnp.broadcast_to(exponent.astype(jnp.int32), (TAIL, value.shape[1])).astype(I16)
    return code, tail


def decode_scale(tail):
    exponent = tail.astype(jnp.int32).astype(F32)[:1]
    return jnp.exp(exponent * math.log(2.0)) * (1.0 / (FULL * FULL))


def decode(code, scale):
    code = code.astype(jnp.int32).astype(F32)
    return code * jnp.abs(code) * scale


def unfold(value, flip):
    high = sum(dot(flip, part) for part in pieces(value[H:], 2))
    rows = jnp.concatenate([value[:H], high], axis=0)
    right = sum(dot(part, flip) for part in pieces(rows[:, H:], 2))
    return jnp.concatenate([rows[:, :H], right], axis=1)


def fold(a_lo, a_hi, b_lo, b_hi, sign, first):
    if first is None:
        return a_lo - sign * b_hi, b_lo + sign * a_hi, a_lo + sign * b_hi, b_lo - sign * a_hi
    a_in = jnp.where(first, 0.0, a_hi)
    b_in = jnp.where(first, 0.0, b_hi)
    return (
        a_lo - sign * b_in,
        b_lo + sign * a_in,
        jnp.where(first, a_hi, a_lo + sign * b_hi),
        jnp.where(first, b_hi, b_lo - sign * a_hi),
    )


def right_stage(re, im, table, half, sign):
    both = dot(jnp.concatenate([re, im], axis=0), table)
    a, b = both[:N], both[N:]
    first = lax.broadcasted_iota(jnp.int32, (N, H), 1) == 0
    re_lo, im_lo, re_hi, im_hi = fold(a[:, :H], a[:, H:], b[:, :H], b[:, H:], sign, first)
    half[:, :H] = re_lo.astype(BF16)
    half[:, H:N] = re_hi.astype(BF16)
    half[:, N : N + H] = im_lo.astype(BF16)
    half[:, N + H :] = im_hi.astype(BF16)


def left_strip(flat, at, sign):
    first = lax.broadcasted_iota(jnp.int32, (STRIP, N), 0) == 0 if at == 0 else None
    low, high = slice(at, at + STRIP), slice(H + at, H + at + STRIP)
    re_lo, im_lo, re_hi, im_hi = fold(flat[low, :N], flat[high, :N], flat[low, N:], flat[high, N:], sign, first)
    return (low, re_lo, im_lo), (high, re_hi, im_hi)


def remote(src, dst, send, recv, scan, tile):
    return pltpu.make_async_remote_copy(
        src_ref=src,
        dst_ref=dst,
        send_sem=send,
        recv_sem=recv,
        device_id={"scan": scan, "tile": tile},
        device_id_type=MESH,
    )


def greet():
    scan_count, tile_count = lax.axis_size("scan"), lax.axis_size("tile")
    me, tile = lax.axis_index("scan"), lax.axis_index("tile")
    barrier = pltpu.get_barrier_semaphore()

    @pl.loop(1, scan_count)
    def _(d):
        pl.semaphore_signal(barrier, 1, device_id={"scan": (me + d) % scan_count, "tile": tile}, device_id_type=MESH)

    @pl.loop(1, tile_count)
    def _(d):
        pl.semaphore_signal(barrier, 1, device_id={"scan": me, "tile": (tile + d) % tile_count}, device_id_type=MESH)

    pl.semaphore_wait(barrier, scan_count + tile_count - 2)


def sweep_kernel(
    field,
    spots,
    table,
    probe,
    patterns,
    coded,
    numer,
    cover,
    block,
    band,
    below,
    cut,
    spots_own,
    spots_above,
    spot_words,
    spot_words_above,
    power_total,
    probe_chunk,
    folded_probe,
    level,
    patch,
    far,
    power,
    halves,
    flats,
    sums,
    update,
    queue,
    slots,
    received,
    core_in,
    x_out,
    x_in,
    y_part,
    y_in,
    z_in,
    den_chunk,
    acc,
    merge_out,
    merge_in,
    send_sem,
    recv_sem,
    spot_send,
    spot_recv,
    cut_send,
    cut_recv,
    move_send,
    move_recv,
    sum_send,
    sum_recv,
    local_sem,
):
    scan_count, tile_count = lax.axis_size("scan"), lax.axis_size("tile")
    me, tile = lax.axis_index("scan"), lax.axis_index("tile")
    x, core = tile // 2, tile % 2
    y, z = me // 4, me % 4
    pair, parity = me // 2, me % 2
    partner = tile + 1 - 2 * core
    next_tile, last_tile = (tile + 1) % tile_count, (tile + tile_count - 1) % tile_count
    per_device = level.shape[0]
    modes = folded_probe.shape[0] // 2
    other_lanes = pl.ds(pl.multiple_of((1 - core) * H, H), H)
    own_lanes = pl.ds(pl.multiple_of(core * H, H), H)

    probe_load = pltpu.make_async_copy(probe, far.at[0], local_sem.at[0])
    probe_load.start()
    pattern_load = pltpu.make_async_copy(patterns, level, local_sem.at[1])
    pattern_load.start()
    block[...] = field[...].astype(BF16)
    greet()

    def spot_copy(d):
        return remote(spots, spots_own.at[me], spot_send.at[d], spot_recv.at[d], (me + d) % scan_count, tile)

    @pl.loop(1, scan_count)
    def _(d):
        spot_copy(d).start()

    def along(plane, stage, d):
        turn_z = (plane == 0) == (stage == 0)
        return 4 * y + (z + d) % 4 if turn_z else 4 * ((y + d) % 4) + z

    sent = []

    def push(src, source, plane, stage, d):
        move = remote(
            src,
            band.at[source, plane],
            send_sem.at[len(sent)],
            recv_sem.at[2 * source + plane],
            along(plane, stage, d),
            tile,
        )
        move.start()
        sent.append(move)

    for stage in range(2):
        for d in (1, 3, 2):
            for plane in range(2):
                push(block.at[plane], me, plane, stage, d)

    def landed(source, plane):
        remote(
            block.at[plane], band.at[source, plane], send_sem.at[0], recv_sem.at[2 * source + plane], along(0, 0, 1), tile
        ).wait_recv()

    spots_own[me] = spots[...]
    band[me] = block[...]
    probe_load.wait()
    total = jnp.zeros((N, N), F32)
    for m in range(modes):
        for plane in range(2):
            value = far[0, m, plane]
            total = total + value * value
    power_total[...] = total

    for d in (3, 1, 2):
        for plane in range(2):
            source = along(plane, 0, d)
            landed(source, plane)
            for turn in (1, 3, 2):
                push(band.at[source, plane], source, plane, 1, turn)

    @pl.loop(1, scan_count)
    def _(d):
        source = (me + scan_count - d) % scan_count
        remote(spots, spots_own.at[source], spot_send.at[d], spot_recv.at[d], source, tile).wait_recv()

    above_copy = remote(spots_own, spots_above, spot_send.at[0], spot_recv.at[0], me, next_tile)
    above_copy.start()
    words_copy = pltpu.make_async_copy(spots_own, spot_words, local_sem.at[2])
    words_copy.start()

    fold_matrix = one_hot(iota(0) == folded(iota(1)))
    chunk_rows = pl.ds(pl.multiple_of(x * 64 + y * 16, 16), 16)

    @pl.loop(0, modes)
    def _(m):
        for plane in range(2):
            folded_probe[2 * m + plane] = permute(far[0, m, plane], fold_matrix, fold_matrix, 3)
            probe_chunk[2 * m + plane] = far[0, m, plane, chunk_rows, own_lanes]

    pattern_load.wait()

    @pl.loop(0, per_device)
    def _(k):
        level[k] = jnp.sqrt(permute(level[k], fold_matrix, fold_matrix, 3))

    cover[...] = jnp.zeros_like(cover)

    def add_cover(words, above):
        @pl.loop(0, scan_count)
        def _(source):
            head, row_shift, col_shift = jnp.int32(-1), jnp.int32(0), jnp.int32(0)
            for k in range(per_device):
                row, col = words[source, 0, 2 * k], words[source, 0, 2 * k + 1]
                owner = col // N
                first = owner == me
                hit = first | ((owner + 1) % scan_count == me)
                head = jnp.where(hit, first.astype(jnp.int32), head)
                row_shift = jnp.where(hit, row % N, row_shift)
                col_shift = jnp.where(hit, col % N, col_shift)
            start = jnp.where(head == 1, col_shift, 0)
            stop = jnp.where(head == 1, N, jnp.where(head == 0, col_shift, 0))
            rows, cols = iota(0), iota(1)
            moved = pltpu.roll(pltpu.roll(power_total[...], row_shift, 0), col_shift, 1)
            keep = (rows < row_shift) if above else (rows >= row_shift)
            cover[...] += jnp.where(keep & (cols >= start) & (cols < stop), moved, 0.0)

    words_copy.wait()
    add_cover(spot_words, False)
    above_copy.wait_recv()
    words_copy = pltpu.make_async_copy(spots_above, spot_words_above, local_sem.at[3])
    words_copy.start()
    words_copy.wait()
    add_cover(spot_words_above, True)

    for d in (3, 1, 2):
        for plane in range(2):
            for turn in (3, 1, 2):
                if plane == 0:
                    source = 4 * ((y + turn) % 4) + (z + d) % 4
                else:
                    source = 4 * ((y + d) % 4) + (z + turn) % 4
                landed(source, plane)
    for turn in (3, 1, 2):
        landed(4 * ((y + turn) % 4) + z, 0)
        landed(4 * y + (z + turn) % 4, 1)

    def composite(col, plane):
        owner, col_shift = col // N, col % N
        after = (owner + 1) % scan_count
        return jnp.where(iota(1) >= col_shift, band[owner, plane].astype(F32), band[after, plane].astype(F32))

    def cut_copy(k):
        return remote(cut.at[k], below.at[k], cut_send.at[k], cut_recv.at[k], me, last_tile)

    @pl.loop(0, per_device)
    def _(k):
        for plane in range(2):
            cut[k, plane] = composite(spot_words_above[me, 0, 2 * k + 1], plane).astype(BF16)
        cut_copy(k).start()

    update[...] = jnp.zeros_like(update)
    sums[...] = jnp.zeros_like(sums)
    acc[...] = jnp.zeros_like(acc)
    queue[per_device] = jnp.zeros(queue.shape[1:], I16)

    @pl.loop(0, per_device)
    def _(k):
        row, col = spot_words[me, 0, 2 * k], spot_words[me, 0, 2 * k + 1]
        row_shift, col_shift = row % N, col % N
        cut_copy(k).wait_recv()
        row_pick = one_hot(iota(1) == (row_shift + folded(iota(0))) % N)
        col_pick = one_hot(iota(0) == (col_shift + folded(iota(1))) % N)
        for plane in range(2):
            top = composite(col, plane)
            window = jnp.where(iota(0) >= row_shift, top, below[k, plane].astype(F32)).astype(BF16)
            patch[k, plane] = dot(dot(row_pick, window).astype(BF16), col_pick)
        sums[0] += patch[k, 0] * patch[k, 0] + patch[k, 1] * patch[k, 1]
        power[k] = jnp.full((N, N), 0.25, F32)

        @pl.loop(0, modes // UNROLL)
        def _(part):
            for u in range(UNROLL):
                m = part * UNROLL + u
                half, flat = halves.at[u], flats.at[u]
                p_re, p_im = folded_probe[2 * m], folded_probe[2 * m + 1]
                o_re, o_im = patch[k, 0], patch[k, 1]
                wave_re = (p_re * o_re - p_im * o_im).astype(BF16)
                wave_im = (p_re * o_im + p_im * o_re).astype(BF16)
                right_stage(wave_re, wave_im, table[0], half, -1.0)
                flat[...] = dot(table[1], half[...])
                for at in range(0, H, STRIP):
                    for rows, f_re, f_im in left_strip(flat, at, -1.0):
                        far[k, m, 0, rows] = f_re
                        far[k, m, 1, rows] = f_im
                        power[k, rows] += f_re * f_re + f_im * f_im

        power[k] = level[k] / jnp.sqrt(power[k])

    half_rows = lax.broadcasted_iota(jnp.int32, (H, H), 0)
    half_cols = lax.broadcasted_iota(jnp.int32, (H, H), 1)
    flip = one_hot(half_rows == (H - half_cols) % H)
    sums[0] = unfold(sums[0], flip)

    PER_GROUP = 20

    def span(g):
        return (0, 2 * modes // GROUPS + 1) if g == 0 else (1 + g * (2 * modes // GROUPS), 2 * modes // GROUPS)

    def sum_copy(src, dst, g, number, scan=None, tile_to=None):
        return remote(
            src,
            dst,
            sum_send.at[g * PER_GROUP + number],
            sum_recv.at[g * PER_GROUP + number],
            me if scan is None else scan,
            tile if tile_to is None else tile_to,
        )

    def core_copy(g):
        start, count = span(g)
        planes = pl.ds(start, count)
        return sum_copy(sums.at[planes, :, other_lanes], core_in.at[planes], g, 0, tile_to=partner)

    def x_copy(g, d):
        used = pl.ds(0, span(g)[1] * 64 + TAIL)
        return sum_copy(
            x_out.at[g, d - 1, used], x_in.at[g, d - 1, used], g, d, tile_to=2 * ((x + d) % 4) + core
        )

    def y_copy(g, d):
        start, count = span(g)
        planes = pl.ds(start, count)
        rows = pl.ds(pl.multiple_of((y + d) % 4 * 16, 16), 16)
        return sum_copy(
            y_part.at[planes, rows], y_in.at[d - 1, planes], g, 3 + d, scan=4 * ((y + d) % 4) + z
        )

    def z_copy(g, d, source):
        planes = pl.ds(*span(g))
        return sum_copy(z_in.at[source, planes], z_in.at[source, planes], g, 6 + d, scan=4 * y + (z + d) % 4)

    def yg_copy(g, d, source):
        at = core * 16 + x * 4 + source
        return sum_copy(coded.at[at, g], coded.at[at, g], g, 9 + d, scan=4 * ((y + d) % 4) + z)

    def xg_copy(g, d, source):
        at = pl.ds(core * 16 + source * 4, 4)
        return sum_copy(coded.at[at, g], coded.at[at, g], g, 12 + d, tile_to=2 * ((x + d) % 4) + core)

    def cg_copy(g, d, side):
        at = pl.ds(side * 16 + (x + 4 - d) % 4 * 4, 4)
        return sum_copy(coded.at[at, g], coded.at[at, g], g, 16 + d, tile_to=partner)

    def stage_core(g):
        core_copy(g).start()

    def stage_x(g):
        start, count = span(g)
        planes = pl.ds(start, count)
        core_copy(g).wait_recv()
        for d in range(1, 4):
            rows = pl.ds(pl.multiple_of((x + d) % 4 * 64, 64), 64)
            chunk = sums[planes, rows, own_lanes] + core_in[planes, rows]
            code, tail = encode(chunk.reshape(count * 64, H))
            x_out[g, d - 1, : count * 64] = code
            x_out[g, d - 1, count * 64 : count * 64 + TAIL] = tail
            x_copy(g, d).start()
        rows = pl.ds(pl.multiple_of(x * 64, 64), 64)
        y_part[planes] = sums[planes, rows, own_lanes] + core_in[planes, rows]

    def stage_y(g):
        start, count = span(g)
        planes = pl.ds(start, count)
        for d in range(1, 4):
            x_copy(g, d).wait_recv()
            scale = decode_scale(x_in[g, d - 1, count * 64 : count * 64 + TAIL])
            y_part[planes] += decode(x_in[g, d - 1, : count * 64], scale).reshape(count, 64, H)
        for d in range(1, 4):
            y_copy(g, d).start()

    def stage_z(g):
        start, count = span(g)
        planes = pl.ds(start, count)
        chunk = y_part[planes, pl.ds(pl.multiple_of(y * 16, 16), 16)]
        for d in range(1, 4):
            y_copy(g, d).wait_recv()
            chunk = chunk + y_in[d - 1, planes]
        z_in[z, planes] = chunk
        for d in range(1, 4):
            z_copy(g, d, z).start()

    def stage_back(g):
        start, count = span(g)
        planes = pl.ds(start, count)
        for d in range(1, 4):
            z_copy(g, d, (z + 4 - d) % 4).wait_recv()
        whole = z_in[0, planes] + z_in[1, planes] + z_in[2, planes] + z_in[3, planes]
        if g == 0:
            den_chunk[...] = 1.0 / (1.0 + whole[0])
            whole = whole[1:]
        width = 2 * modes // GROUPS
        fresh = (probe_chunk[pl.ds(g * width, width)] + whole) * den_chunk[...][None]
        code, tail = encode(fresh.reshape(width * 16, H))
        at = core * 16 + x * 4 + y
        coded[at, g, : width * 16] = code
        coded[at, g, width * 16 :] = tail
        for d in range(1, 4):
            yg_copy(g, d, y).start()

    def stage_x_back(g):
        for d in range(1, 4):
            yg_copy(g, d, (y + 4 - d) % 4).wait_recv()
        for d in range(1, 4):
            xg_copy(g, d, x).start()
        cg_copy(g, 0, core).start()

    def stage_core_back(g):
        for d in range(1, 4):
            xg_copy(g, d, (x + 4 - d) % 4).wait_recv()
            cg_copy(g, d, core).start()

    def stage_end(g):
        for d in range(4):
            cg_copy(g, d, 1 - core).wait_recv()

    stages = (stage_core, stage_x, stage_y, stage_z, stage_back, stage_x_back, stage_core_back, stage_end)

    def tick(n):
        for number in range(len(stages) - 1, -1, -1):
            if 0 <= n - number < GROUPS:
                stages[number](n - number)

    width = modes // GROUPS

    @pl.loop(0, GROUPS)
    def _(n):
        @pl.loop(0, width)
        def _(part):
            m = n * width + part
            for k in range(per_device):
                half, flat = halves.at[k % UNROLL], flats.at[k % UNROLL]
                scaling = power[k]
                fixed_re = (far[k, m, 0] * scaling).astype(BF16)
                fixed_im = (far[k, m, 1] * scaling).astype(BF16)
                right_stage(fixed_re, fixed_im, table[0], half, 1.0)
                flat[...] = dot(table[1], half[...])
                for at in range(0, H, STRIP):
                    for rows, e_re, e_im in left_strip(flat, at, 1.0):
                        p_re, p_im = folded_probe[2 * m, rows], folded_probe[2 * m + 1, rows]
                        o_re, o_im = patch[k, 0, rows], patch[k, 1, rows]
                        update[k, 0, rows] += p_re * e_re + p_im * e_im
                        update[k, 1, rows] += p_re * e_im - p_im * e_re
                        sums[1 + 2 * m, rows] += o_re * e_re + o_im * e_im
                        sums[2 + 2 * m, rows] += o_re * e_im - o_im * e_re
            for plane in range(2):
                at = 1 + 2 * m + plane
                sums[at] = unfold(sums[at], flip)

        for step in range(GROUPS):
            @pl.when(n == step)
            def _():
                tick(step)

    def file_update(k):
        row_shift, col_shift = spot_words[me, 0, 2 * k] % N, spot_words[me, 0, 2 * k + 1] % N
        row_back = one_hot(iota(0) == (row_shift + folded(iota(1))) % N)
        col_back = one_hot(iota(1) == (col_shift + folded(iota(0))) % N)
        for plane in range(2):
            code, tail = encode(permute(update[k, plane], row_back, col_back, 2))
            queue[k, plane, :N] = code
            queue[k, plane, N:] = tail

    pl.loop(0, per_device // 2)(file_update)
    tick(GROUPS)
    pl.loop(per_device // 2, per_device)(file_update)

    @pl.loop(0, scan_count // 2)
    def _(q):
        pick = jnp.int32(per_device)
        for k in range(per_device):
            pick = jnp.where(spot_words[me, 0, 2 * k + 1] // (2 * N) == q, k, pick)
        for plane in range(2):
            slots[2 * q + plane] = queue[pick, plane]

    def update_copy(dy, dz):
        to = 4 * ((y + dy) % 4) + (z + dz) % 4
        j = 4 * dy + dz
        return remote(slots.at[to], received.at[j], move_send.at[j], move_recv.at[j], to, tile)

    hops = (0, 1, 2, 1)
    order = sorted(((dy, dz) for dy in range(4) for dz in range(4) if dy or dz), key=lambda d: -hops[d[0]] - hops[d[1]])
    def launch(picked):
        for dy, dz in picked:
            update_copy(dy, dz).start()

    tick(GROUPS + 1)
    launch(order[:6])

    def collect(source, ref):
        owner, row_shift, col_shift = jnp.int32(-4), jnp.int32(0), jnp.int32(0)
        for k in range(per_device):
            spot_row, spot_col = spot_words[source, 0, 2 * k], spot_words[source, 0, 2 * k + 1]
            hit = spot_col // (2 * N) == pair
            owner = jnp.where(hit, spot_col // N, owner)
            row_shift = jnp.where(hit, spot_row % N, row_shift)
            col_shift = jnp.where(hit, spot_col % N, col_shift)
        side = owner - 2 * pair
        cols = lax.broadcasted_iota(jnp.int32, (STRIP, N), 1)
        right = cols >= col_shift
        head = jnp.broadcast_to(side, (STRIP, N)) == 0
        tail = jnp.broadcast_to(side, (STRIP, N)) == 1
        picks = (head & right, (head & ~right) | (tail & right), tail & ~right)
        scale = decode_scale(ref[N:])

        for part in range(0, N, STRIP):
            rows = lax.broadcasted_iota(jnp.int32, (STRIP, N), 0) + part
            value = decode(ref[part : part + STRIP], scale)
            low = rows < row_shift
            for at in range(3):
                taken = jnp.where(picks[at], value, 0.0)
                acc[0, at, part : part + STRIP] += jnp.where(low, 0.0, taken)
                acc[1, at, part : part + STRIP] += jnp.where(low, taken, 0.0)

    def collect_some(picked):
        for dy, dz in picked:
            update_copy(dy, dz).wait_recv()
            collect(4 * ((y + 4 - dy) % 4) + (z + 4 - dz) % 4, received.at[4 * dy + dz])

    collect(me, slots.at[me])
    tick(GROUPS + 2)
    launch(order[6:9])
    collect_some(order[:3])
    tick(GROUPS + 3)
    launch(order[9:12])
    collect_some(order[3:6])
    tick(GROUPS + 4)
    launch(order[12:])
    collect_some(order[6:9])
    collect_some(order[9:12])
    collect_some(order[12:])

    def merge_copy(number, band_at, kind, plane, to):
        return remote(
            merge_out.at[number],
            merge_in.at[band_at, kind, plane],
            move_send.at[16 + number],
            move_recv.at[16 + 4 * band_at + 2 * kind + plane],
            to,
            (tile + band_at) % tile_count,
        )

    beside = me + 1 - 2 * parity
    after_pair = (2 * pair + 2) % scan_count
    merges = []
    for number, (band_at, at, kind, to) in enumerate(
        (
            (1, 2, 1, after_pair),
            (1, 1 - parity, 0, beside),
            (1, parity, 0, me),
            (0, 2, 1, after_pair),
            (0, 1 - parity, 0, beside),
        )
    ):
        code, tail = encode(acc[band_at, at])
        merge_out[number, :N] = code
        merge_out[number, N:] = tail
        merges.append(merge_copy(number, band_at, kind, parity, to))
        merges[-1].start()
    tick(GROUPS + 5)

    def merged(band_at, kind, plane):
        merge_copy(0, band_at, kind, plane, beside).wait_recv()
        ref = merge_in.at[band_at, kind, plane]
        return decode(ref[:N], decode_scale(ref[N:]))

    numer[1 - parity] = merged(0, 0, 1 - parity)
    numer[1 - parity] += merged(1, 0, 1 - parity)
    numer[parity] = acc[0, parity] + merged(1, 0, parity)

    @pl.when(parity == 0)
    def _():
        for band_at in range(2):
            for plane in range(2):
                numer[plane] += merged(band_at, 1, plane)


    tick(GROUPS + 6)

    for move in sent:
        move.wait_send()
    above_copy.wait_send()

    @pl.loop(1, scan_count)
    def _(d):
        spot_copy(d).wait_send()

    @pl.loop(0, per_device)
    def _(k):
        cut_copy(k).wait_send()

    for dy, dz in order:
        update_copy(dy, dz).wait_send()
    for move in merges:
        move.wait_send()
    for g in range(GROUPS):
        core_copy(g).wait_send()
        cg_copy(g, 0, core).wait_send()
        for d in range(1, 4):
            x_copy(g, d).wait_send()
            y_copy(g, d).wait_send()
            z_copy(g, d, z).wait_send()
            yg_copy(g, d, y).wait_send()
            xg_copy(g, d, x).wait_send()
            cg_copy(g, d, core).wait_send()


def sweep(field, spots, table, probe, patterns, scan_count):
    per_device, modes = patterns.shape[0], probe.shape[0]
    planes = 2 * modes + 1
    width = 2 * modes // GROUPS
    vmem, anywhere = pl.BlockSpec(memory_space=pltpu.VMEM), pl.BlockSpec(memory_space=pl.ANY)
    words = (scan_count,) + spots.shape
    dma, mem = pltpu.SemaphoreType.DMA, pltpu.VMEM
    slot = (N + TAIL, N)
    return pl.pallas_call(
        sweep_kernel,
        in_specs=[vmem, vmem, vmem, anywhere, anywhere],
        out_specs=[vmem, vmem, vmem],
        out_shape=[
            jax.ShapeDtypeStruct((2 * scan_count, GROUPS, width * 16 + TAIL, H), I16),
            jax.ShapeDtypeStruct((2, N, N), F32),
            jax.ShapeDtypeStruct((N, N), F32),
        ],
        scratch_shapes=[
            mem((2, N, N), BF16),
            mem((scan_count, 2, N, N), BF16),
            mem((per_device, 2, N, N), BF16),
            mem((per_device, 2, N, N), BF16),
            mem(words, jnp.int32),
            mem(words, jnp.int32),
            pltpu.SMEM(words, jnp.int32),
            pltpu.SMEM(words, jnp.int32),
            mem((N, N), F32),
            mem((2 * modes, 16, H), F32),
            mem((2 * modes, N, N), F32),
            mem((per_device, N, N), F32),
            mem((per_device, 2, N, N), F32),
            mem((per_device, modes, 2, N, N), F32),
            mem((per_device, N, N), F32),
            mem((UNROLL, N, 2 * N), BF16),
            mem((UNROLL, N, 2 * N), F32),
            mem((planes, N, N), F32),
            mem((per_device, 2, N, N), F32),
            mem((per_device + 1, 2) + slot, I16),
            mem((scan_count,) + slot, I16),
            mem((scan_count,) + slot, I16),
            mem((planes, N, H), F32),
            mem((GROUPS, 3, (width + 1) * 64 + TAIL, H), I16),
            mem((GROUPS, 3, (width + 1) * 64 + TAIL, H), I16),
            mem((planes, 64, H), F32),
            mem((3, planes, 16, H), F32),
            mem((4, planes, 16, H), F32),
            mem((16, H), F32),
            mem((2, 3, N, N), F32),
            mem((5,) + slot, I16),
            mem((2, 2, 2) + slot, I16),
            dma((30,)),
            dma((2 * scan_count,)),
            dma((scan_count,)),
            dma((scan_count,)),
            dma((per_device,)),
            dma((per_device,)),
            dma((24,)),
            dma((24,)),
            dma((20 * GROUPS,)),
            dma((20 * GROUPS,)),
            dma((4,)),
        ],
        compiler_params=pltpu.CompilerParams(
            collective_id=0, has_side_effects=True, vmem_limit_bytes=62 * 2**20
        ),
        name="sweep",
    )(field, spots, table, probe, patterns)


def final_kernel(coded, numer, cover, field, object_out, probe_out):
    share = 1.0 / (1.0 + cover[...])
    for plane in range(2):
        object_out[plane] = (field[plane] + numer[plane]) * share
    width = (coded.shape[4] - TAIL) // 16
    for core in range(2):
        for at in range(4):
            for g in range(GROUPS):
                scale = decode_scale(coded[core, 0, at, g, width * 16 :])
                value = decode(coded[core, 0, at, g, : width * 16], scale).reshape(width, 16, H)
                probe_out[width * g : width * (g + 1), 16 * at : 16 * (at + 1), core * H : (core + 1) * H] = value


def final(coded, numer, cover, field, planes):
    coded = coded.reshape((2, 4, 4) + coded.shape[1:])
    rows = N // 4
    return pl.pallas_call(
        final_kernel,
        grid=(4,),
        in_specs=[
            pl.BlockSpec((2, 1) + coded.shape[2:], lambda i: (0, i, 0, 0, 0, 0)),
            pl.BlockSpec((2, rows, N), lambda i: (0, i, 0)),
            pl.BlockSpec((rows, N), lambda i: (i, 0)),
            pl.BlockSpec((2, rows, N), lambda i: (0, i, 0)),
        ],
        out_specs=[
            pl.BlockSpec((2, rows, N), lambda i: (0, i, 0)),
            pl.BlockSpec((planes, rows, N), lambda i: (0, i, 0)),
        ],
        out_shape=[jax.ShapeDtypeStruct((2, N, N), F32), jax.ShapeDtypeStruct((planes, N, N), F32)],
        compiler_params=pltpu.CompilerParams(vmem_limit_bytes=62 * 2**20),
        name="final",
    )(coded, numer, cover, field)


def body(object_field, probe_modes, patterns, positions):
    scan_count = lax.axis_size("scan")
    table = jnp.asarray(folded_tables())
    spots = jnp.zeros((8, 128), jnp.int32).at[0, : positions.size].set(positions.reshape(-1))
    coded, numer, cover = sweep(object_field, spots, table, probe_modes, patterns, scan_count)
    planes = 2 * probe_modes.shape[0]
    object_now, probe_now = final(coded, numer, cover, object_field, planes)
    return (object_now, probe_now.reshape(probe_modes.shape))


def solution(mesh):
    return jax.shard_map(
        body,
        mesh=mesh,
        in_specs=(
            P(None, "tile", "scan"),
            P(),
            P(("scan", "tile"), None, None),
            P(("scan", "tile"), None),
        ),
        out_specs=(P(None, "tile", "scan"), P()),
        check_vma=False,
    )
```
